32 devices in a mesh: tile: 16 (over z, x, core), grp: 2 (over y).
Axes of the slice: x: 2, y: 2, z: 4, core: 2. Of those that a mesh axis runs over, the one named last changes fastest.
Arguments:
- features: bfloat16 [2, 8192, 64], P('grp', 'tile'), may hold values from -6 to 6
- cotangent: float32 [2, 8192, 64], P('grp', 'tile'), may hold values from -6 to 6
- geom_fine: bfloat16 [2, 8192, 3], P('grp', 'tile'), may hold values from -1 to 1
- geom_mid: bfloat16 [2, 2048, 3], P('grp'), may hold values from -1 to 1
- geom_coarse: bfloat16 [2, 512, 3], P('grp'), may hold values from -1 to 1
- links_fine: int32 [2, 8192, 16], P('grp', 'tile'), may hold values from 0 to 639
- slots_fine: int32 [2, 8192], P('grp', 'tile'), may hold values from 1 to 16, as said below
- send_lists: int32 [2, 2048], P('grp', 'tile'), may hold values from 0 to 511, as said below
- parent_fine: int32 [2, 8192], P('grp', 'tile'), may hold values from 0 to 2047, as said below
- parent_mid: int32 [2, 2048], P('grp'), may hold values from 0 to 511, as said below
- links_mid: int32 [2, 2048, 32], P('grp', 'tile'), may hold values from 0 to 2047
- slots_mid: int32 [2, 2048], P('grp', 'tile'), may hold values from 1 to 32, as said below
- links_coarse: int32 [2, 512, 32], P('grp', 'tile'), may hold values from 0 to 511
- slots_coarse: int32 [2, 512], P('grp', 'tile'), may hold values from 1 to 32, as said below
- kernel_in: float32 [3, 6, 256], P(None, None, ('tile', 'grp')), may hold values from -3 to 3
- kernel_bias: float32 [3, 2, 256], P(None, None, ('tile', 'grp')), may hold values from -0.5 to 0.5
- kernel_mid: float32 [3, 256, 256], P(None, ('tile', 'grp')), may hold values from -0.375 to 0.375
- kernel_out: float32 [3, 256, 4096], P(None, ('tile', 'grp')), may hold values from -0.02734375 to 0.02734375
- first_in: float32 [3, 6, 256], P(None, None, ('tile', 'grp')), may hold values from -0.768 to 0.768
- first_bias: float32 [3, 2, 256], P(None, None, ('tile', 'grp')), may hold values from -1.6384 to 1.6384
- first_mid: float32 [3, 256, 256], P(None, ('tile', 'grp')), may hold values from -8.704 to 8.704
- first_out: float32 [3, 256, 4096], P(None, ('tile', 'grp')), may hold values from -80.384 to 80.384
- second_in: float32 [3, 6, 256], P(None, None, ('tile', 'grp')), may hold values from 0.131072 to 0.524288
- second_bias: float32 [3, 2, 256], P(None, None, ('tile', 'grp')), may hold values from 0.524288 to 2.097152
- second_mid: float32 [3, 256, 256], P(None, ('tile', 'grp')), may hold values from 15.72864 to 62.91456
- second_out: float32 [3, 256, 4096], P(None, ('tile', 'grp')), may hold values from 1284.5056 to 5138.0225
Outputs:
- layer_out: bfloat16 [2, 8192, 64], P('grp', 'tile')
- grad_features: bfloat16 [2, 8192, 64], P('grp', 'tile')
- master_in: float32 [3, 6, 256], P(None, None, ('tile', 'grp'))
- master_bias: float32 [3, 2, 256], P(None, None, ('tile', 'grp'))
- master_mid: float32 [3, 256, 256], P(None, ('tile', 'grp'))
- master_out: float32 [3, 256, 4096], P(None, ('tile', 'grp'))
- moment_in: float32 [3, 6, 256], P(None, None, ('tile', 'grp'))
- moment_bias: float32 [3, 2, 256], P(None, None, ('tile', 'grp'))
- moment_mid: float32 [3, 256, 256], P(None, ('tile', 'grp'))
- moment_out: float32 [3, 256, 4096], P(None, ('tile', 'grp'))
- square_in: float32 [3, 6, 256], P(None, None, ('tile', 'grp'))
- square_bias: float32 [3, 2, 256], P(None, None, ('tile', 'grp'))
- square_mid: float32 [3, 256, 256], P(None, ('tile', 'grp'))
- square_out: float32 [3, 256, 4096], P(None, ('tile', 'grp'))
The draws below stay inside these ranges and needn't reach their ends.
Inputs may be any that keep to these rules, and one draw needn't show every extreme that they name: `slots_fine`: in every tile's rows of each group some node uses all 16 slots. `send_lists`: the first 64 entries of a tile name rows among its first quarter, the last 64 rows among its last quarter. `parent_fine`: the parent of fine node i differs from i // 4 by at most 8, and by exactly that much for some node; a middle node may have no children. `parent_mid`: the parent of middle node j differs from j // 4 by at most 4, and by exactly that much for some node; a coarsest node may have no children. `slots_mid`: among the rows of one index of tile some node uses all 32 slots. `slots_coarse`: among the rows of one index of tile some node uses all 32 slots.
All inputs are finite; a program needn't handle non-finite values.
Results may differ from the reference program's by a relative error of at most 0.0087.
The reference program's roundings to bfloat16 on the way count: a program that leaves them out, or rounds other values in their place, can miss the bound.
Values may be sent and summed in bfloat16 or wider, within the bound.
A program may use at most 128 MiB of HBM per device.

```python
import math
import jax
import jax.numpy as jnp
from jax import lax

C = 64
KW = 256
LEVELS = 3
NODE_DEV = 512
K0 = 16
K1 = 32
HALO = 64
STEP = 5
GROUPS = 2
NF_G = 8192
NC1 = 2048
NC2 = 512
SEND_ALL = 2048
N_TILE = 16
N_GRP = 2
DEVICES = 32


def spread_coords(key, shape, power):
    drawn = jax.random.uniform(key, shape, jnp.float32, -1.0, 1.0)
    return (jnp.sign(drawn) * jnp.abs(drawn) ** power).astype(jnp.float32)


def draw_geom_fine(key, part):
    key = jax.random.fold_in(key, 21)
    return spread_coords(key, (GROUPS, NF_G, 3), 1.0).astype(jnp.bfloat16)


def draw_geom_mid(key, part):
    key = jax.random.fold_in(key, 22)
    return spread_coords(key, (GROUPS, NC1, 3), 1.0).astype(jnp.bfloat16)


def draw_geom_coarse(key, part):
    key = jax.random.fold_in(key, 23)
    return spread_coords(key, (GROUPS, NC2, 3), 1.0).astype(jnp.bfloat16)


def force_most(key, values, block_rows, most):
    total = values.shape[-1]
    block_count = total // block_rows
    chosen = jax.random.randint(key, values.shape[:-1] + (block_count,), 0, block_rows)
    within = jnp.arange(total) % block_rows
    owner = jnp.arange(total) // block_rows
    picked = jnp.take(chosen, owner, axis=-1)
    return jnp.where(within == picked, most, values).astype(jnp.int32)


def draw_slots_fine(key, part):
    key = jax.random.fold_in(key, 11)
    first_key, second_key = jax.random.split(key)
    drawn = jax.random.randint(first_key, (GROUPS, NF_G), 1, K0 + 1)
    return force_most(second_key, drawn, NODE_DEV, K0)


def draw_slots_mid(key, part):
    key = jax.random.fold_in(key, 12)
    first_key, second_key = jax.random.split(key)
    drawn = jax.random.randint(first_key, (GROUPS, NC1), 1, K1 + 1)
    return force_most(second_key, drawn, NODE_DEV // 4, K1)


def draw_slots_coarse(key, part):
    key = jax.random.fold_in(key, 13)
    first_key, second_key = jax.random.split(key)
    drawn = jax.random.randint(first_key, (GROUPS, NC2), 1, K1 + 1)
    return force_most(second_key, drawn, NODE_DEV // 16, K1)


def draw_send_lists(key, part):
    key = jax.random.fold_in(key, 14)
    drawn = jax.random.randint(key, (GROUPS, SEND_ALL), 0, NODE_DEV // 4)
    within = jnp.arange(SEND_ALL) % (2 * HALO)
    shifted = jnp.where(within >= HALO, NODE_DEV - NODE_DEV // 4, 0)
    return (drawn + shifted[None, :]).astype(jnp.int32)


def draw_parent_fine(key, part):
    key = jax.random.fold_in(key, 15)
    reach = min(8, NODE_DEV // 4)
    jitter = jax.random.randint(key, (GROUPS, NF_G), -reach, reach + 1)
    position = jnp.arange(NF_G)
    jitter = jnp.where((position % NODE_DEV == NODE_DEV // 2)[None, :], reach, jitter)
    centre = position // 4
    return jnp.clip(centre[None, :] + jitter, 0, NC1 - 1).astype(jnp.int32)


def draw_parent_mid(key, part):
    key = jax.random.fold_in(key, 16)
    reach = min(4, NODE_DEV // 16)
    jitter = jax.random.randint(key, (GROUPS, NC1), -reach, reach + 1)
    position = jnp.arange(NC1)
    jitter = jnp.where((position % (NODE_DEV // 4) == NODE_DEV // 8)[None, :], reach, jitter)
    centre = position // 4
    return jnp.clip(centre[None, :] + jitter, 0, NC2 - 1).astype(jnp.int32)


def draw_links_mid(key, part):
    key = jax.random.fold_in(key, 17)
    reach = max(1, NC1 // 4)
    offset = jax.random.randint(key, (GROUPS, NC1, K1), -reach, reach + 1)
    centre = jnp.arange(NC1)[None, :, None]
    return jnp.mod(centre + offset, NC1).astype(jnp.int32)


def draw_links_coarse(key, part):
    key = jax.random.fold_in(key, 18)
    first_key, second_key = jax.random.split(key)
    tile_rows = NODE_DEV // 16
    anywhere = jax.random.randint(first_key, (GROUPS, NC2, K1), 0, NC2)
    within = jax.random.randint(second_key, (GROUPS, NC2, K1), 0, tile_rows)
    position = jnp.arange(NC2)
    far_start = jnp.mod(position // tile_rows * tile_rows + NC2 // 2, NC2)
    far = far_start[None, :, None] + within
    slot_even = (jnp.arange(K1) % 2 == 0)[None, None, :]
    return jnp.where(slot_even, far, anywhere).astype(jnp.int32)


def touch_ends(entries, rng, smallest, largest):
    extent = entries.shape
    place = [jax.random.randint(jax.random.fold_in(rng, axis), (), 0, extent[axis]) for axis in range(len(extent))]
    entries = entries.at[tuple(place)].set(smallest)
    longest = extent.index(max(extent))
    place[longest] = (place[longest] + 1) % extent[longest]
    return entries.at[tuple(place)].set(largest)


def shard_levels(own_key, shape, pieces, least, largest):
    factor_of, own = 1.0, jax.random.fold_in(own_key, 6)
    for dim, parts in pieces:
        heights = jnp.exp(jax.random.uniform(jax.random.fold_in(own, dim), (parts,), jnp.float32, least / len(pieces), largest / len(pieces)))
        factor_of = factor_of * jnp.repeat(heights, shape[dim] // parts).reshape([-1 if axis == dim else 1 for axis in range(len(shape))])
    return factor_of


def noise(key, dims, deviation, limit, pieces=(), dtype=jnp.bfloat16):
    level = shard_levels(key, dims, pieces, -0.22, 0.18) if pieces else 1.0
    entries = jax.random.normal(key, dims, jnp.float32) * deviation * level
    return jnp.minimum(jnp.maximum(entries, -limit), limit).astype(dtype)


def setup_inputs(seed: int = 0) -> dict:
    arg_keys = jax.random.split(jax.random.key(seed), 27)
    return {
        "features": noise(arg_keys[0], (GROUPS, NF_G, C), 1.0, 6.0, ((0, 2), (1, 16))),
        "cotangent": noise(arg_keys[1], (GROUPS, NF_G, C), 1.0, 6.0, ((0, 2), (1, 16)), jnp.float32),
        "geom_fine": draw_geom_fine(jax.random.fold_in(arg_keys[26], 71), 0),
        "geom_mid": draw_geom_mid(jax.random.fold_in(arg_keys[26], 71), 0),
        "geom_coarse": draw_geom_coarse(jax.random.fold_in(arg_keys[26], 71), 0),
        "links_fine": touch_ends(jax.random.randint(arg_keys[5], (GROUPS, NF_G, K0), 0, NODE_DEV + 2 * HALO), jax.random.fold_in(arg_keys[5], 1), 0, (NODE_DEV + 2 * HALO) - 1).astype(jnp.int32),
        "slots_fine": draw_slots_fine(jax.random.fold_in(arg_keys[26], 71), 0),
        "send_lists": draw_send_lists(jax.random.fold_in(arg_keys[26], 71), 0),
        "parent_fine": draw_parent_fine(jax.random.fold_in(arg_keys[26], 71), 0),
        "parent_mid": draw_parent_mid(jax.random.fold_in(arg_keys[26], 71), 0),
        "links_mid": draw_links_mid(jax.random.fold_in(arg_keys[26], 71), 0),
        "slots_mid": draw_slots_mid(jax.random.fold_in(arg_keys[26], 71), 0),
        "links_coarse": draw_links_coarse(jax.random.fold_in(arg_keys[26], 71), 0),
        "slots_coarse": draw_slots_coarse(jax.random.fold_in(arg_keys[26], 71), 0),
        "kernel_in": jnp.clip(jax.random.uniform(arg_keys[14], (LEVELS, 6, KW), jnp.float32, -3.0, 3.0) * shard_levels(arg_keys[14], (LEVELS, 6, KW), ((2, 32),), -0.4, 0.0), -3.0, 3.0),
        "kernel_bias": noise(arg_keys[15], (LEVELS, 2, KW), 0.1, 0.5, ((2, 32),), jnp.float32),
        "kernel_mid": noise(arg_keys[16], (LEVELS, KW, KW), KW ** -0.5, 0.375, ((1, 32),), jnp.float32),
        "kernel_out": noise(arg_keys[17], (LEVELS, KW, C * C), (196 * KW) ** -0.5, 0.02734375, ((1, 32),), jnp.float32),
        "first_in": noise(arg_keys[18], (LEVELS, 6, KW), (0.0003 * (NODE_DEV * K0 * DEVICES) ** 0.5), 0.768, ((2, 32),), jnp.float32),
        "first_bias": noise(arg_keys[19], (LEVELS, 2, KW), (0.00064 * (NODE_DEV * K0 * DEVICES) ** 0.5), 1.6384, ((2, 32),), jnp.float32),
        "first_mid": noise(arg_keys[20], (LEVELS, KW, KW), (0.0035 * (NODE_DEV * K0 * DEVICES) ** 0.5), 8.704, ((1, 32),), jnp.float32),
        "first_out": noise(arg_keys[21], (LEVELS, KW, C * C), (0.0315 * (NODE_DEV * K0 * DEVICES) ** 0.5), 80.384, ((1, 32),), jnp.float32),
        "second_in": jnp.clip(jnp.exp(math.log(0.524288) - 1.3862944 * jax.random.uniform(arg_keys[22], (LEVELS, 6, KW), jnp.float32) ** shard_levels(arg_keys[22], (LEVELS, 6, KW), ((2, 32),), -0.2, 0.2)), 0.131072, 0.524288),
        "second_bias": jnp.clip(jnp.exp(math.log(2.097152) - 1.3862944 * jax.random.uniform(arg_keys[23], (LEVELS, 2, KW), jnp.float32) ** shard_levels(arg_keys[23], (LEVELS, 2, KW), ((2, 32),), -0.2, 0.2)), 0.524288, 2.097152),
        "second_mid": jnp.clip(jnp.exp(math.log(62.91456) - 1.3862944 * jax.random.uniform(arg_keys[24], (LEVELS, KW, KW), jnp.float32) ** shard_levels(arg_keys[24], (LEVELS, KW, KW), ((1, 32),), -0.2, 0.2)), 15.72864, 62.91456),
        "second_out": jnp.clip(jnp.exp(math.log(5138.0225) - 1.3862944 * jax.random.uniform(arg_keys[25], (LEVELS, KW, C * C), jnp.float32) ** shard_levels(arg_keys[25], (LEVELS, KW, C * C), ((1, 32),), -0.2, 0.2)), 1284.5056, 5138.0225),
    }


PRECISE = lax.Precision.HIGHEST
B_ONE = 0.9
B_TWO = 0.95
EPSILON = 1e-08
WEIGHT_DECAY = 0.1
RATE_FIRST = 0.4
RATE_MAIN = 0.02

@jax.custom_vjp
def low(v):
    return lax.optimization_barrier(v.astype(jnp.bfloat16)).astype(jnp.float32)

@jax.custom_vjp
def low_back(v):
    return v

def low_keep(v):
    return (low(v), None)

def low_pass(kept, grad):
    return (grad,)

def back_keep(v):
    return (v, None)

def back_low(kept, grad):
    return (low(grad),)
low.defvjp(low_keep, low_pass)
low_back.defvjp(back_keep, back_low)

def messages(level_weights, geom_dst, geom_src, sources, lengths):
    w_first, bias_pair, w_second, w_third = level_weights
    slot_count = geom_src.shape[1]
    feat_width = sources.shape[2]
    inputs = jnp.concatenate([jnp.broadcast_to(geom_dst[:, None, :], geom_src.shape), geom_src], axis=2)
    pre_one = jnp.einsum('bki,ih->bkh', inputs, w_first, precision=PRECISE) + bias_pair[0]
    act_one = low(jax.nn.silu(pre_one))
    pre_two = low_back(jnp.einsum('bkh,hj->bkj', act_one, w_second, precision=PRECISE) + bias_pair[1])
    act_two = low(jax.nn.silu(pre_two))
    kernel = low_back(low(jnp.einsum('bkj,jq->bkq', act_two, w_third, precision=PRECISE)))
    kernel = kernel.reshape(geom_dst.shape[0], slot_count, feat_width, feat_width)
    slot_mask = (lax.broadcasted_iota(jnp.int32, (geom_dst.shape[0], slot_count), 1) < lengths[:, None]).astype(jnp.float32)
    applied = jnp.einsum('bkoc,bkc->bko', kernel, sources, precision=PRECISE)
    total = low_back(lax.optimization_barrier(jnp.sum(applied * slot_mask[:, :, None], axis=1)))
    return total / lengths.astype(jnp.float32)[:, None]

def apply_level(level_weights, geom_dst, geom_src, sources, lengths, tile_count):

    def block_sum(block_data):
        return messages(level_weights, block_data[0], block_data[1], block_data[2], block_data[3])

    def to_blocks(array):
        return array.reshape((tile_count, array.shape[0] // tile_count) + array.shape[1:])
    result = lax.map(jax.checkpoint(block_sum), (to_blocks(geom_dst), to_blocks(geom_src), to_blocks(sources), to_blocks(lengths)))
    return result.reshape(geom_dst.shape[0], -1)

def group_forward(feats, weights, geom_fine, geom_mid, geom_coarse, links_fine, slots_fine, send_lists, parent_fine, parent_mid, links_mid, slots_mid, links_coarse, slots_coarse):
    tile_count = N_TILE
    row_count = feats.shape[0] // tile_count
    feat_width = feats.shape[1]
    halo_rows = send_lists.shape[0] // (2 * tile_count)
    slot_count = links_fine.shape[1]

    def level_weights(level_index):
        return tuple((member[level_index] for member in weights))
    node_table = jnp.concatenate([feats, geom_fine], axis=1).reshape(tile_count, row_count, feat_width + 3)
    send_table = send_lists.reshape(tile_count, 2 * halo_rows).astype(jnp.int32)
    sent_rows = jnp.take_along_axis(node_table, send_table[:, :, None], axis=1)
    zero_rows = jnp.zeros((1, halo_rows, feat_width + 3), jnp.float32)
    from_left = jnp.concatenate([zero_rows, sent_rows[:-1, halo_rows:]], axis=0)
    from_right = jnp.concatenate([sent_rows[1:, :halo_rows], zero_rows], axis=0)
    extended = jnp.concatenate([node_table, from_left, from_right], axis=1)
    link_table = links_fine.reshape(tile_count, row_count * slot_count).astype(jnp.int32)
    gathered = jnp.take_along_axis(extended, link_table[:, :, None], axis=1)
    gathered = gathered.reshape(tile_count * row_count, slot_count, feat_width + 3)
    sources = gathered[:, :, :feat_width]
    geom_src = gathered[:, :, feat_width:]
    base = feats + apply_level(level_weights(0), geom_fine, geom_src, sources, slots_fine, tile_count)
    mid_count = geom_mid.shape[0]
    count_mid = jax.ops.segment_sum(jnp.ones(parent_fine.shape, jnp.float32), parent_fine, num_segments=mid_count)
    mid_value = jax.ops.segment_sum(base, parent_fine, num_segments=mid_count) / jnp.maximum(count_mid, 1.0)[:, None]
    mid_source = low(mid_value)
    mid_out = mid_value + apply_level(level_weights(1), geom_mid, geom_mid[links_mid], mid_source[links_mid], slots_mid, tile_count)
    coarse_count = geom_coarse.shape[0]
    count_coarse = jax.ops.segment_sum(jnp.ones(parent_mid.shape, jnp.float32), parent_mid, num_segments=coarse_count)
    coarse_value = jax.ops.segment_sum(mid_out, parent_mid, num_segments=coarse_count) / jnp.maximum(count_coarse, 1.0)[:, None]
    coarse_source = low(coarse_value)
    coarse_out = coarse_value + apply_level(level_weights(2), geom_coarse, geom_coarse[links_coarse], coarse_source[links_coarse], slots_coarse, tile_count)
    up_mid = mid_out + coarse_out[parent_mid]
    up_fine = base + up_mid[parent_fine]
    return jax.nn.silu(up_fine)

def adamw(master, moment, square, grad, learn_rate):
    moment_new = B_ONE * moment + (1.0 - B_ONE) * grad
    square_new = B_TWO * square + (1.0 - B_TWO) * grad * grad
    fix_one = 1.0 - B_ONE ** STEP
    fix_two = 1.0 - B_TWO ** STEP
    master_new = master - learn_rate * (moment_new / fix_one / (jnp.sqrt(square_new / fix_two) + EPSILON) + WEIGHT_DECAY * master)
    return (master_new, moment_new, square_new)

def reference(features, cotangent, geom_fine, geom_mid, geom_coarse, links_fine, slots_fine, send_lists, parent_fine, parent_mid, links_mid, slots_mid, links_coarse, slots_coarse, kernel_in, kernel_bias, kernel_mid, kernel_out, first_in, first_bias, first_mid, first_out, second_in, second_bias, second_mid, second_out):
    masters = (kernel_in, kernel_bias, kernel_mid, kernel_out)

    def forward(feats, params):
        weights = tuple((low(member) for member in params))
        results = []
        for group_index in range(N_GRP):
            results.append(group_forward(feats[group_index], weights, geom_fine[group_index].astype(jnp.float32), geom_mid[group_index].astype(jnp.float32), geom_coarse[group_index].astype(jnp.float32), links_fine[group_index], slots_fine[group_index], send_lists[group_index], parent_fine[group_index], parent_mid[group_index], links_mid[group_index], slots_mid[group_index], links_coarse[group_index], slots_coarse[group_index]))
        return jnp.stack(results)
    result, pullback = jax.vjp(forward, features.astype(jnp.float32), masters)
    grad_feats, grads = pullback(cotangent)
    new_in = adamw(kernel_in, first_in, second_in, grads[0], RATE_FIRST)
    new_bias = adamw(kernel_bias, first_bias, second_bias, grads[1], RATE_MAIN)
    new_mid = adamw(kernel_mid, first_mid, second_mid, grads[2], RATE_MAIN)
    new_out = adamw(kernel_out, first_out, second_out, grads[3], RATE_MAIN)
    return (result.astype(jnp.bfloat16), grad_feats.astype(jnp.bfloat16), new_in[0], new_bias[0], new_mid[0], new_out[0], new_in[1], new_bias[1], new_mid[1], new_out[1], new_in[2], new_bias[2], new_mid[2], new_out[2])
```

```python
import functools

import jax
import jax.numpy as jnp
from jax import lax
from jax.experimental import pallas as pl
from jax.experimental.pallas import tpu as pltpu
from jax.sharding import PartitionSpec as P

STEP = 5
B_ONE = 0.9
B_TWO = 0.95
EPSILON = 1e-08
WEIGHT_DECAY = 0.1
RATE_FIRST = 0.4
RATE_MAIN = 0.02

BF = jnp.bfloat16
F32 = jnp.float32
I32 = jnp.int32
MESH = pl.DeviceIdType.MESH
NN = ((1,), (0,))
NT = ((1,), (1,))
TN = ((0,), (0,))
LANES = 512
GROUP = 16


def dot(a, b, dims=NN):
    return lax.dot_general(a, b, (dims, ((), ())), preferred_element_type=F32)


def sig(v):
    return 0.5 + 0.5 * jnp.tanh(0.5 * v)


def split3(v):
    high = v.astype(BF)
    rest = v - high.astype(F32)
    mid = rest.astype(BF)
    low = (rest - mid.astype(F32)).astype(BF)
    return jnp.concatenate([high, mid, low], axis=0)


def join3(v):
    n = v.shape[0] // 3
    return v[:n] + v[n : 2 * n] + v[2 * n :]


def iota(shape, dim):
    return lax.broadcasted_iota(I32, shape, dim)


def group_mask(width):
    slots = width // GROUP
    return (iota((GROUP, width), 1) // slots == iota((GROUP, width), 0)).astype(F32)


def one_hot(row, start, rows):
    return (iota((rows, row.shape[1]), 0) + start == row).astype(F32).astype(BF)


def spread(x, mask):
    return (x[:, None, :] * mask[None]).reshape(x.shape[0] * GROUP, mask.shape[1]).astype(BF)


class Level:
    def __init__(self, index, nodes, slots, sources):
        self.index, self.nodes, self.slots, self.sources = index, nodes, slots, sources
        self.steps = nodes * slots // LANES
        self.width = GROUP * slots
        self.blocks = LANES // self.width
        self.chunk = sources if sources <= 1024 else 512


def make_kernel(T, NG, C, KW, fine, mid, coarse, halo, inside):
    H = T // 4
    NCH = T // 2 * NG
    A = KW // (32 * NG)
    NB = KW // 16
    HALF = C * C // 2
    QH = HALF // 2
    SMW = KW + 128
    levels = (fine, mid, coarse)
    NM, NC = mid.nodes, coarse.nodes

    def kernel(
        tab, cot, send, lkf, lkm, lkc, zdf, zdm, zdc, nf, nm, nc, pf, pw, gm, gc, wsm, wc,
        layer, gradf, gwc, gsmall,
        ext, extT, agbuf, wt, s0buf, smbuf, waT, wbT, wbr, bbc,
        mt0, mt1, mt2, xs0, xs1, xs2, zs0, zs1, zs2,
        ohp, tx_s, rx_s, tx_w, rx_w, tx_q, rx_q, tx_u, rx_u, tx_g, rx_g, tx_c, rx_c, tx_b, rx_b, tx_f, rx_f, tx_h, rx_h,
        x1T, x2b, acc0, acc1, acc2, acc1b, acc2b, rs1buf, rs2buf, v0s, gys,
        rsr0, rsr1, rsr2, rsr3, rsf, rsr4, gsb, rcA, rcB, sems,
    ):
        t = lax.axis_index("tile")
        g = lax.axis_index("grp")
        core = lax.rem(t, 2)
        r = t // 2
        lo = lax.rem(r, 2)
        hi = r // 2
        ch = r * NG + g
        ocore, olo, og = 1 - core, 1 - lo, 1 - g

        def tile_of(hi_, lo_, core_):
            return (hi_ * 2 + lo_) * 2 + core_

        partner = {"tile": tile_of(hi, lo, ocore), "grp": g}
        xn = {"tile": tile_of(hi, olo, core), "grp": g}
        yn = {"tile": t, "grp": og}

        counter = [0]

        def sem_block(n):
            base = counter[0]
            counter[0] += n
            return base

        def copy(src, dst, ssem, rsem, dev):
            return pltpu.make_async_remote_copy(
                src_ref=src, dst_ref=dst, send_sem=sems.at[ssem], recv_sem=sems.at[rsem],
                device_id=dev, device_id_type=MESH,
            )

        local = sem_block(1)

        def own_copy(src, dst):
            c = pltpu.make_async_copy(src, dst, sems.at[local])
            c.start()
            c.wait()

        class One:
            def __init__(self, src, dst, dev):
                self.s, self.r = sem_block(1), sem_block(1)
                self.d = None
                self.parts = (src, dst, self.s, self.r, dev)

            def start(self):
                self.d = copy(*self.parts)
                self.d.start()

            def recv(self):
                self.d.wait_recv()

            def sent(self):
                self.d.wait_send()

        class Ring:
            def __init__(self, n, src, dst, dev):
                self.n, self.src, self.dst, self.dev = n, src, dst, dev
                self.s, self.r = sem_block(n - 1), sem_block(n - 1)

            def each(self, f):
                def body(i, _):
                    d = i + 1
                    f(copy(self.src(d), self.dst(d), self.s + i, self.r + i, self.dev(d)))
                    return 0

                lax.fori_loop(0, self.n - 1, body, 0)

            def start(self):
                self.each(lambda c: c.start())

            def recv(self):
                self.each(lambda c: c.wait_recv())

            def sent(self):
                self.each(lambda c: c.wait_send())

        class Sides:
            def __init__(self, src_left, src_right, rx):
                self.ls, self.lr, self.rs, self.rr = (sem_block(1) for _ in range(4))
                self.rx = rx
                self.to_left = copy(src_left, rx.at[1], self.ls, self.lr, {"tile": t - 1, "grp": g})
                self.to_right = copy(src_right, rx.at[0], self.rs, self.rr, {"tile": t + 1, "grp": g})

            def start(self):
                @pl.when(t > 0)
                def _():
                    self.to_left.start()

                @pl.when(t < T - 1)
                def _():
                    self.to_right.start()

                @pl.when(t == 0)
                def _():
                    self.rx[0] = jnp.zeros(self.rx.shape[1:], self.rx.dtype)

                @pl.when(t == T - 1)
                def _():
                    self.rx[1] = jnp.zeros(self.rx.shape[1:], self.rx.dtype)

            def recv(self):
                @pl.when(t < T - 1)
                def _():
                    self.to_left.wait_recv()

                @pl.when(t > 0)
                def _():
                    self.to_right.wait_recv()

            def sent(self):
                @pl.when(t > 0)
                def _():
                    self.to_left.wait_send()

                @pl.when(t < T - 1)
                def _():
                    self.to_right.wait_send()

        pending = []

        def started(c):
            c.start()
            pending.append(c)
            return c

        barrier = pltpu.get_barrier_semaphore()
        total = T * NG
        me = t * NG + g

        def greet(i, _):
            other = lax.rem(me + i + 1, total)
            pl.semaphore_signal(
                barrier, inc=1, device_id={"tile": other // NG, "grp": lax.rem(other, NG)}, device_id_type=MESH
            )
            return 0

        lax.fori_loop(0, total - 1, greet, 0)

        ohs = one_hot(send[...], 0, fine.nodes)
        sent_rows = dot(ohs, tab[...], TN).astype(BF)
        ext[0 : fine.nodes] = tab[...]
        tx_s[...] = sent_rows
        ohp[...] = one_hot(pf[...], 0, 2 * NM)
        if inside:
            smbuf[:, ch, core] = wsm[...]
        else:
            smbuf[...] = wsm[...].reshape(smbuf.shape)
            own_copy(wc, agbuf)
        pl.semaphore_wait(barrier, total - 1)

        def chip_dev(d):
            o = lax.rem(ch + d, NCH)
            return {"tile": (o // NG) * 2 + core, "grp": lax.rem(o, NG)}

        if inside:
            sm_a0 = started(Ring(NCH, lambda d: smbuf.at[0, ch, core], lambda d: smbuf.at[0, ch, core], chip_dev))
        halo_x = started(Sides(tx_s.at[0:halo], tx_s.at[halo : 2 * halo], rx_s))
        if inside:
            s0c = [started(One(wc.at[l, ocore], s0buf.at[l], partner)) for l in range(3)]
            sm_a12 = started(Ring(NCH, lambda d: smbuf.at[1:3, ch, core], lambda d: smbuf.at[1:3, ch, core], chip_dev))

        ag = [[] for _ in range(3)]

        def ag_s1(l):
            if not inside:
                return
            s0c[l].recv()
            mine, theirs = wc[l, core], s0buf[l]
            first = core == 0
            agbuf[l, core, hi, lo, g] = jnp.concatenate(
                [jnp.where(first, mine, theirs), jnp.where(first, theirs, mine)], axis=0
            ).astype(BF)
            c = Ring(
                H,
                lambda d: agbuf.at[l, core, hi, lo, g],
                lambda d: agbuf.at[l, core, hi, lo, g],
                lambda d: {"tile": tile_of(lax.rem(hi + d, H), lo, core), "grp": g},
            )
            c.start()
            ag[l].append([c])

        def ag_next(l, *copies):
            if not inside:
                return
            for c in ag[l][-1]:
                c.recv()
            for c in copies:
                c.start()
            ag[l].append(copies)

        def ag_s2(l):
            part = agbuf.at[l, core, :, lo, g]
            ag_next(l, One(part, part, xn), One(part, part, yn))

        def ag_s3(l):
            a = agbuf.at[l, core, :, olo, g, :, 0:QH]
            b = agbuf.at[l, core, :, lo, og, :, QH:HALF]
            ag_next(l, One(a, a, yn), One(b, b, xn))

        def ag_s4(l):
            part = agbuf.at[l, core]
            ag_next(l, One(part, part, partner))

        def ag_fin(l):
            if inside:
                for c in ag[l][-1]:
                    c.recv()
                for cs in ag[l]:
                    for c in cs:
                        c.sent()
            n = HALF // 128

            def body(i, _):
                half, k = i // n, lax.rem(i, n)
                block = agbuf[l, half, :, :, :, :, pl.ds(pl.multiple_of(k * 128, 128), 128)].reshape(KW, 128)
                wt[l, pl.ds(i * 2, 2)] = block.T.reshape(2, C, KW)
                return 0

            lax.fori_loop(0, 2 * n, body, 0)

        def unpack_small(l):
            block = smbuf[l].reshape(KW, SMW)
            second = block[:, 0:KW]
            wbr[l] = second.astype(BF)
            wbT[l] = second.T.astype(BF)
            waT[l] = block[:, KW : KW + 8].astype(BF)
            bbc[l] = jnp.broadcast_to(block[:, KW + 8 : KW + 9], (KW, 128))

        lks, zds, mts, xss, zss = (lkf, lkm, lkc), (zdf, zdm, zdc), (mt0, mt1, mt2), (xs0, xs1, xs2), (zs0, zs1, zs2)

        def pair(ref, lv, i):
            if lv.blocks == 1:
                return ref[i]
            return jnp.concatenate([ref[lv.blocks * i + k] for k in range(lv.blocks)], axis=1)

        def take(table, row, lv):
            rows = lv.chunk
            if lv.sources == rows:
                return dot(table[...], one_hot(row, 0, rows))
            n = lv.sources // rows

            def body(k, acc):
                start = pl.multiple_of(k * rows, rows)
                return acc + dot(table[:, pl.ds(start, rows)], one_hot(row, start, rows))

            return lax.fori_loop(0, n, body, jnp.zeros((table.shape[0], LANES), F32))

        def put(acc, values, row, lv):
            rows = lv.chunk
            if lv.sources == rows:
                acc[...] += dot(values, one_hot(row, 0, rows), NT)
                return
            n = lv.sources // rows

            def body(k, _):
                start = pl.multiple_of(k * rows, rows)
                at = pl.ds(start, rows)
                acc[:, at] += dot(values, one_hot(row, start, rows), NT)
                return 0

            lax.fori_loop(0, n, body, 0)

        def edges_forward(lv, x_table, g_table, first, last):
            l = lv.index
            mask = group_mask(lv.width)

            def body(i, _):
                row = pair(lks[l], lv, i)
                if g_table is None:
                    got = take(x_table, row, lv)
                    x, z = got[0:C], got[C : C + 8] + pair(zds[l], lv, i)
                else:
                    x = take(x_table, row, lv)
                    z = take(g_table, row, lv)[0:8] + pair(zds[l], lv, i)
                xss[l][i] = x.astype(BF)
                zss[l][i] = z
                t1 = dot(waT[l], z.astype(BF))
                a1 = (t1 * sig(t1)).astype(BF)
                t2 = dot(wbT[l], a1) + bbc[l][:, 0:1]
                a2 = (t2 * sig(t2)).astype(BF)
                for k in range(lv.blocks):
                    sl = slice(lv.width * k, lv.width * (k + 1))
                    m = dot(spread(x[:, sl], mask), a2[:, sl], NT)
                    at = pl.ds(pl.multiple_of((lv.blocks * i + k) * GROUP, GROUP), GROUP)
                    mts[l][:, at, :] = m.astype(BF).reshape(C, GROUP, KW)
                return 0

            lax.fori_loop(first, last, body, 0)

        def node_sums(lv):
            l = lv.index

            def body(i, acc):
                for u in range(4):
                    acc = acc + dot(wt[l, 4 * i + u], mts[l][4 * i + u], NT)
                return acc

            return lax.fori_loop(0, C // 4, body, jnp.zeros((C, lv.nodes), F32))

        def third_grad(lv, gsT):
            l = lv.index
            n = C // 4

            def body(i, _):
                both = jnp.concatenate([dot(gsT, mts[l][2 * i]), dot(gsT, mts[l][2 * i + 1])], axis=0)
                out = both.T.astype(BF).reshape(A, 2, NG, 16, 128)
                agbuf[l, i // n, :, :, :, :, pl.ds(pl.multiple_of(lax.rem(i, n) * 128, 128), 128)] = out
                return 0

            lax.fori_loop(0, C // 2, body, 0)

        def node_weights(lv, gs):
            l = lv.index

            def body(c, _):
                mts[l][c] = dot(gs, wt[l, c]).astype(BF)
                return 0

            lax.fori_loop(0, C, body, 0)

        def edges_backward(lv, acc, first, last):
            l = lv.index
            mask = group_mask(lv.width)
            fold = (iota((C, C * GROUP), 1) // GROUP == iota((C, C * GROUP), 0)).astype(F32).astype(BF)

            def body(i, _):
                zb = zss[l][i].astype(BF)
                t1 = dot(waT[l], zb)
                s1 = sig(t1)
                f1 = t1 * s1
                d1 = s1 + f1 * (1.0 - s1)
                a1 = f1.astype(BF)
                t2 = dot(wbT[l], a1) + bbc[l][:, 0:1]
                s2 = sig(t2)
                f2 = t2 * s2
                d2 = s2 + f2 * (1.0 - s2)
                a2 = f2.astype(BF)
                x = xss[l][i].astype(F32)
                g2s, gxs = [], []
                for k in range(lv.blocks):
                    sl = slice(lv.width * k, lv.width * (k + 1))
                    at = pl.ds(pl.multiple_of((lv.blocks * i + k) * GROUP, GROUP), GROUP)
                    q = mts[l][:, at, :].reshape(C * GROUP, KW)
                    g2s.append((dot(q, spread(x[:, sl], mask), TN) * d2[:, sl]).astype(BF))
                    every = dot(q, a2[:, sl])
                    own = (every.reshape(C, GROUP, lv.width) * mask[None]).reshape(C * GROUP, lv.width).astype(BF)
                    gxs.append(dot(fold, own).astype(BF))
                g2 = jnp.concatenate(g2s, axis=1)
                gx = jnp.concatenate(gxs, axis=1)
                g1 = (dot(wbr[l], g2) * d1).astype(BF)
                sm2 = dot(a1, g2, NT)
                p1 = dot(g1, zb, NT)
                p2 = dot(g2, zb, NT)
                gsb[l, :, :, :, 0:KW] += sm2.reshape(NB, 2, 8, KW)
                gsb[l, :, :, :, KW : KW + 8] += p1.reshape(NB, 2, 8, 8)
                gsb[l, :, :, :, KW + 8 : KW + 16] += p2.reshape(NB, 2, 8, 8)
                put(acc, gx, pair(lks[l], lv, i), lv)
                return 0

            lax.fori_loop(first, last, body, 0)

        def roll_pick(left, right, n_left, left_lane, right_lane):
            lane = iota((1, 128), 1)
            a = pltpu.roll(left, (left_lane - (n_left - 8)) % 128, 1)
            b = pltpu.roll(right, right_lane % 128, 1)
            return jnp.where((lane >= left_lane) & (lane < left_lane + 8), a, 0.0) + jnp.where(
                (lane >= right_lane) & (lane < right_lane + 8), b, 0.0
            )

        def margin_pick(from_left, from_right, n_own, left_at, right_at):
            lane = iota((1, 128), 1)
            a = pltpu.roll(from_left, (0 - right_at) % 128, 1)
            b = pltpu.roll(from_right, (n_own - 8 - left_at) % 128, 1)
            return jnp.where(lane < 8, a, 0.0) + jnp.where((lane >= n_own - 8) & (lane < n_own), b, 0.0)

        ag_s1(0)
        halo_x.recv()
        ext[fine.nodes : fine.nodes + halo] = rx_s[0]
        ext[fine.nodes + halo :] = rx_s[1]
        extT[...] = ext[...].T[0:80]
        ag_s1(1)
        ag_s1(2)
        if inside:
            sm_a0.recv()
            sm_b0 = started(One(smbuf.at[0, :, core], smbuf.at[0, :, core], partner))
            ag_s2(0)
            sm_a12.recv()
            sm_b12 = started(One(smbuf.at[1:3, :, core], smbuf.at[1:3, :, core], partner))
            sm_b0.recv()
        unpack_small(0)
        quarter = fine.steps // 4
        edges_forward(fine, extT, None, 0, quarter)
        ag_s3(0)
        ag_s2(1)
        edges_forward(fine, extT, None, quarter, 2 * quarter)
        ag_s4(0)
        ag_s3(1)
        ag_s2(2)
        edges_forward(fine, extT, None, 2 * quarter, 3 * quarter)
        ag_s4(1)
        ag_s3(2)
        edges_forward(fine, extT, None, 3 * quarter, fine.steps)
        ag_s4(2)
        ag_fin(0)
        v0 = extT[0:C, 0 : fine.nodes].astype(F32) + node_sums(fine) / nf[...]
        v0s[...] = v0

        ones8 = jnp.ones((8, fine.nodes), BF)
        part = dot(jnp.concatenate([split3(v0), ones8], axis=0), ohp[...], NT)
        sums = jnp.concatenate([join3(part[0 : 3 * C]), part[3 * C :]], axis=0)
        tx_w[0] = sums[:, NM:]
        ex_w = started(Sides(tx_w.at[0], tx_w.at[0], rx_w))
        if inside:
            sm_b12.recv()
        unpack_small(1)
        ag_fin(1)
        ex_w.recv()
        own = sums[:, 0:NM] + margin_pick(rx_w[0], rx_w[1], NM, 0, 8)
        inv1 = 1.0 / jnp.maximum(own[C : C + 1], 1.0)
        v1 = own[0:C] / jnp.maximum(own[C : C + 1], 1.0)
        x1T[:, pl.ds(pl.multiple_of(t * NM, NM), NM)] = v1.astype(BF)

        def tile_dev(d):
            return {"tile": lax.rem(t + d, T), "grp": g}

        x1own = x1T.at[:, pl.ds(pl.multiple_of(t * NM, NM), NM)]
        ag1 = started(Ring(T, lambda d: x1own, lambda d: x1own, tile_dev))
        unpack_small(2)
        ag_fin(2)
        ag1.recv()

        edges_forward(mid, x1T, gm, 0, mid.steps)
        w1 = v1 + node_sums(mid) / nm[...]
        tx_q[0, 0:C] = w1
        ohq = one_hot(pw[...], 0, 128)
        part = dot(jnp.concatenate([split3(w1), jnp.ones((8, NM), BF)], axis=0), ohq[:, 0:NM], NT)
        tx_q[0, C : 2 * C + 8] = jnp.concatenate([join3(part[0 : 3 * C]), part[3 * C :]], axis=0)
        ex_q = started(Sides(tx_q.at[0], tx_q.at[0], rx_q))
        ex_q.recv()
        own = tx_q[0, C : 2 * C + 8] + margin_pick(rx_q[0, C : 2 * C + 8], rx_q[1, C : 2 * C + 8], NC, NC, NC + 8)
        w1m = roll_pick(rx_q[0, 0:C], rx_q[1, 0:C], NM, 0, 8)
        w1win = jnp.concatenate([w1, w1m], axis=1)
        lane = iota((1, 128), 1)
        mine = lane < NC
        cnt2 = jnp.maximum(own[C : C + 1], 1.0)
        v2 = jnp.where(mine, own[0:C] / cnt2, 0.0)

        x2b[t] = v2.astype(BF)
        ag2 = started(Ring(T, lambda d: x2b.at[t], lambda d: x2b.at[t], tile_dev))
        ag2.recv()
        per = 128 // NC
        cols = []
        for k in range(coarse.sources // 128):
            block = x2b[per * k].astype(F32)
            for u in range(1, per):
                block = block + pltpu.roll(x2b[per * k + u].astype(F32), NC * u, 1)
            cols.append(block.astype(BF))
        for k, block in enumerate(cols):
            acc2[:, 128 * k : 128 * k + 128] = block.astype(F32)
        x2T = acc2[...].astype(BF)
        acc2b[0:C] = x2T
        edges_forward(coarse, acc2b.at[0:C], gc, 0, coarse.steps)
        sc = node_sums(coarse)
        sc = jnp.concatenate([sc, jnp.zeros((C, 128 - NC), F32)], axis=1)
        w2 = v2 + jnp.where(mine, sc / nc[...], 0.0)
        tx_u[0] = w2
        ex_u = started(Sides(tx_u.at[0], tx_u.at[0], rx_u))
        ex_u.recv()
        w2win = w2 + roll_pick(rx_u[0], rx_u[1], NC, NC, NC + 8)

        y1win = w1win + join3(dot(split3(w2win), ohq))
        y0 = v0s[...] + join3(dot(split3(y1win), ohp[...]))
        s0 = sig(y0)
        f0 = y0 * s0
        layer[...] = f0.T.astype(BF)
        gy0 = cot[...].T * (s0 + f0 * (1.0 - s0))
        gys[...] = gy0
        gy1p = join3(dot(split3(gy0), ohp[...], NT))
        gw2p = join3(dot(split3(gy1p), ohq, NT))
        tx_g[0, 0:C] = gy1p[:, NM:]
        tx_g[0, C : 2 * C] = gw2p
        ex_g = started(Sides(tx_g.at[0], tx_g.at[0], rx_g))
        ex_g.recv()
        gy1 = gy1p[:, 0:NM] + margin_pick(rx_g[0, 0:C], rx_g[1, 0:C], NM, 0, 8)
        gw2 = jnp.where(mine, gw2p + margin_pick(rx_g[0, C:], rx_g[1, C:], NC, NC, NC + 8), 0.0)

        rs = [[] for _ in range(3)]

        def rs_step(l, fix, *copies):
            if not inside:
                return
            if rs[l]:
                for c in rs[l][-1]:
                    c.recv()
            fix()
            for c in copies:
                c.start()
            rs[l].append(copies)
            pending.extend(copies)

        def rs_s0(l):
            rs_step(l, lambda: None, One(agbuf.at[l, ocore], rsr0.at[l], partner))

        def rs_s1(l):
            def fix():
                def body(i, _):
                    both = agbuf[l, core, i].astype(F32) + rsr0[l, i].astype(F32)
                    agbuf[l, core, i] = both.astype(BF)
                    return 0

                lax.fori_loop(0, H, body, 0)

            rs_step(
                l, fix,
                One(agbuf.at[l, core, :, olo, og, :, 0:QH], rsr1.at[l, 0], xn),
                One(agbuf.at[l, core, :, olo, og, :, QH:HALF], rsr1.at[l, 1], yn),
            )

        def rs_s2(l):
            def fix():
                def body(i, _):
                    a = agbuf[l, core, i, lo, og, :, 0:QH].astype(F32) + rsr1[l, 0, i].astype(F32)
                    agbuf[l, core, i, lo, og, :, 0:QH] = a.astype(BF)
                    b = agbuf[l, core, i, olo, g, :, QH:HALF].astype(F32) + rsr1[l, 1, i].astype(F32)
                    agbuf[l, core, i, olo, g, :, QH:HALF] = b.astype(BF)
                    return 0

                lax.fori_loop(0, H, body, 0)

            rs_step(
                l, fix,
                One(agbuf.at[l, core, :, lo, og], rsr2.at[l, 0], yn),
                One(agbuf.at[l, core, :, olo, g], rsr2.at[l, 1], xn),
            )

        def rs_s3(l):
            def fix():
                def body(i, _):
                    a = agbuf[l, core, i, lo, g].astype(F32) + rsr2[l, 0, i].astype(F32) + rsr2[l, 1, i].astype(F32)
                    agbuf[l, core, i, lo, g] = a.astype(BF)
                    return 0

                lax.fori_loop(0, H, body, 0)

            rs_step(
                l, fix,
                Ring(
                    H,
                    lambda d: agbuf.at[l, core, lax.rem(hi + d, H), lo, g],
                    lambda d: rsr3.at[l, d - 1],
                    lambda d: {"tile": tile_of(lax.rem(hi + d, H), lo, core), "grp": g},
                ),
            )

        def rs_s4(l):
            def fix():
                tot = agbuf[l, core, hi, lo, g].astype(F32)
                for k in range(H - 1):
                    tot = tot + rsr3[l, k].astype(F32)
                rsf[l, 0] = tot[0:8]
                rsf[l, 1] = tot[8:16]

            rs_step(l, fix, One(rsf.at[l, ocore], rsr4.at[l], partner))

        def rs_s5(l):
            if not inside:
                own_copy(agbuf.at[l], gwc.at[l])
                return
            for c in rs[l][-1]:
                c.recv()
            gwc[l, core] = rsf[l, core]
            gwc[l, ocore] = rsr4[l]

        gsb[...] = jnp.zeros(gsb.shape, F32)

        gs2T = jnp.where(mine, gw2 / nc[...], 0.0).astype(BF)
        third_grad(coarse, gs2T[:, 0:NC])
        rs_s0(2)
        node_weights(coarse, gs2T.astype(F32).T[0:NC].astype(BF))
        acc2[...] = jnp.zeros(acc2.shape, F32)
        edges_backward(coarse, acc2, 0, coarse.steps)
        a2rows = jnp.concatenate([acc2[...], jnp.zeros(acc2.shape, F32)], axis=0)
        tx_c[...] = a2rows.T.astype(BF)
        ag_r2 = started(
            Ring(
                T,
                lambda d: tx_c.at[pl.ds(pl.multiple_of(lax.rem(t + d, T) * NC, NC), NC)],
                lambda d: rs2buf.at[d - 1],
                tile_dev,
            )
        )
        rs_s1(2)
        ag_r2.recv()

        def add2(k, acc):
            return acc + rs2buf[k].astype(F32)

        own2 = lax.fori_loop(
            0, T - 1, add2, tx_c[pl.ds(pl.multiple_of(t * NC, NC), NC)].astype(F32)
        )
        own2 = jnp.concatenate([own2, jnp.zeros((128 - NC, 128), F32)], axis=0).T[0:C]
        gv2 = jnp.where(mine, (gw2 + own2) / cnt2, 0.0)
        tx_b[0, 0:C] = gv2
        ex_b = started(Sides(tx_b.at[0, 0:C], tx_b.at[0, 0:C], rx_b))
        rs_s2(2)
        ex_b.recv()
        gv2win = gv2 + roll_pick(rx_b[0], rx_b[1], NC, NC, NC + 8)
        gw1 = gy1 + join3(dot(split3(gv2win), ohq[:, 0:NM]))

        gs1T = (gw1 / nm[...]).astype(BF)
        third_grad(mid, gs1T)
        rs_s0(1)
        rs_s3(2)
        node_weights(mid, gs1T.astype(F32).T.astype(BF))
        acc1[...] = jnp.zeros(acc1.shape, F32)
        edges_backward(mid, acc1, 0, mid.steps)
        acc1b[...] = acc1[...].astype(BF)
        ag_r1 = started(
            Ring(
                T,
                lambda d: acc1b.at[:, pl.ds(pl.multiple_of(lax.rem(t + d, T) * NM, NM), NM)],
                lambda d: rs1buf.at[d - 1],
                tile_dev,
            )
        )
        rs_s1(1)
        rs_s4(2)
        ag_r1.recv()

        def add1(k, acc):
            return acc + rs1buf[k].astype(F32)

        own1 = lax.fori_loop(0, T - 1, add1, acc1[:, pl.ds(pl.multiple_of(t * NM, NM), NM)])
        gv1 = (gw1 + own1) * inv1
        tx_f[0] = gv1
        ex_f = started(Sides(tx_f.at[0], tx_f.at[0], rx_f))
        rs_s2(1)
        rs_s5(2)
        ex_f.recv()
        gv1win = jnp.concatenate([gv1, roll_pick(rx_f[0], rx_f[1], NM, 0, 8)], axis=1)
        gv0 = gys[...] + join3(dot(split3(gv1win), ohp[...]))
        gys[...] = gv0

        gs0 = gv0 / nf[...]
        gs0T = gs0.astype(BF)
        third_grad(fine, gs0T)
        rs_s0(0)
        rs_s3(1)
        node_weights(fine, gs0T.astype(F32).T.astype(BF))
        acc0[...] = jnp.zeros(acc0.shape, F32)
        rs_s1(0)
        rs_s4(1)
        edges_backward(fine, acc0, 0, quarter)
        rs_s2(0)
        rs_s5(1)
        edges_backward(fine, acc0, quarter, 2 * quarter)
        rs_s3(0)
        edges_backward(fine, acc0, 2 * quarter, 3 * quarter)
        rs_s4(0)
        edges_backward(fine, acc0, 3 * quarter, fine.steps)
        tx_h[0] = acc0[:, fine.nodes : fine.nodes + 2 * halo]
        ex_h = started(Sides(tx_h.at[0], tx_h.at[0], rx_h))

        if inside:
            gs_a = started(One(gsb.at[:, :, ocore], rcA, partner))
        rs_s5(0)
        ex_h.recv()
        lane1 = iota((1, 128), 1)
        back = jnp.where(lane1 < halo, pltpu.roll(rx_h[0], halo, 1), pltpu.roll(rx_h[1], halo, 1))
        ohs2 = one_hot(send[...], 0, fine.nodes)
        gf = gys[...] + acc0[:, 0 : fine.nodes] + join3(dot(split3(back), ohs2, NT))
        gradf[...] = gf.T.astype(BF)
        if inside:
            gs_a.recv()
            for l in range(3):
                gsb[l, :, core] += rcA[l]
            gs_b = started(
                Ring(
                    NCH,
                    lambda d: gsb.at[:, lax.rem(ch + d, NCH), core],
                    lambda d: rcB.at[d - 1],
                    chip_dev,
                )
            )
            gs_b.recv()

            def add3(k, acc):
                return acc + rcB[k]

            gsmall[...] = lax.fori_loop(0, NCH - 1, add3, gsb[:, ch, core])
        else:
            gsmall[...] = gsb[...]

        for c in pending:
            c.sent()

    n_sems = (
        2 * (2 * (NCH - 1)) + 4 + 2 * 3 + 3 * (2 * (H - 1) + 4 + 4 + 2) + 4
        + 4 * 7 + 4 * (2 * (T - 1)) + 3 * (2 + 4 + 4 + 2 * (H - 1) + 2) + 2 + 2 * (NCH - 1) + 9
    )
    V = pltpu.VMEM
    ls = 3 if inside else 1
    nf, nm_, nc_ = fine.nodes, NM, NC
    scratch = [
        V((nf + 2 * halo, 128), BF), V((80, nf + 2 * halo), BF),
        V((3, 2, A, 2, NG, 16, HALF), BF), V((3, C, C, KW), BF), V((3, 8, HALF), F32),
        V((3, NB, 2, 8, SMW), F32), V((3, KW, 8), BF), V((3, KW, KW), BF), V((3, KW, KW), BF), V((3, KW, 128), F32),
        V((C, nf, KW), BF), V((C, nm_, KW), BF), V((C, nc_, KW), BF),
        V((fine.steps, C, LANES), BF), V((mid.steps, C, LANES), BF), V((coarse.steps, C, LANES), BF),
        V((fine.steps, 8, LANES), F32), V((mid.steps, 8, LANES), F32), V((coarse.steps, 8, LANES), F32),
        V((2 * NM, nf), BF),
        V((2 * halo, 128), BF), V((2, halo, 128), BF),
        V((1, C + 8, 128), F32), V((2, C + 8, 128), F32),
        V((1, 2 * C + 8, 128), F32), V((2, 2 * C + 8, 128), F32),
        V((1, C, 128), F32), V((2, C, 128), F32),
        V((1, 2 * C, 128), F32), V((2, 2 * C, 128), F32),
        V((coarse.sources, 128), BF), V((1, 8, 128), F32),
        V((1, C, 128), F32), V((2, C, 128), F32),
        V((1, C, 128), F32), V((2, C, 128), F32),
        V((1, C, 128), F32), V((2, C, 128), F32),
        V((C, mid.sources), BF), V((T, C, 128), BF),
        V((C, nf + 2 * halo), F32), V((C, mid.sources), F32), V((C, coarse.sources), F32),
        V((C, mid.sources), BF), V((C, coarse.sources), BF),
        V((T - 1, C, 128), BF), V((T, NC, 128), BF), V((C, nf), F32), V((C, nf), F32),
        V((ls, A, 2, NG, 16, HALF), BF), V((ls, 2, A, 16, QH), BF), V((ls, 2, A, 16, HALF), BF),
        V((ls, A - 1, 16, HALF), BF), V((ls, 2, 8, HALF), F32), V((ls, 8, HALF), F32),
        V((3, NB, 2, 8, SMW), F32), V((ls, NB, 8, SMW), F32), V((NB - 1, ls, 8, SMW), F32),
        pltpu.SemaphoreType.DMA((n_sems,)),
    ]
    return kernel, scratch


def adamw(master, moment, square, grad, learn_rate):
    moment_new = B_ONE * moment + (1.0 - B_ONE) * grad
    square_new = B_TWO * square + (1.0 - B_TWO) * grad * grad
    fix_one = 1.0 - B_ONE**STEP
    fix_two = 1.0 - B_TWO**STEP
    master_new = master - learn_rate * (
        moment_new / fix_one / (jnp.sqrt(square_new / fix_two) + EPSILON) + WEIGHT_DECAY * master
    )
    return (master_new, moment_new, square_new)


def per_device(
    T, NG,
    features, cotangent, geom_fine, geom_mid, geom_coarse, links_fine, slots_fine, send_lists, parent_fine,
    parent_mid, links_mid, slots_mid, links_coarse, slots_coarse, kernel_in, kernel_bias, kernel_mid, kernel_out,
    first_in, first_bias, first_mid, first_out, second_in, second_bias, second_mid, second_out,
):
    C = features.shape[2]
    KW = kernel_mid.shape[2]
    R = T // 2
    NM, NC = links_mid.shape[1], links_coarse.shape[1]
    halo = send_lists.shape[1] // 2
    nf = features.shape[1]
    fine = Level(0, nf, links_fine.shape[2], nf + 2 * halo)
    mid = Level(1, NM, links_mid.shape[2], geom_mid.shape[1])
    coarse = Level(2, NC, links_coarse.shape[2], geom_coarse.shape[1])
    t = lax.axis_index("tile")

    def edge_rows(links, slots, lv):
        used = lax.broadcasted_iota(I32, links.shape, 1) < slots[:, None]
        return jnp.where(used, links, -1).reshape(-1, 1, lv.width)

    def edge_geom(geom, lv):
        n = geom.shape[0]
        rows = jnp.concatenate(
            [jnp.zeros((n, 1), F32), geom.astype(F32), jnp.ones((n, 1), F32), jnp.zeros((n, 3), F32)], axis=1
        )
        rows = rows.reshape(n // GROUP, GROUP, 8).transpose(0, 2, 1)
        return jnp.broadcast_to(rows[..., None], rows.shape + (lv.slots,)).reshape(n // GROUP, 8, lv.width)

    def source_geom(geom):
        return jnp.pad(geom.T, ((5, 8), (0, 0)))

    tab = jnp.concatenate(
        [features[0], jnp.zeros((nf, 5), BF), geom_fine[0], jnp.zeros((nf, 128 - C - 8), BF)], axis=1
    )
    mid_start, coarse_start = t * NM, t * NC
    own_geom_mid = lax.dynamic_slice_in_dim(geom_mid[0], mid_start, NM, 0)
    own_geom_coarse = lax.dynamic_slice_in_dim(geom_coarse[0], coarse_start, NC, 0)

    def window(index, start, n, at):
        off = index - start
        return jnp.where(off < 0, off + at + 8, jnp.where(off >= n, off - n + at + 8, off))

    pf = window(parent_fine[0], mid_start, NM, NM)[None]
    padded = jnp.pad(parent_mid[0], (8, 8), constant_values=-(1 << 20))
    around = lax.dynamic_slice_in_dim(padded, mid_start, NM + 16, 0)
    around = jnp.concatenate([around[8 : 8 + NM], around[:8], around[8 + NM :]])
    pw = jnp.where(around < 0, -1, window(around, coarse_start, NC, NC))
    pw = jnp.pad(pw, (0, 2 * NM - pw.shape[0]), constant_values=-1)[None]
    row = lambda s, n: jnp.pad(s.astype(F32), (0, n - s.shape[0]), constant_values=1.0)[None]

    def columns(v):
        return v.reshape(v.shape[:-1] + (R, 2, NG, 8)).swapaxes(-3, -2).reshape(v.shape)

    turned = kernel_in.swapaxes(1, 2)
    biases = kernel_bias.swapaxes(1, 2)
    per = kernel_mid.shape[1]
    inside = per == 8
    zero = jnp.zeros((3, per, 1), F32)
    wsm = jnp.concatenate(
        [columns(kernel_mid) if inside else kernel_mid, zero, turned[..., 0:3], biases[..., 0:1], turned[..., 3:6], biases[..., 1:2],
         jnp.zeros((3, per, 119), F32)], axis=2
    )
    wc = kernel_out.reshape(3, per, C, C).transpose(0, 3, 2, 1).reshape(3, 2, C * C // 2, per).swapaxes(2, 3)
    everyone = ("tile", "grp")
    grid = (3, 2, KW // (32 * NG), 2, NG, 16, C * C // 2)
    if not inside:
        wsm = lax.all_gather(wsm, everyone, axis=1, tiled=True)
        wc = lax.all_gather(wc.astype(BF), everyone, axis=2, tiled=True).reshape(grid)

    kernel, scratch = make_kernel(T, NG, C, KW, fine, mid, coarse, halo, inside)
    S = jax.ShapeDtypeStruct
    vm = pl.BlockSpec(memory_space=pltpu.VMEM)
    far = pl.BlockSpec(memory_space=pl.ANY)
    operands = (
        tab, cotangent[0], send_lists,
        edge_rows(links_fine[0], slots_fine[0], fine), edge_rows(links_mid[0], slots_mid[0], mid),
        edge_rows(links_coarse[0], slots_coarse[0], coarse),
        edge_geom(geom_fine[0], fine), edge_geom(own_geom_mid, mid), edge_geom(own_geom_coarse, coarse),
        row(slots_fine[0], nf), row(slots_mid[0], NM), row(slots_coarse[0], 128),
        pf, pw, source_geom(geom_mid[0]), source_geom(geom_coarse[0]), wsm, wc,
    )
    layer, gradf, gwc, gsmall = pl.pallas_call(
        kernel,
        out_shape=(S((nf, C), BF), S((nf, C), BF), S((3, 2, 8, C * C // 2), F32) if inside else S(grid, BF),
                   S((3, 8, KW + 128) if inside else (3, KW // 16, 2, 8, KW + 128), F32)),
        in_specs=[vm] * (len(operands) - 1) + [vm if inside else far],
        out_specs=(vm, vm, vm if inside else far, vm),
        scratch_shapes=scratch,
        compiler_params=pltpu.CompilerParams(
            collective_id=0, has_side_effects=True, vmem_limit_bytes=63 << 20
        ),
        name="layer",
    )(*operands)

    def uncolumns(v):
        return v.reshape(v.shape[:-1] + (R, NG, 2, 8)).swapaxes(-3, -2).reshape(v.shape)

    if not inside:
        gwc = gwc.astype(F32).reshape(3, 2, KW, C * C // 2)
        gwc = lax.psum_scatter(gwc, everyone, scatter_dimension=2, tiled=True)
        gsmall = lax.psum_scatter(gsmall.reshape(3, KW, KW + 128), everyone, scatter_dimension=1, tiled=True)
    grad_out = gwc.swapaxes(1, 2).reshape(3, per, C, C).swapaxes(2, 3).reshape(3, per, C * C)
    grad_mid = uncolumns(gsmall[..., 0:KW]) if inside else gsmall[..., 0:KW]
    small = gsmall[..., KW:].swapaxes(1, 2)
    grad_in = jnp.concatenate([small[:, 1:4], small[:, 5:8]], axis=1)
    grad_bias = jnp.concatenate([small[:, 4:5], small[:, 12:13]], axis=1)
    new_in = adamw(kernel_in, first_in, second_in, grad_in, RATE_FIRST)
    new_bias = adamw(kernel_bias, first_bias, second_bias, grad_bias, RATE_MAIN)
    new_mid = adamw(kernel_mid, first_mid, second_mid, grad_mid, RATE_MAIN)
    new_out = adamw(kernel_out, first_out, second_out, grad_out, RATE_MAIN)
    return (layer[None], gradf[None]) + tuple(
        new[k] for k in range(3) for new in (new_in, new_bias, new_mid, new_out)
    )


def solution(mesh):
    nodes = P("grp", "tile", None)
    rows = P("grp", "tile")
    by_column = P(None, None, ("tile", "grp"))
    by_row = P(None, ("tile", "grp"), None)
    shards = (by_column, by_column, by_row, by_row)
    return jax.shard_map(
        functools.partial(per_device, mesh.shape["tile"], mesh.shape["grp"]),
        mesh=mesh,
        in_specs=(
            nodes, nodes, nodes, P("grp", None, None), P("grp", None, None), nodes, rows, rows, rows,
            P("grp", None), nodes, rows, nodes, rows,
        ) + shards * 3,
        out_specs=(nodes, nodes) + shards * 3,
        check_vma=False,
    )
```

```python
import functools

import jax
import jax.numpy as jnp
from jax import lax
from jax.experimental import pallas as pl
from jax.experimental.pallas import tpu as pltpu
from jax.sharding import PartitionSpec as P

STEP = 5
B_ONE = 0.9
B_TWO = 0.95
EPSILON = 1e-08
WEIGHT_DECAY = 0.1
RATE_FIRST = 0.4
RATE_MAIN = 0.02

BF = jnp.bfloat16
F32 = jnp.float32
I32 = jnp.int32
MESH = pl.DeviceIdType.MESH
NN = ((1,), (0,))
NT = ((1,), (1,))
TN = ((0,), (0,))
LANES = 512
GROUP = 16


def dot(a, b, dims=NN):
    return lax.dot_general(a, b, (dims, ((), ())), preferred_element_type=F32)


def sig(v):
    return 0.5 + 0.5 * jnp.tanh(0.5 * v)


def split3(v):
    high = v.astype(BF)
    rest = v - high.astype(F32)
    mid = rest.astype(BF)
    low = (rest - mid.astype(F32)).astype(BF)
    return jnp.concatenate([high, mid, low], axis=0)


def join3(v):
    n = v.shape[0] // 3
    return v[:n] + v[n : 2 * n] + v[2 * n :]


def iota(shape, dim):
    return lax.broadcasted_iota(I32, shape, dim)


def log2(n):
    assert n & (n - 1) == 0
    return n.bit_length() - 1


def group_mask(width):
    return (iota((GROUP, width), 1) >> log2(width // GROUP) == iota((GROUP, width), 0)).astype(F32)


def one_hot(row, start, rows):
    return (iota((rows, row.shape[1]), 0) + start == row).astype(F32).astype(BF)


def spread(x, mask):
    return (x[:, None, :] * mask[None]).reshape(x.shape[0] * GROUP, mask.shape[1]).astype(BF)


def place(rows, columns, pairs):
    r, c = iota((rows, columns), 0), iota((rows, columns), 1)
    hit = jnp.zeros((rows, columns), F32)
    for row, column, count in pairs:
        hit = hit + jnp.where((r - row == c - column) & (r >= row) & (r < row + count), 1.0, 0.0)
    return hit.astype(BF)


def column_order(KW, NG, natural_rows):
    p = iota((KW, KW), 1 if natural_rows else 0)
    n = iota((KW, KW), 0 if natural_rows else 1)
    shift = log2(NG)
    inner, core, grp, chip = p & 7, (p >> 3) & 1, (p >> 4) & (NG - 1), p >> (4 + shift)
    return ((((((chip << 1) + core) << shift) + grp) << 3) + inner == n).astype(F32).astype(BF)


class Level:
    def __init__(self, index, nodes, slots, sources):
        self.index, self.nodes, self.slots, self.sources = index, nodes, slots, sources
        self.steps = nodes * slots // LANES
        self.width = GROUP * slots
        self.blocks = LANES // self.width
        self.chunk = sources if sources <= 1024 else 512


def make_kernel(T, NG, C, KW, fine, mid, coarse, halo, inside):
    H = T // 4
    NCH = T // 2 * NG
    A = KW // (32 * NG)
    NB = KW // 16
    R = T // 2
    HALF = C * C // 2
    QH = HALF // 2
    SMW = KW + 128
    levels = (fine, mid, coarse)
    NM, NC = mid.nodes, coarse.nodes

    def kernel(
        feat_h, cot_h, geof_h, geom_h, geoc_h, lkf_h, slf_h, send_h, parf_h, parm_h, lkm_h, slm_h, lkc_h, slc_h,
        kin_h, kb_h, kmid_h, kout_h,
        layer, gradf, gwc, gsmall,
        feat, cot, geof, geom, geoc, lkf, slf, send, parf, parm, lkm, slm, lkc, slc, kin, kb, kmid, ownw,
        geom_own, lkc_wide, slc_wide, pk0, pk1, pk2, gm, gc,
        extT, agbuf, gbuf, s0buf, smbuf, waT, wbT, wbr, bbc,
        mt0, mt1, mt2, qt1, qt2, as1, as2, xs0, xs1, xs2, zs0, zs1, zs2,
        ohp, tx_s, rx_s, tx_w, rx_w, tx_q, rx_q, tx_u, rx_u, tx_g, rx_g, tx_b, rx_b, tx_f, rx_f, tx_h, rx_h,
        x1T, x1b, x2T, x2b, acc0, acc1, acc2, acc1b, acc2b, rs1a, rs2a, rs1buf, rs2buf, v0s, gys,
        rsr0, rsr1, rsr2, rsr3, rsf, rsr4, gsb, rcA, rcB, sems,
    ):
        t = lax.axis_index("tile")
        g = lax.axis_index("grp")
        core = lax.rem(t, 2)
        r = t // 2
        lo = lax.rem(r, 2)
        hi = r // 2
        ch = r * NG + g
        ocore, olo, og = 1 - core, 1 - lo, 1 - g

        def tile_of(hi_, lo_, core_):
            return (hi_ * 2 + lo_) * 2 + core_

        partner = {"tile": tile_of(hi, lo, ocore), "grp": g}
        xn = {"tile": tile_of(hi, olo, core), "grp": g}
        yn = {"tile": t, "grp": og}

        counter = [0]
        open_recv, open_send = [], []

        def sem_block(n):
            base = counter[0]
            counter[0] += n
            return base

        def copy(src, dst, ssem, rsem, dev):
            return pltpu.make_async_remote_copy(
                src_ref=src, dst_ref=dst, send_sem=sems.at[ssem], recv_sem=sems.at[rsem],
                device_id=dev, device_id_type=MESH,
            )

        local = sem_block(1)

        def own_copy(src, dst):
            c = pltpu.make_async_copy(src, dst, sems.at[local])
            c.start()
            c.wait()

        class One:
            def __init__(self, src, dst, dev):
                self.s, self.r = sem_block(1), sem_block(1)
                self.d = None
                self.parts = (src, dst, self.s, self.r, dev)

            def start(self):
                self.d = copy(*self.parts)
                self.d.start()
                open_recv.append(self)
                open_send.append(self)

            def recv(self):
                open_recv.remove(self)
                self.d.wait_recv()

            def sent(self):
                open_send.remove(self)
                self.d.wait_send()

        class Ring:
            def __init__(self, n, src, dst, dev):
                self.n, self.src, self.dst, self.dev = n, src, dst, dev
                self.s, self.r = sem_block(n - 1), sem_block(n - 1)

            def each(self, f):
                def body(i, _):
                    d = i + 1
                    f(copy(self.src(d), self.dst(d), self.s + i, self.r + i, self.dev(d)))
                    return 0

                lax.fori_loop(0, self.n - 1, body, 0)

            def start(self):
                self.each(lambda c: c.start())
                open_recv.append(self)
                open_send.append(self)

            def recv(self):
                open_recv.remove(self)
                self.each(lambda c: c.wait_recv())

            def sent(self):
                open_send.remove(self)
                self.each(lambda c: c.wait_send())

        class Sides:
            def __init__(self, src_left, src_right, rx):
                self.ls, self.lr, self.rs, self.rr = (sem_block(1) for _ in range(4))
                self.rx = rx
                self.to_left = copy(src_left, rx.at[1], self.ls, self.lr, {"tile": t - 1, "grp": g})
                self.to_right = copy(src_right, rx.at[0], self.rs, self.rr, {"tile": t + 1, "grp": g})

            def start(self):
                open_recv.append(self)
                open_send.append(self)

                @pl.when(t > 0)
                def _():
                    self.to_left.start()

                @pl.when(t < T - 1)
                def _():
                    self.to_right.start()

                @pl.when(t == 0)
                def _():
                    self.rx[0] = jnp.zeros(self.rx.shape[1:], self.rx.dtype)

                @pl.when(t == T - 1)
                def _():
                    self.rx[1] = jnp.zeros(self.rx.shape[1:], self.rx.dtype)

            def recv(self):
                open_recv.remove(self)

                @pl.when(t < T - 1)
                def _():
                    self.to_left.wait_recv()

                @pl.when(t > 0)
                def _():
                    self.to_right.wait_recv()

            def sent(self):
                open_send.remove(self)

                @pl.when(t > 0)
                def _():
                    self.to_left.wait_send()

                @pl.when(t < T - 1)
                def _():
                    self.to_right.wait_send()

        def started(c):
            c.start()
            return c

        def finish():
            for c in tuple(open_recv):
                c.recv()
            for c in tuple(open_send):
                c.sent()

        barrier = pltpu.get_barrier_semaphore()
        total = T * NG
        me = t * NG + g

        def greet(i, _):
            other = lax.rem(me + i + 1, total)
            pl.semaphore_signal(
                barrier, inc=1, device_id={"tile": other // NG, "grp": lax.rem(other, NG)}, device_id_type=MESH
            )
            return 0

        lax.fori_loop(0, total - 1, greet, 0)

        loads = []

        def load(src, dst):
            c = pltpu.make_async_copy(src, dst, sems.at[sem_block(1)])
            c.start()
            loads.append(c)

        for src, dst in (
            (feat_h, feat), (geof_h, geof), (send_h, send), (kin_h, kin), (kb_h, kb), (kmid_h, kmid), (lkf_h, lkf),
            (slf_h, slf), (parf_h, parf), (geom_h, geom), (geoc_h, geoc), (parm_h, parm), (lkm_h, lkm), (slm_h, slm),
            (lkc_h, lkc), (slc_h, slc), (cot_h, cot),
        ):
            if inside or not any(dst is v for v in (kin, kb, kmid)):
                load(src, dst)
        own_lanes = pl.ds(pl.multiple_of(t * NM, NM), NM)
        load(geom_h.at[:, own_lanes], geom_own)
        if inside:
            for l in range(3):
                load(kout_h.at[l, core], ownw.at[l])
        for c in loads:
            c.wait()

        n0 = fine.nodes
        extT[:, 0:n0] = (
            dot(place(80, C, [(0, 0, C)]), feat[...]) + dot(place(80, 3, [(C + 5, 0, 3)]), geof[...])
        ).astype(BF)
        tx_s[0] = dot(extT[:, 0:n0], one_hot(send[...], 0, n0)).astype(BF)

        def window(index, start, n, at):
            off = index - start
            return jnp.where(off < 0, off + at + 8, jnp.where(off >= n, off - n + at + 8, off))

        ohp[...] = one_hot(window(parf[...], t * NM, NM, NM), 0, 2 * NM)
        if inside:
            order = column_order(KW, NG, True)
            for l in range(3):
                second = dot(kmid[l].astype(BF), order)
                first = dot(kin[l].astype(BF), place(6, 128, [(0, 0, 3), (3, 5, 3)]), TN)
                first = first + dot(kb[l].astype(BF), place(2, 128, [(0, 3, 1), (1, 8, 1)]), TN)
                smbuf[l, ch, core] = jnp.concatenate([second, first], axis=1)
        else:
            own_copy(kmid_h, smbuf)
            own_copy(kout_h, agbuf)
        pl.semaphore_wait(barrier, total - 1)

        def chip_dev(d):
            o = lax.rem(ch + d, NCH)
            return {"tile": (o // NG) * 2 + core, "grp": lax.rem(o, NG)}

        if inside:
            sm_a0 = started(Ring(NCH, lambda d: smbuf.at[0, ch, core], lambda d: smbuf.at[0, ch, core], chip_dev))
        halo_x = started(Sides(tx_s.at[0], tx_s.at[0], rx_s))
        if inside:
            s0c = [started(One(kout_h.at[l, ocore], s0buf.at[l], partner)) for l in range(3)]
            sm_a12 = started(Ring(NCH, lambda d: smbuf.at[1:3, ch, core], lambda d: smbuf.at[1:3, ch, core], chip_dev))

        ag = [[] for _ in range(3)]

        def ag_s1(l):
            if not inside:
                return
            s0c[l].recv()
            mine, theirs = ownw[l], s0buf[l]
            first = core == 0
            agbuf[l, core, hi, lo, g] = jnp.concatenate(
                [jnp.where(first, mine, theirs), jnp.where(first, theirs, mine)], axis=0
            ).astype(BF)
            c = Ring(
                H,
                lambda d: agbuf.at[l, core, hi, lo, g],
                lambda d: agbuf.at[l, core, hi, lo, g],
                lambda d: {"tile": tile_of(lax.rem(hi + d, H), lo, core), "grp": g},
            )
            c.start()
            ag[l].append([c])

        def ag_next(l, *copies):
            if not inside:
                return
            for c in ag[l][-1]:
                c.recv()
            for c in copies:
                c.start()
            ag[l].append(copies)

        def ag_s2(l):
            part = agbuf.at[l, core, :, lo, g]
            ag_next(l, One(part, part, xn), One(part, part, yn))

        def ag_s3(l):
            a = agbuf.at[l, core, :, olo, g, :, 0:QH]
            b = agbuf.at[l, core, :, lo, og, :, QH:HALF]
            ag_next(l, One(a, a, yn), One(b, b, xn))

        def ag_s4(l):
            part = agbuf.at[l, core]
            ag_next(l, One(part, part, partner))

        def ag_fin(l):
            if inside:
                for c in ag[l][-1]:
                    c.recv()
                for cs in ag[l]:
                    for c in cs:
                        c.sent()
        def unpack_small(l):
            block = smbuf[l].reshape(KW, SMW)
            second = block[:, 0:KW]
            wbr[l] = second.astype(BF)
            wbT[l] = second.T.astype(BF)
            waT[l] = block[:, KW : KW + 8].astype(BF)
            bbc[l] = jnp.broadcast_to(block[:, KW + 8 : KW + 9], (KW, 128))

        mts, qts = (mt0, mt1, mt2), (mt0, qt1, qt2)
        xss, zss, pks, a2s = (xs0, xs1, xs2), (zs0, zs1, zs2), (pk0, pk1, pk2), (None, as1, as2)

        def pack_nodes(lv, links, used, geometry):
            k, n = links.shape
            links = jnp.where(iota((k, n), 0) < used, links, -1).astype(F32)
            high = links.astype(BF).astype(F32)
            rows = dot(place(8, 3, [(0, 0, 3)]), geometry) + jnp.where(iota((8, n), 0) == 3, 1.0, 0.0)
            pad = jnp.zeros((128 - 2 * k - 8, n), F32)
            pks[lv.index][...] = jnp.concatenate([high, links - high, rows, pad], axis=0).T.astype(BF)

        def edge_columns(lv, i):
            k = lv.slots
            n = LANES // k
            at = pl.ds(pl.multiple_of(i * n, n), n)
            nodes = (iota((n, LANES), 1) >> log2(k) == iota((n, LANES), 0)).astype(F32).astype(BF)
            got = dot(pks[lv.index][at, :], nodes, TN)
            slot = iota((k, LANES), 1) & (k - 1) == iota((k, LANES), 0)
            links = jnp.sum(jnp.where(slot, got[0:k] + got[k : 2 * k], 0.0), axis=0, keepdims=True)
            return links, got[2 * k : 2 * k + 8]

        def take(table, row, lv):
            rows = lv.chunk
            if lv.sources == rows:
                return dot(table[...], one_hot(row, 0, rows))
            n = lv.sources // rows

            def body(k, acc):
                start = pl.multiple_of(k * rows, rows)
                return acc + dot(table[:, pl.ds(start, rows)], one_hot(row, start, rows))

            return lax.fori_loop(0, n, body, jnp.zeros((table.shape[0], LANES), F32))

        def put(acc, values, row, lv):
            rows = lv.chunk
            if lv.sources == rows:
                acc[...] += dot(values, one_hot(row, 0, rows), NT)
                return
            n = lv.sources // rows

            def body(k, _):
                start = pl.multiple_of(k * rows, rows)
                at = pl.ds(start, rows)
                acc[:, at] += dot(values, one_hot(row, start, rows), NT)
                return 0

            lax.fori_loop(0, n, body, 0)

        def edge_geometry(lv, x_table, g_table, first, last):
            l = lv.index

            def body(i, _):
                links, z = edge_columns(lv, i)
                row = links.astype(I32)
                if g_table is None:
                    got = take(x_table, row, lv)
                    xss[l][i] = got[0:C].astype(BF)
                    z = z + got[C : C + 8]
                else:
                    z = z + take(g_table, row, lv)[0:8]
                zss[l][i] = jnp.where(iota((8, LANES), 0) == 4, links, z)
                return 0

            lax.fori_loop(first, last, body, 0)

        def hidden(l, z):
            t1 = dot(waT[l], z.astype(BF))
            a1 = (t1 * sig(t1)).astype(BF)
            t2 = dot(wbT[l], a1) + bbc[l][:, 0:1]
            return (t2 * sig(t2)).astype(BF)

        def edge_hidden(lv):
            l = lv.index

            def body(i, _):
                a2s[l][i] = hidden(l, zss[l][i])
                return 0

            lax.fori_loop(0, lv.steps, body, 0)

        def edges_forward(lv, x_table, first, last):
            l = lv.index
            mask = group_mask(lv.width)

            def body(i, _):
                if x_table is None:
                    x = xss[l][i].astype(F32)
                    a2 = hidden(l, zss[l][i])
                else:
                    x = take(x_table, zss[l][i, 4:5, :].astype(I32), lv)
                    xss[l][i] = x.astype(BF)
                    a2 = a2s[l][i]
                for k in range(lv.blocks):
                    sl = slice(lv.width * k, lv.width * (k + 1))
                    m = dot(spread(x[:, sl], mask), a2[:, sl], NT)
                    at = pl.ds(pl.multiple_of((lv.blocks * i + k) * GROUP, GROUP), GROUP)
                    mts[l][:, at, :] = m.astype(BF).reshape(C, GROUP, KW)
                return 0

            lax.fori_loop(first, last, body, 0)

        def third(l, pair):
            per_half = C // 4
            half, k = pair // per_half, lax.rem(pair, per_half)
            return agbuf[l, half, :, :, :, :, pl.ds(pl.multiple_of(k * 128, 128), 128)].reshape(KW, 2 * C)

        def node_sums(lv):
            l = lv.index
            each = 4

            def body(i, accs):
                w = jnp.concatenate([third(l, each * i + u) for u in range(each)], axis=0)
                out = []
                for odd in range(2):
                    m = jnp.concatenate([mts[l][2 * (each * i + u) + odd] for u in range(each)], axis=1)
                    out.append(accs[odd] + dot(m, w))
                return tuple(out)

            zero = jnp.zeros((lv.nodes, 2 * C), F32)
            even, odd = lax.fori_loop(0, C // 2 // each, body, (zero, zero))
            return even.T[0:C] + odd.T[C:]

        stage = (gbuf, agbuf.at[1], agbuf.at[2])

        def third_grad(lv, gsT):
            l = lv.index
            n = C // 4
            each = 4

            def body(j, _):
                for u in range(each):
                    i = each * j + u
                    both = jnp.concatenate([dot(gsT, mts[l][2 * i]), dot(gsT, mts[l][2 * i + 1])], axis=0)
                    out = both.T.astype(BF).reshape(A, 2, NG, 16, 128)
                    stage[l][i // n, :, :, :, :, pl.ds(pl.multiple_of(lax.rem(i, n) * 128, 128), 128)] = out
                return 0

            lax.fori_loop(0, C // 2 // each, body, 0)

        def node_weights(lv, gsT):
            l = lv.index
            each = 4
            gsT = gsT.astype(F32)
            zero = jnp.zeros(gsT.shape, F32)
            low = jnp.concatenate([gsT, zero], axis=0).T[0 : lv.nodes].astype(BF)
            high = jnp.concatenate([zero, gsT], axis=0).T[0 : lv.nodes].astype(BF)

            def body(j, _):
                for u in range(each):
                    w = third(l, each * j + u)
                    c = 2 * (each * j + u)
                    qts[l][c] = dot(low, w, NT).astype(BF)
                    qts[l][c + 1] = dot(high, w, NT).astype(BF)
                return 0

            lax.fori_loop(0, C // 2 // each, body, 0)

        def edges_backward(lv, acc, first, last):
            l = lv.index
            mask = group_mask(lv.width)
            fold = (iota((C, C * GROUP), 1) >> log2(GROUP) == iota((C, C * GROUP), 0)).astype(F32).astype(BF)

            def body(i, _):
                zb = zss[l][i].astype(BF)
                t1 = dot(waT[l], zb)
                s1 = sig(t1)
                f1 = t1 * s1
                d1 = s1 + f1 * (1.0 - s1)
                a1 = f1.astype(BF)
                t2 = dot(wbT[l], a1) + bbc[l][:, 0:1]
                s2 = sig(t2)
                f2 = t2 * s2
                d2 = s2 + f2 * (1.0 - s2)
                a2 = f2.astype(BF)
                x = xss[l][i].astype(F32)
                g2s, gxs = [], []
                for k in range(lv.blocks):
                    sl = slice(lv.width * k, lv.width * (k + 1))
                    at = pl.ds(pl.multiple_of((lv.blocks * i + k) * GROUP, GROUP), GROUP)
                    q = qts[l][:, at, :].reshape(C * GROUP, KW)
                    g2s.append((dot(q, spread(x[:, sl], mask), TN) * d2[:, sl]).astype(BF))
                    every = dot(q, a2[:, sl])
                    own = (every.reshape(C, GROUP, lv.width) * mask[None]).reshape(C * GROUP, lv.width).astype(BF)
                    gxs.append(dot(fold, own).astype(BF))
                g2 = jnp.concatenate(g2s, axis=1)
                gx = jnp.concatenate(gxs, axis=1)
                g1 = (dot(wbr[l], g2) * d1).astype(BF)
                sm2 = dot(a1, g2, NT)
                p1 = dot(g1, zb, NT)
                p2 = dot(g2, zb, NT)
                gsb[l, :, :, :, 0:KW] += sm2.reshape(NB, 2, 8, KW)
                gsb[l, :, :, :, KW : KW + 8] += p1.reshape(NB, 2, 8, 8)
                gsb[l, :, :, :, KW + 8 : KW + 16] += p2.reshape(NB, 2, 8, 8)
                put(acc, gx, zss[l][i, 4:5, :].astype(I32), lv)
                return 0

            lax.fori_loop(first, last, body, 0)

        def roll_pick(left, right, n_left, left_lane, right_lane):
            lane = iota((1, 128), 1)
            a = pltpu.roll(left, (left_lane - (n_left - 8)) % 128, 1)
            b = pltpu.roll(right, right_lane % 128, 1)
            return jnp.where((lane >= left_lane) & (lane < left_lane + 8), a, 0.0) + jnp.where(
                (lane >= right_lane) & (lane < right_lane + 8), b, 0.0
            )

        def margin_pick(from_left, from_right, n_own, left_at, right_at):
            lane = iota((1, 128), 1)
            a = pltpu.roll(from_left, (0 - right_at) % 128, 1)
            b = pltpu.roll(from_right, (n_own - 8 - left_at) % 128, 1)
            return jnp.where(lane < 8, a, 0.0) + jnp.where((lane >= n_own - 8) & (lane < n_own), b, 0.0)

        ag_s1(0)
        halo_x.recv()
        near, far = (pltpu.roll(rx_s[k].astype(F32), halo, 1) for k in (0, 1))
        extT[:, n0:] = jnp.where(iota((1, 128), 1) < halo, near, far).astype(BF)
        pack_nodes(fine, lkf[...], slf[...], geof[...])
        pack_nodes(mid, lkm[...], slm[...], geom_own[...])
        lkc_wide[...] = jnp.zeros(lkc_wide.shape, F32)
        lkc_wide[0:NC] = lkc[...].astype(F32)
        slc_wide[...] = jnp.ones(slc_wide.shape, I32)
        slc_wide[:, 0:NC] = slc[...]
        eye = place(coarse.slots, coarse.slots, [(0, 0, coarse.slots)])
        high = lkc_wide[...].astype(BF)
        low = (lkc_wide[...] - high.astype(F32)).astype(BF)
        turned = (dot(eye, high, NT) + dot(eye, low, NT)).astype(I32)
        lanes = iota((1, 128), 1)
        own_c = jnp.where(lanes < NC, t * NC + lanes, -1)
        geo = dot(geoc[...], one_hot(own_c, 0, coarse.sources)).astype(BF)
        pack_nodes(coarse, turned, jnp.where(lanes < NC, slc_wide[...], 0), geo)
        to_rows = place(16, 3, [(5, 0, 3)])
        gm[...] = dot(to_rows, geom[...]).astype(BF)
        gc[...] = dot(to_rows, geoc[...]).astype(BF)
        nf, nm, nc = (v[...].astype(F32) for v in (slf, slm, slc_wide))
        blocks = [parm[:, pl.ds(pl.multiple_of(b * NM, NM), NM)].astype(F32)
                  for b in (jnp.maximum(t - 1, 0), t, jnp.minimum(t + 1, T - 1))]
        before, after = (pltpu.roll(jnp.broadcast_to(v, (8, NM)), 8, 1)[0:1] for v in (blocks[0], blocks[2]))
        sides = jnp.where((lanes < 8) & (t > 0), before, jnp.where((lanes >= 8) & (lanes < 16) & (t < T - 1), after, -1.0))
        around = jnp.concatenate([blocks[1], sides], axis=1).astype(I32)
        pw = jnp.where(around < 0, -1, window(around, t * NC, NC, NC))
        edge_geometry(fine, extT, None, 0, fine.steps)
        edge_geometry(mid, None, gm, 0, mid.steps)
        edge_geometry(coarse, None, gc, 0, coarse.steps)
        if inside:
            sm_a0.recv()
            sm_b0 = started(One(smbuf.at[0, :, core], smbuf.at[0, :, core], partner))
            ag_s2(0)
            sm_a12.recv()
            sm_b12 = started(One(smbuf.at[1:3, :, core], smbuf.at[1:3, :, core], partner))
            sm_b0.recv()
        unpack_small(0)
        n = fine.steps
        quarter = n // 4
        cuts = (0, n // 4, n // 2, 3 * n // 4, n)
        edges_forward(fine, None, cuts[0], cuts[1])
        ag_s1(1)
        edges_forward(fine, None, cuts[1], cuts[2])
        ag_s3(0)
        ag_s2(1)
        ag_s1(2)
        edges_forward(fine, None, cuts[2], cuts[3])
        ag_s4(0)
        edges_forward(fine, None, cuts[3], cuts[4])
        ag_s3(1)
        ag_s2(2)
        ag_fin(0)
        v0 = extT[0:C, 0 : fine.nodes].astype(F32) + node_sums(fine) / nf
        v0s[...] = v0

        ones8 = jnp.ones((8, fine.nodes), BF)
        part = dot(jnp.concatenate([split3(v0), ones8], axis=0), ohp[...], NT)
        sums = jnp.concatenate([join3(part[0 : 3 * C]), part[3 * C :]], axis=0)
        tx_w[0] = sums[:, NM:]
        ex_w = started(Sides(tx_w.at[0], tx_w.at[0], rx_w))
        if inside:
            sm_b12.recv()
        unpack_small(1)
        ag_s4(1)
        ex_w.recv()
        own = sums[:, 0:NM] + margin_pick(rx_w[0], rx_w[1], NM, 0, 8)
        inv1 = 1.0 / jnp.maximum(own[C : C + 1], 1.0)
        v1 = own[0:C] / jnp.maximum(own[C : C + 1], 1.0)
        x1b[r, core] = v1.astype(BF)

        def chip_ring(src, dst):
            return Ring(R, src, dst, lambda d: {"tile": lax.rem(r + d, R) * 2 + core, "grp": g})

        ag1 = started(chip_ring(lambda d: x1b.at[r, core], lambda d: x1b.at[r, core]))
        edge_hidden(mid)
        ag_s3(2)
        ag1.recv()
        ag1p = started(One(x1b.at[:, core], x1b.at[:, core], partner))
        unpack_small(2)
        ag1p.recv()
        for k in range(T):
            x1T[:, NM * k : NM * (k + 1)] = x1b[k // 2, k % 2]

        edges_forward(mid, x1T, 0, mid.steps)
        ag_fin(1)
        w1 = v1 + node_sums(mid) / nm
        tx_q[0, 0:C] = w1
        ohq = one_hot(pw, 0, 128)
        part = dot(jnp.concatenate([split3(w1), jnp.ones((8, NM), BF)], axis=0), ohq[:, 0:NM], NT)
        tx_q[0, C : 2 * C + 8] = jnp.concatenate([join3(part[0 : 3 * C]), part[3 * C :]], axis=0)
        ex_q = started(Sides(tx_q.at[0], tx_q.at[0], rx_q))
        edge_hidden(coarse)
        ag_s4(2)
        ex_q.recv()
        own = tx_q[0, C : 2 * C + 8] + margin_pick(rx_q[0, C : 2 * C + 8], rx_q[1, C : 2 * C + 8], NC, NC, NC + 8)
        w1m = roll_pick(rx_q[0, 0:C], rx_q[1, 0:C], NM, 0, 8)
        w1win = jnp.concatenate([w1, w1m], axis=1)
        lane = iota((1, 128), 1)
        mine = lane < NC
        cnt2 = jnp.maximum(own[C : C + 1], 1.0)
        v2 = jnp.where(mine, own[0:C] / cnt2, 0.0)

        x2b[r, core] = v2.astype(BF)
        ag2 = started(chip_ring(lambda d: x2b.at[r, core], lambda d: x2b.at[r, core]))
        ag2.recv()
        ag2p = started(One(x2b.at[:, core], x2b.at[:, core], partner))
        ag2p.recv()
        per = 128 // NC
        cols = []
        for k in range(coarse.sources // 128):
            block = x2b[per * k // 2, 0].astype(F32)
            for u in range(1, per):
                block = block + pltpu.roll(x2b[(per * k + u) // 2, (per * k + u) % 2].astype(F32), NC * u, 1)
            cols.append(block.astype(BF))
        for k, block in enumerate(cols):
            x2T[:, 128 * k : 128 * k + 128] = block
        edges_forward(coarse, x2T, 0, coarse.steps)
        ag_fin(2)
        sc = node_sums(coarse)
        sc = jnp.concatenate([sc, jnp.zeros((C, 128 - NC), F32)], axis=1)
        w2 = v2 + jnp.where(mine, sc / nc, 0.0)
        tx_u[0] = w2
        ex_u = started(Sides(tx_u.at[0], tx_u.at[0], rx_u))
        ex_u.recv()
        w2win = w2 + roll_pick(rx_u[0], rx_u[1], NC, NC, NC + 8)

        y1win = w1win + join3(dot(split3(w2win), ohq))
        y0 = v0s[...] + join3(dot(split3(y1win), ohp[...]))
        s0 = sig(y0)
        f0 = y0 * s0
        layer[...] = f0.astype(BF)
        gy0 = cot[...] * (s0 + f0 * (1.0 - s0))
        gys[...] = gy0
        gy1p = join3(dot(split3(gy0), ohp[...], NT))
        gw2p = join3(dot(split3(gy1p), ohq, NT))
        tx_g[0, 0:C] = gy1p[:, NM:]
        tx_g[0, C : 2 * C] = gw2p
        ex_g = started(Sides(tx_g.at[0], tx_g.at[0], rx_g))
        ex_g.recv()
        gy1 = gy1p[:, 0:NM] + margin_pick(rx_g[0, 0:C], rx_g[1, 0:C], NM, 0, 8)
        gw2 = jnp.where(mine, gw2p + margin_pick(rx_g[0, C:], rx_g[1, C:], NC, NC, NC + 8), 0.0)

        rs = [[] for _ in range(3)]

        def rs_step(l, fix, *copies):
            if not inside:
                return
            if rs[l]:
                for c in rs[l][-1]:
                    c.recv()
            fix()
            for c in copies:
                c.start()
            rs[l].append(copies)

        def rs_s0(l):
            rs_step(l, lambda: None, One(stage[l].at[ocore], rsr0.at[l], partner))

        def rs_s1(l):
            def fix():
                def body(i, _):
                    both = stage[l][core, i].astype(F32) + rsr0[l, i].astype(F32)
                    stage[l][core, i] = both.astype(BF)
                    return 0

                lax.fori_loop(0, H, body, 0)

            rs_step(
                l, fix,
                One(stage[l].at[core, :, olo, og, :, 0:QH], rsr1.at[l, 0], xn),
                One(stage[l].at[core, :, olo, og, :, QH:HALF], rsr1.at[l, 1], yn),
            )

        def rs_s2(l):
            def fix():
                def body(i, _):
                    a = stage[l][core, i, lo, og, :, 0:QH].astype(F32) + rsr1[l, 0, i].astype(F32)
                    stage[l][core, i, lo, og, :, 0:QH] = a.astype(BF)
                    b = stage[l][core, i, olo, g, :, QH:HALF].astype(F32) + rsr1[l, 1, i].astype(F32)
                    stage[l][core, i, olo, g, :, QH:HALF] = b.astype(BF)
                    return 0

                lax.fori_loop(0, H, body, 0)

            rs_step(
                l, fix,
                One(stage[l].at[core, :, lo, og], rsr2.at[l, 0], yn),
                One(stage[l].at[core, :, olo, g], rsr2.at[l, 1], xn),
            )

        def rs_s3(l):
            def fix():
                def body(i, _):
                    a = stage[l][core, i, lo, g].astype(F32) + rsr2[l, 0, i].astype(F32) + rsr2[l, 1, i].astype(F32)
                    stage[l][core, i, lo, g] = a.astype(BF)
                    return 0

                lax.fori_loop(0, H, body, 0)

            rs_step(
                l, fix,
                Ring(
                    H,
                    lambda d: stage[l].at[core, lax.rem(hi + d, H), lo, g],
                    lambda d: rsr3.at[l, d - 1],
                    lambda d: {"tile": tile_of(lax.rem(hi + d, H), lo, core), "grp": g},
                ),
            )

        def rs_s4(l):
            def fix():
                tot = stage[l][core, hi, lo, g].astype(F32)
                for k in range(H - 1):
                    tot = tot + rsr3[l, k].astype(F32)
                rsf[l, 0] = tot[0:8]
                rsf[l, 1] = tot[8:16]

            rs_step(l, fix, One(rsf.at[l, ocore], rsr4.at[l], partner))

        def rs_s5(l):
            if not inside:
                own_copy(stage[l], gwc.at[l])
                return
            for c in rs[l][-1]:
                c.recv()
            gwc[l, core] = rsf[l, core]
            gwc[l, ocore] = rsr4[l]

        gsb[...] = jnp.zeros(gsb.shape, F32)
        gs_copies = {}

        def gs_start(a, b):
            if inside:
                gs_copies[a] = started(One(gsb.at[a:b, :, ocore], rcA.at[a:b], partner))

        def gs_ring(a, b):
            if inside:
                gs_copies[a].recv()
                for l in range(a, b):
                    gsb[l, :, core] += rcA[l]
                gs_copies[a] = started(
                    Ring(
                        NCH,
                        lambda d: gsb.at[a:b, lax.rem(ch + d, NCH), core],
                        lambda d: rcB.at[d - 1, a:b],
                        chip_dev,
                    )
                )

        def gs_end(a, b):
            if not inside:
                gsmall[a:b] = gsb[a:b]
                return
            gs_copies[a].recv()

            def add3(k, acc):
                return acc + rcB[k, a:b]

            gsmall[a:b] = lax.fori_loop(0, NCH - 1, add3, gsb[a:b, ch, core])


        gs2T = jnp.where(mine, gw2 / nc, 0.0).astype(BF)
        node_weights(coarse, gs2T)
        acc2[...] = jnp.zeros(acc2.shape, F32)
        edges_backward(coarse, acc2, 0, coarse.steps)
        a2rows = jnp.concatenate([acc2[...], jnp.zeros(acc2.shape, F32)], axis=0)
        acc2b[...] = a2rows.T.astype(BF).reshape(R, 2, NC, 128)
        r2p = started(One(acc2b.at[:, ocore], rs2a, partner))
        third_grad(coarse, gs2T[:, 0:NC])
        r2p.recv()
        acc2b[:, core] = (acc2b[:, core].astype(F32) + rs2a[...].astype(F32)).astype(BF)
        r2 = started(chip_ring(lambda d: acc2b.at[lax.rem(r + d, R), core], lambda d: rs2buf.at[d - 1]))
        rs_s0(2)
        r2.recv()

        def add2(k, acc):
            return acc + rs2buf[k].astype(F32)

        own2 = lax.fori_loop(0, R - 1, add2, acc2b[r, core].astype(F32))
        own2 = jnp.concatenate([own2, jnp.zeros((128 - NC, 128), F32)], axis=0).T[0:C]
        gv2 = jnp.where(mine, (gw2 + own2) / cnt2, 0.0)
        tx_b[0] = gv2
        ex_b = started(Sides(tx_b.at[0], tx_b.at[0], rx_b))
        rs_s1(2)
        ex_b.recv()
        gv2win = gv2 + roll_pick(rx_b[0], rx_b[1], NC, NC, NC + 8)
        gw1 = gy1 + join3(dot(split3(gv2win), ohq[:, 0:NM]))

        gs1T = (gw1 / nm).astype(BF)
        node_weights(mid, gs1T)
        acc1[...] = jnp.zeros(acc1.shape, F32)
        edges_backward(mid, acc1, 0, mid.steps)
        for k in range(T):
            acc1b[k // 2, k % 2] = acc1[:, NM * k : NM * (k + 1)].astype(BF)
        r1p = started(One(acc1b.at[:, ocore], rs1a, partner))
        rs_s2(2)
        r1p.recv()
        acc1b[:, core] = (acc1b[:, core].astype(F32) + rs1a[...].astype(F32)).astype(BF)
        r1 = started(chip_ring(lambda d: acc1b.at[lax.rem(r + d, R), core], lambda d: rs1buf.at[d - 1]))
        third_grad(mid, gs1T)
        rs_s0(1)
        r1.recv()

        def add1(k, acc):
            return acc + rs1buf[k].astype(F32)

        own1 = lax.fori_loop(0, R - 1, add1, acc1b[r, core].astype(F32))
        gv1 = (gw1 + own1) * inv1
        tx_f[0] = gv1
        ex_f = started(Sides(tx_f.at[0], tx_f.at[0], rx_f))
        gs_start(1, 3)
        rs_s1(1)
        ex_f.recv()
        gv1win = jnp.concatenate([gv1, roll_pick(rx_f[0], rx_f[1], NM, 0, 8)], axis=1)
        gv0 = gys[...] + join3(dot(split3(gv1win), ohp[...]))
        gys[...] = gv0

        gs0 = gv0 / nf
        gs0T = gs0.astype(BF)
        third_grad(fine, gs0T)
        rs_s0(0)
        rs_s3(2)
        rs_s2(1)
        node_weights(fine, gs0T)
        acc0[...] = jnp.zeros(acc0.shape, F32)
        rs_s1(0)
        gs_ring(1, 3)
        edges_backward(fine, acc0, cuts[0], cuts[1])
        rs_s2(0)
        rs_s3(1)
        rs_s4(2)
        edges_backward(fine, acc0, cuts[1], cuts[2])
        rs_s3(0)
        rs_s4(1)
        rs_s5(2)
        edges_backward(fine, acc0, cuts[2], cuts[3])
        rs_s4(0)
        rs_s5(1)
        gs_end(1, 3)
        edges_backward(fine, acc0, cuts[3], cuts[4])
        tx_h[0] = acc0[:, fine.nodes : fine.nodes + 2 * halo]
        ex_h = started(Sides(tx_h.at[0], tx_h.at[0], rx_h))

        gs_start(0, 1)
        rs_s5(0)
        ex_h.recv()
        lane1 = iota((1, 128), 1)
        back = jnp.where(lane1 < halo, pltpu.roll(rx_h[0], halo, 1), pltpu.roll(rx_h[1], halo, 1))
        ohs2 = one_hot(send[...], 0, n0)
        gf = gys[...] + acc0[:, 0 : fine.nodes] + join3(dot(split3(back), ohs2, NT))
        gradf[...] = gf.astype(BF)
        gs_ring(0, 1)
        gs_end(0, 1)

        finish()

    n_sems = (
        2 * (2 * (NCH - 1)) + 4 + 2 * 3 + 3 * (2 * (H - 1) + 4 + 4 + 2) + 4
        + 4 * 7 + 4 * (2 * (T - 1)) + 4 * NCH + 3 * (2 + 4 + 4 + 2 * (H - 1) + 2) + 2 + 2 * (NCH - 1) + 32
    )
    V = pltpu.VMEM
    ls = 3 if inside else 1
    nf, nm_, nc_ = fine.nodes, NM, NC
    scratch = [
        V((C, nf), BF), V((C, nf), F32), V((3, nf), BF), V((3, mid.sources), BF), V((3, coarse.sources), BF),
        V((fine.slots, nf), I32), V((1, nf), I32), V((1, 2 * halo), I32), V((1, nf), I32), V((1, mid.sources), I32),
        V((mid.slots, nm_), I32), V((1, nm_), I32), V((nc_, coarse.slots), I32), V((1, nc_), I32),
        V((3, 6, 8), F32), V((3, 2, 8), F32), V((3, 8, KW), F32), V((ls, 8, HALF), F32),
        V((3, nm_), BF), V((128, coarse.slots), F32), V((1, 128), I32),
        V((nf, 128), BF), V((nm_, 128), BF), V((128, 128), BF), V((16, mid.sources), BF), V((16, coarse.sources), BF),
        V((80, nf + 2 * halo), BF),
        V((3, 2, A, 2, NG, 16, HALF), BF), V((2, A, 2, NG, 16, HALF), BF), V((ls, 8, HALF), F32),
        V((3, NB, 2, 8, SMW), F32), V((3, KW, 8), BF), V((3, KW, KW), BF), V((3, KW, KW), BF), V((3, KW, 128), F32),
        V((C, nf, KW), BF), V((C, nm_, KW), BF), V((C, nc_, KW), BF), V((C, nm_, KW), BF), V((C, nc_, KW), BF),
        V((mid.steps, KW, LANES), BF), V((coarse.steps, KW, LANES), BF),
        V((fine.steps, C, LANES), BF), V((mid.steps, C, LANES), BF), V((coarse.steps, C, LANES), BF),
        V((fine.steps, 8, LANES), F32), V((mid.steps, 8, LANES), F32), V((coarse.steps, 8, LANES), F32),
        V((2 * NM, nf), BF),
        V((1, 80, 128), BF), V((2, 80, 128), BF),
        V((1, C + 8, 128), F32), V((2, C + 8, 128), F32),
        V((1, 2 * C + 8, 128), F32), V((2, 2 * C + 8, 128), F32),
        V((1, C, 128), F32), V((2, C, 128), F32),
        V((1, 2 * C, 128), F32), V((2, 2 * C, 128), F32),
        V((1, C, 128), F32), V((2, C, 128), F32),
        V((1, C, 128), F32), V((2, C, 128), F32),
        V((1, C, 128), F32), V((2, C, 128), F32),
        V((C, mid.sources), BF), V((R, 2, C, 128), BF), V((C, coarse.sources), BF), V((R, 2, C, 128), BF),
        V((C, nf + 2 * halo), F32), V((C, mid.sources), F32), V((C, coarse.sources), F32),
        V((R, 2, C, 128), BF), V((R, 2, NC, 128), BF), V((R, C, 128), BF), V((R, NC, 128), BF),
        V((R - 1, C, 128), BF), V((R - 1, NC, 128), BF), V((C, nf), F32), V((C, nf), F32),
        V((ls, A, 2, NG, 16, HALF), BF), V((ls, 2, A, 16, QH), BF), V((ls, 2, A, 16, HALF), BF),
        V((ls, A - 1, 16, HALF), BF), V((ls, 2, 8, HALF), F32), V((ls, 8, HALF), F32),
        V((3, NB, 2, 8, SMW), F32), V((ls, NB, 8, SMW), F32), V((NB - 1, 3, 8, SMW), F32),
        pltpu.SemaphoreType.DMA((n_sems,)),
    ]
    return kernel, scratch


def adamw(master, moment, square, grad, learn_rate):
    moment_new = B_ONE * moment + (1.0 - B_ONE) * grad
    square_new = B_TWO * square + (1.0 - B_TWO) * grad * grad
    fix_one = 1.0 - B_ONE**STEP
    fix_two = 1.0 - B_TWO**STEP
    master_new = master - learn_rate * (
        moment_new / fix_one / (jnp.sqrt(square_new / fix_two) + EPSILON) + WEIGHT_DECAY * master
    )
    return (master_new, moment_new, square_new)


def make_update(KW, NG, per, inside):
    rates = (RATE_FIRST, RATE_MAIN, RATE_MAIN, RATE_MAIN)

    def kernel(*refs):
        far_in, far_out, near_in, near_out, sems = refs[0:14], refs[14:26], refs[26:40], refs[40:52], refs[52]
        copies = [pltpu.make_async_copy(a, b, sems.at[k]) for k, (a, b) in enumerate(zip(far_in, near_in))]
        for c in copies:
            c.start()
        for c in copies:
            c.wait()
        gwc, gsmall = near_in[0:2]
        order = column_order(KW, NG, False)
        out = []

        def update(k, index, grad):
            new = adamw(*(near_in[2 + 4 * m + k][index] for m in range(3)), grad, rates[k])
            for m in range(3):
                near_out[4 * m + k][index] = new[m]

        def done(k):
            for m in range(3):
                c = pltpu.make_async_copy(near_out[4 * m + k], far_out[4 * m + k], sems.at[14 + 4 * m + k])
                c.start()
                out.append(c)

        for l in range(3):
            update(3, l, gwc[l])
        done(3)
        for l in range(3):
            grad = gsmall[l, :, 0:KW]
            update(2, l, join3(dot(split3(grad), order)) if inside else grad)
        done(2)
        for l in range(3):
            parts = split3(gsmall[l, :, KW:])
            parts = [parts[per * k : per * (k + 1)] for k in range(3)]
            for k, picks, rows in ((0, [(0, 0, 3), (3, 5, 3)], 6), (1, [(0, 3, 1), (1, 11, 1)], 2)):
                pick = place(rows, 128, picks)
                update(k, l, sum(dot(pick, part, NT) for part in parts))
        done(0)
        done(1)
        for c in out:
            c.wait()

    return kernel


def per_device(
    T, NG,
    features, cotangent, geom_fine, geom_mid, geom_coarse, links_fine, slots_fine, send_lists, parent_fine,
    parent_mid, links_mid, slots_mid, links_coarse, slots_coarse, kernel_in, kernel_bias, kernel_mid, kernel_out,
    *moments,
):
    C = features.shape[2]
    KW = kernel_mid.shape[2]
    NM, NC = links_mid.shape[1], links_coarse.shape[1]
    halo = send_lists.shape[1] // 2
    nf = features.shape[1]
    fine = Level(0, nf, links_fine.shape[2], nf + 2 * halo)
    mid = Level(1, NM, links_mid.shape[2], geom_mid.shape[1])
    coarse = Level(2, NC, links_coarse.shape[2], geom_coarse.shape[1])
    per = kernel_mid.shape[1]
    inside = per == 8
    everyone = ("tile", "grp")
    half = C * C // 2
    grid = (3, 2, KW // (32 * NG), 2, NG, 16, half)
    small = kernel_mid
    large = kernel_out.reshape(3, per, C, C).transpose(0, 3, 2, 1).reshape(3, 2, half, per).swapaxes(2, 3)
    if not inside:
        zero = jnp.zeros((3, per, 1), F32)
        first = kernel_in.swapaxes(1, 2)
        bias = kernel_bias.swapaxes(1, 2)
        small = jnp.concatenate(
            [kernel_mid, first[..., 0:3], bias[..., 0:1], zero, first[..., 3:6], bias[..., 1:2],
             jnp.zeros((3, per, 119), F32)], axis=2
        )
        small = lax.all_gather(small, everyone, axis=1, tiled=True).reshape(3, KW // 16, 2, 8, KW + 128)
        large = lax.all_gather(large.astype(BF), everyone, axis=2, tiled=True).reshape(grid)

    kernel, scratch = make_kernel(T, NG, C, KW, fine, mid, coarse, halo, inside)
    S = jax.ShapeDtypeStruct
    vm = pl.BlockSpec(memory_space=pltpu.VMEM)
    far = pl.BlockSpec(memory_space=pl.ANY)
    turn = lambda v: v[0].swapaxes(0, 1)
    operands = (
        turn(features), turn(cotangent), turn(geom_fine), turn(geom_mid), turn(geom_coarse),
        turn(links_fine), slots_fine, send_lists, parent_fine, parent_mid, turn(links_mid), slots_mid,
        links_coarse[0], slots_coarse, kernel_in, kernel_bias, small, large,
    )
    layer, gradf, gwc, gsmall = pl.pallas_call(
        kernel,
        out_shape=(S((C, nf), BF), S((C, nf), BF), S((3, 2, 8, half), F32) if inside else S(grid, BF),
                   S((3, 8, KW + 128) if inside else (3, KW // 16, 2, 8, KW + 128), F32)),
        in_specs=[far] * len(operands),
        out_specs=(vm, vm, vm if inside else far, vm),
        scratch_shapes=scratch,
        compiler_params=pltpu.CompilerParams(
            collective_id=0, has_side_effects=True, vmem_limit_bytes=63 << 20
        ),
        name="layer",
    )(*operands)
    if not inside:
        gwc = gwc.astype(F32).reshape(3, 2, KW, half)
        gwc = lax.psum_scatter(gwc, everyone, scatter_dimension=2, tiled=True)
        gsmall = lax.psum_scatter(gsmall.reshape(3, KW, KW + 128), everyone, scatter_dimension=1, tiled=True)
    gwc = gwc.swapaxes(1, 2).reshape(3, per, C, C).swapaxes(2, 3).reshape(3, per, C * C)
    state = (kernel_in, kernel_bias, kernel_mid, kernel_out) + moments
    new = pl.pallas_call(
        make_update(KW, NG, per, inside),
        out_shape=tuple(S(v.shape, F32) for v in state),
        in_specs=[far] * 14,
        out_specs=(far,) * 12,
        scratch_shapes=[pltpu.VMEM(v.shape, F32) for v in (gwc, gsmall) + state]
        + [pltpu.VMEM(v.shape, F32) for v in state] + [pltpu.SemaphoreType.DMA((26,))],
        compiler_params=pltpu.CompilerParams(vmem_limit_bytes=63 << 20),
        name="update",
    )(gwc, gsmall, *state)
    return (layer.swapaxes(0, 1)[None], gradf.swapaxes(0, 1)[None]) + tuple(new)


def solution(mesh):
    nodes = P("grp", "tile", None)
    rows = P("grp", "tile")
    by_column = P(None, None, ("tile", "grp"))
    by_row = P(None, ("tile", "grp"), None)
    shards = (by_column, by_column, by_row, by_row)
    return jax.shard_map(
        functools.partial(per_device, mesh.shape["tile"], mesh.shape["grp"]),
        mesh=mesh,
        in_specs=(
            nodes, nodes, nodes, P("grp", None, None), P("grp", None, None), nodes, rows, rows, rows,
            P("grp", None), nodes, rows, nodes, rows,
        ) + shards * 3,
        out_specs=(nodes, nodes) + shards * 3,
        check_vma=False,
    )
```

```python
import functools

import jax
import jax.numpy as jnp
from jax import lax
from jax.experimental import pallas as pl
from jax.experimental.pallas import tpu as pltpu
from jax.sharding import PartitionSpec as P

STEP = 5
B_ONE = 0.9
B_TWO = 0.95
EPSILON = 1e-08
WEIGHT_DECAY = 0.1
RATE_FIRST = 0.4
RATE_MAIN = 0.02

BF = jnp.bfloat16
F32 = jnp.float32
I32 = jnp.int32
MESH = pl.DeviceIdType.MESH
NN = ((1,), (0,))
NT = ((1,), (1,))
TN = ((0,), (0,))
LANES = 512
GROUP = 8


def dot(a, b, dims=NN):
    return lax.dot_general(a, b, (dims, ((), ())), preferred_element_type=F32)


def sig(v):
    return 0.5 + 0.5 * jnp.tanh(0.5 * v)


def split3(v):
    high = v.astype(BF)
    rest = v - high.astype(F32)
    mid = rest.astype(BF)
    low = (rest - mid.astype(F32)).astype(BF)
    return jnp.concatenate([high, mid, low], axis=0)


def join3(v):
    n = v.shape[0] // 3
    return v[:n] + v[n : 2 * n] + v[2 * n :]


def iota(shape, dim):
    return lax.broadcasted_iota(I32, shape, dim)


def log2(n):
    assert n & (n - 1) == 0
    return n.bit_length() - 1


def group_mask(width):
    return (iota((GROUP, width), 1) >> log2(width // GROUP) == iota((GROUP, width), 0)).astype(F32)


def one_hot(row, start, rows):
    return (iota((rows, row.shape[1]), 0) + start == row).astype(F32).astype(BF)


def spread(x, mask):
    return (x[:, None, :] * mask[None]).reshape(x.shape[0] * GROUP, mask.shape[1]).astype(BF)


def place(rows, columns, pairs):
    r, c = iota((rows, columns), 0), iota((rows, columns), 1)
    hit = jnp.zeros((rows, columns), F32)
    for row, column, count in pairs:
        hit = hit + jnp.where((r - row == c - column) & (r >= row) & (r < row + count), 1.0, 0.0)
    return hit.astype(BF)


def column_order(KW, NG, natural_rows):
    p = iota((KW, KW), 1 if natural_rows else 0)
    n = iota((KW, KW), 0 if natural_rows else 1)
    shift = log2(NG)
    inner, core, grp, chip = p & 7, (p >> 3) & 1, (p >> 4) & (NG - 1), p >> (4 + shift)
    return ((((((chip << 1) + core) << shift) + grp) << 3) + inner == n).astype(F32).astype(BF)


class Level:
    def __init__(self, index, nodes, slots, sources):
        self.index, self.nodes, self.slots, self.sources = index, nodes, slots, sources
        self.steps = nodes * slots // LANES
        self.width = GROUP * slots
        self.blocks = LANES // self.width
        self.parts = sources // 128


def make_kernel(T, NG, C, KW, fine, mid, coarse, halo, inside):
    H = T // 4
    NCH = T // 2 * NG
    A = KW // (32 * NG)
    NB = KW // 16
    R = T // 2
    HALF = C * C // 2
    QH = HALF // 2
    SMW = KW + 128
    BW = HALF + KW
    levels = (fine, mid, coarse)
    NM, NC = mid.nodes, coarse.nodes

    def kernel(
        feat_h, cot_h, geof_h, geom_h, geoc_h, lkf_h, slf_h, send_h, parf_h, parm_h, lkm_h, slm_h, lkc_h, slc_h,
        kin_h, kb_h, kmid_h, kout_h,
        layer, gradf, gwc, gsmall,
        feat, cot, geof, geom, geoc, lkf, slf, send, parf, parm, lkm, slm, lkc, slc, kin, kb, kmid, ownw,
        geom_own, lkc_wide, slc_wide, pk0, pk1, pk2, gm, gc,
        extT, agbuf, gbuf, s0buf, s0x, smx, smbuf, smfull, waT, wbT, wbr, bbc,
        mt0, mt1, mt2, qt1, qt2, as0, as1, as2, xs0, xs1, xs2, zs0, zs1, zs2,
        ohp, tx_s, rx_s, tx_w, rx_w, tx_q, rx_q, tx_u, rx_u, tx_g, rx_g, tx_b, rx_b, tx_f, rx_f, tx_h, rx_h,
        x1b, x2T, x2b, acc0, acc1, acc2, acc1b, acc2b, rs1a, rs2a, rs1buf, rs2buf, v0s, gys,
        rsr0, rsr1, rsr2, rsr3, rsf, rsr4, gsb, rcA, rcB, sems,
    ):
        t = lax.axis_index("tile")
        g = lax.axis_index("grp")
        core = lax.rem(t, 2)
        r = t // 2
        lo = lax.rem(r, 2)
        hi = r // 2
        ch = r * NG + g
        ocore, olo, og = 1 - core, 1 - lo, 1 - g

        def tile_of(hi_, lo_, core_):
            return (hi_ * 2 + lo_) * 2 + core_

        partner = {"tile": tile_of(hi, lo, ocore), "grp": g}
        xn = {"tile": tile_of(hi, olo, core), "grp": g}
        yn = {"tile": t, "grp": og}

        nil = t - t

        levels_at = [nil + k for k in range(3)]

        def ix(k):
            return levels_at[k]

        counter = [0]
        open_recv, open_send = [], []

        def sem_block(n):
            base = counter[0]
            counter[0] += n
            return base

        def copy(src, dst, ssem, rsem, dev):
            return pltpu.make_async_remote_copy(
                src_ref=src, dst_ref=dst, send_sem=sems.at[nil + ssem], recv_sem=sems.at[nil + rsem],
                device_id=dev, device_id_type=MESH,
            )

        local = sem_block(1)

        def own_copy(src, dst):
            c = pltpu.make_async_copy(src, dst, sems.at[local])
            c.start()
            c.wait()

        class One:
            def __init__(self, src, dst, dev):
                self.s, self.r = sem_block(1), sem_block(1)
                self.parts = (src, dst, self.s, self.r, dev)

            def start(self):
                copy(*self.parts).start()
                open_recv.append(self)
                open_send.append(self)

            def recv(self):
                open_recv.remove(self)
                copy(*self.parts).wait_recv()

            def sent(self):
                open_send.remove(self)
                copy(*self.parts).wait_send()

        class Ring:
            def __init__(self, n, src, dst, dev):
                self.n, self.src, self.dst, self.dev = n, src, dst, dev
                self.s, self.r = sem_block(n - 1), sem_block(n - 1)

            def each(self, f):
                def body(i, _):
                    d = i + 1
                    f(copy(self.src(d), self.dst(d), self.s + i, self.r + i, self.dev(d)))
                    return 0

                lax.fori_loop(0, self.n - 1, body, 0)

            def start(self):
                self.each(lambda c: c.start())
                open_recv.append(self)
                open_send.append(self)

            def recv(self):
                open_recv.remove(self)
                self.each(lambda c: c.wait_recv())

            def sent(self):
                open_send.remove(self)
                self.each(lambda c: c.wait_send())

        class Sides:
            def __init__(self, src_left, src_right, rx):
                self.ls, self.lr, self.rs, self.rr = (sem_block(1) for _ in range(4))
                self.rx = rx
                self.src_left, self.src_right = src_left, src_right

            @property
            def to_left(self):
                return copy(self.src_left, self.rx.at[1], self.ls, self.lr, {"tile": t - 1, "grp": g})

            @property
            def to_right(self):
                return copy(self.src_right, self.rx.at[0], self.rs, self.rr, {"tile": t + 1, "grp": g})

            def start(self):
                open_recv.append(self)
                open_send.append(self)

                @pl.when(t > 0)
                def _():
                    self.to_left.start()

                @pl.when(t < T - 1)
                def _():
                    self.to_right.start()

                @pl.when(t == 0)
                def _():
                    self.rx[0] = jnp.zeros(self.rx.shape[1:], self.rx.dtype)

                @pl.when(t == T - 1)
                def _():
                    self.rx[1] = jnp.zeros(self.rx.shape[1:], self.rx.dtype)

            def recv(self):
                open_recv.remove(self)

                @pl.when(t < T - 1)
                def _():
                    self.to_left.wait_recv()

                @pl.when(t > 0)
                def _():
                    self.to_right.wait_recv()

            def sent(self):
                open_send.remove(self)

                @pl.when(t > 0)
                def _():
                    self.to_left.wait_send()

                @pl.when(t < T - 1)
                def _():
                    self.to_right.wait_send()

        def started(c):
            c.start()
            return c

        def finish():
            for c in tuple(open_recv):
                c.recv()
            for c in tuple(open_send):
                c.sent()

        barrier = pltpu.get_barrier_semaphore()

        def chip_dev(d):
            o = lax.rem(ch + d, NCH)
            return {"tile": (o // NG) * 2 + core, "grp": lax.rem(o, NG)}

        def greet(dev):
            pl.semaphore_signal(barrier, inc=1, device_id=dev, device_id_type=MESH)

        def greet_chip(i, _):
            greet(chip_dev(i + 1))
            return 0

        lax.fori_loop(0, NCH - 1, greet_chip, 0)
        greet(partner)
        beside = t - 1 + 2 * core
        has_beside = (beside >= 0) & (beside < T)

        @pl.when(has_beside)
        def _():
            greet({"tile": beside, "grp": g})

        loads = {}

        def load(name, src, dst):
            c = pltpu.make_async_copy(src, dst, sems.at[sem_block(1)])
            c.start()
            loads[name] = c

        def loaded(*names):
            for name in names:
                loads.pop(name).wait()

        if inside:
            load("kmid", kmid_h, kmid)
            load("kin", kin_h, kin)
            load("kb", kb_h, kb)
        load("feat", feat_h, feat)
        load("geof", geof_h, geof)
        load("send", send_h, send)
        if inside:
            for l in range(3):
                load(l, kout_h.at[l, core], ownw.at[l])
        own_lanes = pl.ds(pl.multiple_of(t * NM, NM), NM)
        for name, src, dst in (
            ("lkf", lkf_h, lkf), ("slf", slf_h, slf), ("lkm", lkm_h, lkm), ("slm", slm_h, slm),
            ("own", geom_h.at[:, own_lanes], geom_own), ("lkc", lkc_h, lkc), ("slc", slc_h, slc), ("geom", geom_h, geom),
            ("geoc", geoc_h, geoc), ("parf", parf_h, parf), ("parm", parm_h, parm), ("cot", cot_h, cot),
        ):
            load(name, src, dst)

        if inside:
            loaded("kmid", "kin", "kb")
            order = column_order(KW, NG, True)
            for l in range(3):
                second = dot(kmid[l].astype(BF), order)
                first = dot(kin[l].astype(BF), place(6, 128, [(0, 0, 3), (3, 5, 3)]), TN)
                first = first + dot(kb[l].astype(BF), place(2, 128, [(0, 3, 1), (1, 8, 1)]), TN)
                if l == 0:
                    smbuf[ch, core] = jnp.concatenate([second, first], axis=1)
                else:
                    smx[l - 1, 0] = second
                    smx[l - 1, 1] = jnp.concatenate([first, jnp.zeros((8, KW - 128), F32)], axis=1)
        pl.semaphore_wait(barrier, NCH + has_beside.astype(I32))
        if inside:
            sm_a0 = started(Ring(NCH, lambda d: smbuf.at[ch, core], lambda d: smbuf.at[ch, core], chip_dev))
            s0c = [[started(One(kout_h.at[l, ocore], s0buf.at[l], partner))] for l in range(3)]
            for l in range(2):
                s0c[l].append(started(One(smx.at[l, ocore], s0x.at[l], partner)))
        loaded("feat", "geof", "send")
        n0 = fine.nodes
        extT[:, 0:n0] = (
            dot(place(80, C, [(0, 0, C)]), feat[...]) + dot(place(80, 3, [(C + 5, 0, 3)]), geof[...])
        ).astype(BF)
        tx_s[0] = dot(extT[:, 0:n0], one_hot(send[...], 0, n0)).astype(BF)
        halo_x = started(Sides(tx_s.at[0], tx_s.at[0], rx_s))

        def window(index, start, n, at):
            off = index - start
            return jnp.where(off < 0, off + at + 8, jnp.where(off >= n, off - n + at + 8, off))

        if not inside:
            own_copy(kmid_h, smfull)
            own_copy(kout_h, agbuf)

        ag = [[] for _ in range(3)]
        wide = (BW, BW, HALF)

        def ag_s1(l):
            if not inside:
                return
            for c in s0c[l]:
                c.recv()
            mine, theirs = ownw[l], s0buf[l]
            if l < 2:
                mine = jnp.concatenate([mine, smx[l, core]], axis=1)
                theirs = jnp.concatenate([theirs, s0x[l]], axis=1)
            first = core == 0
            agbuf[l, core, hi, lo, g, :, 0 : wide[l]] = jnp.concatenate(
                [jnp.where(first, mine, theirs), jnp.where(first, theirs, mine)], axis=0
            ).astype(BF)

            def part(d):
                return agbuf.at[ix(l), core, hi, lo, g, :, 0 : wide[l]]

            c = Ring(H, part, part, lambda d: {"tile": tile_of(lax.rem(hi + d, H), lo, core), "grp": g})
            c.start()
            ag[l].append([c])

        def ag_next(l, *copies):
            if not inside:
                return
            for c in ag[l][-1]:
                c.recv()
            for c in copies:
                c.start()
            ag[l].append(copies)

        def ag_s2(l):
            part = agbuf.at[ix(l), core, :, lo, g, :, 0 : wide[l]]
            ag_next(l, One(part, part, xn), One(part, part, yn))

        def ag_s3(l):
            a = agbuf.at[ix(l), core, :, olo, g, :, 0:QH]
            b = agbuf.at[ix(l), core, :, lo, og, :, QH : wide[l]]
            ag_next(l, One(a, a, yn), One(b, b, xn))

        def ag_s4(l):
            part = agbuf.at[ix(l), core, :, :, :, :, 0 : wide[l]]
            ag_next(l, One(part, part, partner))

        def ag_fin(l):
            if inside:
                for c in ag[l][-1]:
                    c.recv()
                for cs in ag[l]:
                    for c in cs:
                        c.sent()
        def unpack_small(l):
            if not inside:
                block = smfull[l].reshape(KW, SMW)
                second, first = block[:, 0:KW], block[:, KW:]
            elif l == 0:
                block = smbuf[...].reshape(KW, SMW)
                second, first = block[:, 0:KW], block[:, KW:]
            else:
                second = agbuf[l - 1, 0, :, :, :, :, HALF:BW].reshape(KW, KW).astype(F32)
                first = agbuf[l - 1, 1, :, :, :, :, HALF : HALF + 128].reshape(KW, 128).astype(F32)
            wbr[l] = second.astype(BF)
            wbT[l] = second.T.astype(BF)
            waT[l] = first[:, 0:8].astype(BF)
            bbc[l] = jnp.broadcast_to(first[:, 8:9], (KW, 128))

        mts, qts = (mt0, mt1, mt2), (mt0, qt1, qt2)
        xss, zss, pks, a2s = (xs0, xs1, xs2), (zs0, zs1, zs2), (pk0, pk1, pk2), (as0, as1, as2)

        def pack_nodes(lv, links, used, geometry):
            k, n = links.shape
            links = jnp.where(iota((k, n), 0) < used, links, -1).astype(F32)
            high = links.astype(BF).astype(F32)
            rows = dot(place(8, 3, [(0, 0, 3)]), geometry) + jnp.where(iota((8, n), 0) == 3, 1.0, 0.0)
            pad = jnp.zeros((128 - 2 * k - 8, n), F32)
            pks[lv.index][...] = jnp.concatenate([high, links - high, rows, pad], axis=0).T.astype(BF)

        def edge_columns(lv, i):
            k = lv.slots
            n = LANES // k
            at = pl.ds(pl.multiple_of(i * n, n), n)
            nodes = (iota((n, LANES), 1) >> log2(k) == iota((n, LANES), 0)).astype(F32).astype(BF)
            got = dot(pks[lv.index][at, :], nodes, TN)
            slot = iota((k, LANES), 1) & (k - 1) == iota((k, LANES), 0)
            links = jnp.sum(jnp.where(slot, got[0:k] + got[k : 2 * k], 0.0), axis=0, keepdims=True)
            return links, got[2 * k : 2 * k + 8]

        def take(table, row, lv, rows):
            top, hot = row >> 7, one_hot(row & 127, 0, 128)
            n = min(lv.parts, 16)

            def some(first):
                got = dot(table(first, n), hot)
                acc = jnp.zeros((rows, LANES), F32)
                for h in range(n):
                    acc = acc + jnp.where(top == first + h, got[rows * h : rows * (h + 1)], 0.0)
                return acc

            if n == lv.parts:
                return some(0)
            return lax.fori_loop(0, lv.parts // n, lambda k, acc: acc + some(k * n), jnp.zeros((rows, LANES), F32))

        def put(acc, values, row, lv):
            top, hot = row >> 7, one_hot(row & 127, 0, 128)
            n = min(lv.parts, 16)

            def some(first):
                each = [values * jnp.where(top == first + h, 1.0, 0.0).astype(BF) for h in range(n)]
                acc[pl.ds(first, n)] += dot(jnp.concatenate(each, axis=0), hot, NT).reshape(n, C, 128)

            if n == lv.parts:
                some(0)
                return

            def body(k, _):
                some(k * n)
                return 0

            lax.fori_loop(0, lv.parts // n, body, 0)

        def edge_geometry(lv, x_table, g_table, first, last):
            l = lv.index

            def body(i, _):
                links, z = edge_columns(lv, i)
                row = links.astype(I32)
                if g_table is None:
                    got = dot(x_table[...], one_hot(row, 0, lv.sources))
                    xss[l][i] = got[0:C].astype(BF)
                    z = z + got[C : C + 8]
                else:
                    z = z + take(g_table, row, lv, 8)
                zss[l][i] = jnp.where(iota((8, LANES), 0) == 4, links, z)
                return 0

            lax.fori_loop(first, last, body, 0)

        def hidden(l, z):
            t1 = dot(waT[l], z.astype(BF))
            a1 = (t1 * sig(t1)).astype(BF)
            t2 = dot(wbT[l], a1) + bbc[l][:, 0:1]
            return (t2 * sig(t2)).astype(BF)

        def edge_hidden(lv):
            l = lv.index

            def body(i, _):
                a2s[l][i] = hidden(l, zss[l][i])
                return 0

            lax.fori_loop(0, lv.steps, body, 0)

        def at_step(i, events):
            for when, call in events:

                @pl.when(i == when)
                def _():
                    call()

        def edges_forward(lv, x_table, events=()):
            l = lv.index
            mask = group_mask(lv.width)

            def body(i, _):
                at_step(i, events)
                if x_table is None:
                    x = xss[l][i].astype(F32)
                    a2 = hidden(l, zss[l][i])
                    a2s[l][i] = a2
                else:
                    x = take(x_table, zss[l][i, 4:5, :].astype(I32), lv, C)
                    xss[l][i] = x.astype(BF)
                    a2 = a2s[l][i]
                for k in range(lv.blocks):
                    sl = slice(lv.width * k, lv.width * (k + 1))
                    m = dot(spread(x[:, sl], mask), a2[:, sl], NT)
                    mts[l][:, lv.blocks * i + k] = m.astype(BF).reshape(C // 2, 2 * GROUP, KW)
                return 0

            lax.fori_loop(0, lv.steps, body, 0)

        def third(l, pair):
            per_half = C // 4
            half, k = pair // per_half, lax.rem(pair, per_half)
            return agbuf[l, half, :, :, :, :, pl.ds(pl.multiple_of(k * 128, 128), 128)].reshape(KW, 2 * C)

        def node_sums(lv):
            l, n = lv.index, lv.nodes
            each = 4

            def body(i, acc):
                w = jnp.concatenate([third(l, each * i + u) for u in range(each)], axis=0)
                m = jnp.concatenate([mts[l][each * i + u].reshape(2 * n, KW) for u in range(each)], axis=1)
                return acc + dot(m, w)

            acc = lax.fori_loop(0, C // 2 // each, body, jnp.zeros((2 * n, 2 * C), F32))
            acc = acc.reshape(n // GROUP, 2, GROUP, 2 * C)
            both = acc[:, 0].reshape(n, 2 * C) + pltpu.roll(acc[:, 1].reshape(n, 2 * C), C, 1)
            return both.T[0:C]

        def by_parity(lv, gsT):
            n = lv.nodes
            gsT = gsT.astype(F32)
            even = jnp.concatenate([gsT, jnp.zeros(gsT.shape, F32)], axis=0).T[0:n]
            odd = pltpu.roll(even, C, 1)
            shape = (n // GROUP, 1, GROUP, 2 * C)
            return jnp.concatenate([even.reshape(shape), odd.reshape(shape)], axis=1).reshape(2 * n, 2 * C)

        def stage(l):
            return agbuf.at[ix(l), :, :, :, :, :, 0:HALF] if l else gbuf

        def third_grad(lv, gs):
            l = lv.index
            n = C // 4
            each = 4
            turned = gs.T.astype(BF)

            def body(j, _):
                for u in range(each):
                    i = each * j + u
                    both = dot(turned, mts[l][i].reshape(2 * lv.nodes, KW))
                    out = both.T.astype(BF).reshape(A, 2, NG, 16, 128)
                    stage(l)[i // n, :, :, :, :, pl.ds(pl.multiple_of(lax.rem(i, n) * 128, 128), 128)] = out
                return 0

            lax.fori_loop(0, C // 2 // each, body, 0)

        def node_weights(lv, gs):
            l = lv.index
            each = 4
            gs = gs.astype(BF)

            def body(j, _):
                for u in range(each):
                    i = each * j + u
                    q = dot(gs, third(l, i), NT)
                    qts[l][i] = q.astype(BF).reshape(lv.nodes // GROUP, 2 * GROUP, KW)
                return 0

            lax.fori_loop(0, C // 2 // each, body, 0)

        def source_grads(lv, acc, events=()):
            l = lv.index
            mask = group_mask(lv.width)
            fold = (iota((C, C * GROUP), 1) >> log2(GROUP) == iota((C, C * GROUP), 0)).astype(F32).astype(BF)

            def body(i, _):
                at_step(i, events)
                gxs = []
                for k in range(lv.blocks):
                    sl = slice(lv.width * k, lv.width * (k + 1))
                    q = qts[l][:, lv.blocks * i + k].reshape(C * GROUP, KW)
                    every = dot(q, a2s[l][i, :, sl])
                    own = (every.reshape(C, GROUP, lv.width) * mask[None]).reshape(C * GROUP, lv.width).astype(BF)
                    gxs.append(own)
                gx = dot(fold, jnp.concatenate(gxs, axis=1)).astype(BF)
                put(acc, gx, zss[l][i, 4:5, :].astype(I32), lv)
                return 0

            lax.fori_loop(0, lv.steps, body, 0)

        def weight_grads(lv, first, last, events=()):
            l = lv.index
            mask = group_mask(lv.width)

            def body(i, _):
                at_step(i, events)
                zb = zss[l][i].astype(BF)
                t1 = dot(waT[l], zb)
                s1 = sig(t1)
                f1 = t1 * s1
                d1 = s1 + f1 * (1.0 - s1)
                a1 = f1.astype(BF)
                t2 = dot(wbT[l], a1) + bbc[l][:, 0:1]
                s2 = sig(t2)
                d2 = s2 + t2 * s2 * (1.0 - s2)
                x = xss[l][i].astype(F32)
                g2s = []
                for k in range(lv.blocks):
                    sl = slice(lv.width * k, lv.width * (k + 1))
                    q = qts[l][:, lv.blocks * i + k].reshape(C * GROUP, KW)
                    g2s.append((dot(q, spread(x[:, sl], mask), TN) * d2[:, sl]).astype(BF))
                g2 = jnp.concatenate(g2s, axis=1)
                g1 = (dot(wbr[l], g2) * d1).astype(BF)
                sm2 = dot(a1, g2, NT)
                p1 = dot(g1, zb, NT)
                p2 = dot(g2, zb, NT)
                gsb[l, :, :, :, 0:KW] += sm2.reshape(NB, 2, 8, KW)
                gsb[l, :, :, :, KW : KW + 8] += p1.reshape(NB, 2, 8, 8)
                gsb[l, :, :, :, KW + 8 : KW + 16] += p2.reshape(NB, 2, 8, 8)
                return 0

            lax.fori_loop(first, last, body, 0)

        def roll_pick(left, right, n_left, left_lane, right_lane):
            lane = iota((1, 128), 1)
            a = pltpu.roll(left, (left_lane - (n_left - 8)) % 128, 1)
            b = pltpu.roll(right, right_lane % 128, 1)
            return jnp.where((lane >= left_lane) & (lane < left_lane + 8), a, 0.0) + jnp.where(
                (lane >= right_lane) & (lane < right_lane + 8), b, 0.0
            )

        def margin_pick(from_left, from_right, n_own, left_at, right_at):
            lane = iota((1, 128), 1)
            a = pltpu.roll(from_left, (0 - right_at) % 128, 1)
            b = pltpu.roll(from_right, (n_own - 8 - left_at) % 128, 1)
            return jnp.where(lane < 8, a, 0.0) + jnp.where((lane >= n_own - 8) & (lane < n_own), b, 0.0)

        if inside:
            loaded(0, 1, 2)
        ag_s1(0)
        loaded("lkf", "slf", "parf")
        pack_nodes(fine, lkf[...], slf[...], geof[...])
        ohp[...] = one_hot(window(parf[...], t * NM, NM, NM), 0, 2 * NM)
        halo_x.recv()
        near, far = (pltpu.roll(rx_s[k].astype(F32), halo, 1) for k in (0, 1))
        extT[:, n0:] = jnp.where(iota((1, 128), 1) < halo, near, far).astype(BF)
        edge_geometry(fine, extT, None, 0, fine.steps)
        if inside:
            sm_a0.recv()
            sm_b0 = started(One(smbuf.at[:, core], smbuf.at[:, core], partner))
        ag_s2(0)
        ag_s1(1)
        loaded("lkm", "slm", "own", "lkc", "slc", "geom", "geoc", "parm", "cot")
        pack_nodes(mid, lkm[...], slm[...], geom_own[...])
        lkc_wide[...] = jnp.zeros(lkc_wide.shape, F32)
        lkc_wide[0:NC] = lkc[...].astype(F32)
        slc_wide[...] = jnp.ones(slc_wide.shape, I32)
        slc_wide[:, 0:NC] = slc[...]
        eye = place(coarse.slots, coarse.slots, [(0, 0, coarse.slots)])
        high = lkc_wide[...].astype(BF)
        low = (lkc_wide[...] - high.astype(F32)).astype(BF)
        turned = (dot(eye, high, NT) + dot(eye, low, NT)).astype(I32)
        lanes = iota((1, 128), 1)
        own_c = jnp.where(lanes < NC, t * NC + lanes, -1)
        geo = dot(geoc[...], one_hot(own_c, 0, coarse.sources)).astype(BF)
        pack_nodes(coarse, turned, jnp.where(lanes < NC, slc_wide[...], 0), geo)
        to_rows = place(8, 3, [(5, 0, 3)])
        for table, source, lv in ((gm, geom, mid), (gc, geoc, coarse)):
            rows = dot(to_rows, source[...])
            for k in range(lv.parts):
                table[k] = rows[:, 128 * k : 128 * (k + 1)]
        nf, nm, nc = (v[...].astype(F32) for v in (slf, slm, slc_wide))
        blocks = [parm[:, pl.ds(pl.multiple_of(b * NM, NM), NM)].astype(F32)
                  for b in (jnp.maximum(t - 1, 0), t, jnp.minimum(t + 1, T - 1))]
        before, after = (pltpu.roll(jnp.broadcast_to(v, (8, NM)), 8, 1)[0:1] for v in (blocks[0], blocks[2]))
        sides = jnp.where((lanes < 8) & (t > 0), before, jnp.where((lanes >= 8) & (lanes < 16) & (t < T - 1), after, -1.0))
        around = jnp.concatenate([blocks[1], sides], axis=1).astype(I32)
        pw = jnp.where(around < 0, -1, window(around, t * NC, NC, NC))
        if inside:
            sm_b0.recv()
        unpack_small(0)
        edges_forward(
            fine, None,
            [(8, lambda: ag_s3(0)), (8, lambda: ag_s1(2)), (12, lambda: ag_s4(0)), (12, lambda: ag_s2(1))],
        )
        g_rows = lambda table: lambda first, n: table[pl.ds(first, n)].reshape(n * 8, 128).astype(BF)
        edge_geometry(mid, None, g_rows(gm), 0, mid.steps)
        edge_geometry(coarse, None, g_rows(gc), 0, coarse.steps)
        ag_fin(0)
        v0 = extT[0:C, 0 : fine.nodes].astype(F32) + node_sums(fine) / nf
        v0s[...] = v0

        ones8 = jnp.ones((8, fine.nodes), BF)
        part = dot(jnp.concatenate([split3(v0), ones8], axis=0), ohp[...], NT)
        sums = jnp.concatenate([join3(part[0 : 3 * C]), part[3 * C :]], axis=0)
        tx_w[0] = sums[:, NM:]
        ex_w = started(Sides(tx_w.at[0], tx_w.at[0], rx_w))
        unpack_small(1)
        ag_s3(1)
        ex_w.recv()
        own = sums[:, 0:NM] + margin_pick(rx_w[0], rx_w[1], NM, 0, 8)
        inv1 = 1.0 / jnp.maximum(own[C : C + 1], 1.0)
        v1 = own[0:C] / jnp.maximum(own[C : C + 1], 1.0)
        x1b[r, core] = v1.astype(BF)

        def chip_ring(src, dst):
            return Ring(R, src, dst, lambda d: {"tile": lax.rem(r + d, R) * 2 + core, "grp": g})

        ag1 = started(chip_ring(lambda d: x1b.at[r, core], lambda d: x1b.at[r, core]))
        ag_s2(2)
        edge_hidden(mid)
        ag_s4(1)
        ag1.recv()
        ag1p = started(One(x1b.at[:, core], x1b.at[:, core], partner))
        ag1p.recv()

        def x1_rows(first, n):
            return x1b[pl.ds(first // 2, n // 2)].reshape(n * C, 128)

        edges_forward(mid, x1_rows, [(4, lambda: ag_s3(2))])
        ag_fin(1)
        unpack_small(2)
        w1 = v1 + node_sums(mid) / nm
        tx_q[0, 0:C] = w1
        ohq = one_hot(pw, 0, 128)
        part = dot(jnp.concatenate([split3(w1), jnp.ones((8, NM), BF)], axis=0), ohq[:, 0:NM], NT)
        tx_q[0, C : 2 * C + 8] = jnp.concatenate([join3(part[0 : 3 * C]), part[3 * C :]], axis=0)
        ex_q = started(Sides(tx_q.at[0], tx_q.at[0], rx_q))
        edge_hidden(coarse)
        ag_s4(2)
        ex_q.recv()
        own = tx_q[0, C : 2 * C + 8] + margin_pick(rx_q[0, C : 2 * C + 8], rx_q[1, C : 2 * C + 8], NC, NC, NC + 8)
        w1m = roll_pick(rx_q[0, 0:C], rx_q[1, 0:C], NM, 0, 8)
        w1win = jnp.concatenate([w1, w1m], axis=1)
        lane = iota((1, 128), 1)
        mine = lane < NC
        cnt2 = jnp.maximum(own[C : C + 1], 1.0)
        v2 = jnp.where(mine, own[0:C] / cnt2, 0.0)

        x2b[r, core] = v2.astype(BF)
        ag2 = started(chip_ring(lambda d: x2b.at[r, core], lambda d: x2b.at[r, core]))
        ag2.recv()
        ag2p = started(One(x2b.at[:, core], x2b.at[:, core], partner))
        ag2p.recv()
        per = 128 // NC
        cols = []
        for k in range(coarse.sources // 128):
            block = x2b[per * k // 2, 0].astype(F32)
            for u in range(1, per):
                block = block + pltpu.roll(x2b[(per * k + u) // 2, (per * k + u) % 2].astype(F32), NC * u, 1)
            cols.append(block.astype(BF))
        for k, block in enumerate(cols):
            x2T[k] = block
        edges_forward(coarse, lambda first, n: x2T[pl.ds(first, n)].reshape(n * C, 128))
        ag_fin(2)
        sc = node_sums(coarse)
        sc = jnp.concatenate([sc, jnp.zeros((C, 128 - NC), F32)], axis=1)
        w2 = v2 + jnp.where(mine, sc / nc, 0.0)
        tx_u[0] = w2
        ex_u = started(Sides(tx_u.at[0], tx_u.at[0], rx_u))
        ex_u.recv()
        w2win = w2 + roll_pick(rx_u[0], rx_u[1], NC, NC, NC + 8)

        y1win = w1win + join3(dot(split3(w2win), ohq))
        y0 = v0s[...] + join3(dot(split3(y1win), ohp[...]))
        s0 = sig(y0)
        f0 = y0 * s0
        layer[...] = f0.astype(BF)
        gy0 = cot[...] * (s0 + f0 * (1.0 - s0))
        gys[...] = gy0
        gy1p = join3(dot(split3(gy0), ohp[...], NT))
        gw2p = join3(dot(split3(gy1p), ohq, NT))
        tx_g[0, 0:C] = gy1p[:, NM:]
        tx_g[0, C : 2 * C] = gw2p
        ex_g = started(Sides(tx_g.at[0], tx_g.at[0], rx_g))
        ex_g.recv()
        gy1 = gy1p[:, 0:NM] + margin_pick(rx_g[0, 0:C], rx_g[1, 0:C], NM, 0, 8)
        gw2 = jnp.where(mine, gw2p + margin_pick(rx_g[0, C:], rx_g[1, C:], NC, NC, NC + 8), 0.0)

        rs = [[] for _ in range(3)]

        def rs_step(l, fix, *copies):
            if not inside:
                return
            if rs[l]:
                for c in rs[l][-1]:
                    c.recv()
            fix()
            for c in copies:
                c.start()
            rs[l].append(copies)

        def rs_s0(l):
            rs_step(l, lambda: None, One(stage(l).at[ocore], rsr0.at[ix(l % 2)], partner))

        def rs_s1(l):
            def fix():
                def body(i, _):
                    both = stage(l)[core, i].astype(F32) + rsr0[l % 2, i].astype(F32)
                    stage(l)[core, i] = both.astype(BF)
                    return 0

                lax.fori_loop(0, H, body, 0)

            rs_step(
                l, fix,
                One(stage(l).at[core, :, olo, og, :, 0:QH], rsr1.at[ix(l), ix(0)], xn),
                One(stage(l).at[core, :, olo, og, :, QH:HALF], rsr1.at[ix(l), ix(1)], yn),
            )

        def rs_s2(l):
            def fix():
                def body(i, _):
                    a = stage(l)[core, i, lo, og, :, 0:QH].astype(F32) + rsr1[l, 0, i].astype(F32)
                    stage(l)[core, i, lo, og, :, 0:QH] = a.astype(BF)
                    b = stage(l)[core, i, olo, g, :, QH:HALF].astype(F32) + rsr1[l, 1, i].astype(F32)
                    stage(l)[core, i, olo, g, :, QH:HALF] = b.astype(BF)
                    return 0

                lax.fori_loop(0, H, body, 0)

            rs_step(
                l, fix,
                One(stage(l).at[core, :, lo, og], rsr2.at[ix(l), ix(0)], yn),
                One(stage(l).at[core, :, olo, g], rsr2.at[ix(l), ix(1)], xn),
            )

        def rs_s3(l):
            def fix():
                def body(i, _):
                    a = stage(l)[core, i, lo, g].astype(F32) + rsr2[l, 0, i].astype(F32) + rsr2[l, 1, i].astype(F32)
                    stage(l)[core, i, lo, g] = a.astype(BF)
                    return 0

                lax.fori_loop(0, H, body, 0)

            rs_step(
                l, fix,
                Ring(
                    H,
                    lambda d: stage(l).at[core, lax.rem(hi + d, H), lo, g],
                    lambda d: rsr3.at[ix(l), d - 1],
                    lambda d: {"tile": tile_of(lax.rem(hi + d, H), lo, core), "grp": g},
                ),
            )

        def rs_s4(l):
            def fix():
                tot = stage(l)[core, hi, lo, g].astype(F32)
                for k in range(H - 1):
                    tot = tot + rsr3[l, k].astype(F32)
                rsf[l, 0] = tot[0:8]
                rsf[l, 1] = tot[8:16]

            rs_step(l, fix, One(rsf.at[ix(l), ocore], rsr4.at[ix(l)], partner))

        def rs_s5(l):
            if not inside:
                own_copy(stage(l), gwc.at[l])
                return
            for c in rs[l][-1]:
                c.recv()
            gwc[l, core] = rsf[l, core]
            gwc[l, ocore] = rsr4[l]

        gsb[...] = jnp.zeros(gsb.shape, F32)
        gs_copies = {}

        def gs_start(a, b):
            if inside:
                gs_copies[a] = started(One(gsb.at[a:b, :, ocore], rcA.at[a:b], partner))

        def gs_ring(a, b):
            if inside:
                gs_copies[a].recv()
                for l in range(a, b):
                    gsb[l, :, core] += rcA[l]
                gs_copies[a] = started(
                    Ring(
                        NCH,
                        lambda d: gsb.at[a:b, lax.rem(ch + d, NCH), core],
                        lambda d: rcB.at[d - 1, a:b],
                        chip_dev,
                    )
                )

        def gs_end(a, b):
            if not inside:
                gsmall[a:b] = gsb[a:b]
                return
            gs_copies[a].recv()

            def add3(k, acc):
                return acc + rcB[k, a:b]

            gsmall[a:b] = lax.fori_loop(0, NCH - 1, add3, gsb[a:b, ch, core])


        gs2T = jnp.where(mine, gw2 / nc, 0.0).astype(BF)
        gs2 = by_parity(coarse, gs2T)
        node_weights(coarse, gs2)
        acc2[...] = jnp.zeros(acc2.shape, F32)
        source_grads(coarse, acc2)
        zero = jnp.zeros((C, 128), F32)
        for k in range(coarse.parts):
            rows = jnp.concatenate([acc2[k], zero], axis=0).T.astype(BF)
            acc2b[per // 2 * k : per // 2 * (k + 1)] = rows.reshape(per // 2, 2, NC, 128)
        r2p = started(One(acc2b.at[:, ocore], rs2a, partner))
        weight_grads(coarse, 0, 1)
        r2p.recv()
        acc2b[:, core] = (acc2b[:, core].astype(F32) + rs2a[...].astype(F32)).astype(BF)
        r2 = started(chip_ring(lambda d: acc2b.at[lax.rem(r + d, R), core], lambda d: rs2buf.at[d - 1]))
        weight_grads(coarse, 1, coarse.steps)
        third_grad(coarse, gs2)
        r2.recv()

        def add2(k, acc):
            return acc + rs2buf[k].astype(F32)

        own2 = lax.fori_loop(0, R - 1, add2, acc2b[r, core].astype(F32))
        own2 = jnp.concatenate([own2, jnp.zeros((128 - NC, 128), F32)], axis=0).T[0:C]
        gv2 = jnp.where(mine, (gw2 + own2) / cnt2, 0.0)
        tx_b[0] = gv2
        ex_b = started(Sides(tx_b.at[0], tx_b.at[0], rx_b))
        rs_s0(2)
        ex_b.recv()
        gv2win = gv2 + roll_pick(rx_b[0], rx_b[1], NC, NC, NC + 8)
        gw1 = gy1 + join3(dot(split3(gv2win), ohq[:, 0:NM]))

        gs1T = (gw1 / nm).astype(BF)
        gs1 = by_parity(mid, gs1T)
        node_weights(mid, gs1)
        acc1[...] = jnp.zeros(acc1.shape, F32)
        rs_s1(2)
        source_grads(mid, acc1, [(5, lambda: rs_s2(2))])
        acc1b[...] = acc1[...].astype(BF).reshape(acc1b.shape)
        r1p = started(One(acc1b.at[:, ocore], rs1a, partner))
        half = mid.steps // 2
        third_grad(mid, gs1)
        r1p.recv()
        acc1b[:, core] = (acc1b[:, core].astype(F32) + rs1a[...].astype(F32)).astype(BF)
        r1 = started(chip_ring(lambda d: acc1b.at[lax.rem(r + d, R), core], lambda d: rs1buf.at[d - 1]))
        rs_s0(1)
        weight_grads(mid, 0, half)
        r1.recv()

        def add1(k, acc):
            return acc + rs1buf[k].astype(F32)

        own1 = lax.fori_loop(0, R - 1, add1, acc1b[r, core].astype(F32))
        gv1 = (gw1 + own1) * inv1
        tx_f[0] = gv1
        ex_f = started(Sides(tx_f.at[0], tx_f.at[0], rx_f))
        rs_s1(1)
        rs_s3(2)
        weight_grads(mid, half, mid.steps)
        ex_f.recv()
        gv1win = jnp.concatenate([gv1, roll_pick(rx_f[0], rx_f[1], NM, 0, 8)], axis=1)
        gv0 = gys[...] + join3(dot(split3(gv1win), ohp[...]))
        gys[...] = gv0

        gs0 = gv0 / nf
        gs0T = gs0.astype(BF)
        gs0 = by_parity(fine, gs0T)
        rs_s2(1)
        third_grad(fine, gs0)
        rs_s0(0)
        node_weights(fine, gs0)
        rs_s1(0)
        rs_s3(1)
        rs_s4(2)
        weight_grads(
            fine, 0, fine.steps,
            [(1, lambda: gs_start(1, 3)), (5, lambda: rs_s2(0)), (6, lambda: rs_s4(1)), (7, lambda: rs_s5(2)),
             (8, lambda: gs_ring(1, 3)), (9, lambda: rs_s5(1)), (13, lambda: rs_s3(0))],
        )
        gs_start(0, 1)
        acc0[...] = jnp.zeros(acc0.shape, F32)
        source_grads(
            fine, acc0, [(2, lambda: gs_ring(0, 1)), (6, lambda: gs_end(1, 3)), (12, lambda: rs_s4(0))]
        )
        tx_h[0] = acc0[fine.parts - 1]
        ex_h = started(Sides(tx_h.at[0], tx_h.at[0], rx_h))
        rs_s5(0)
        gs_end(0, 1)
        ex_h.recv()
        lane1 = iota((1, 128), 1)
        back = jnp.where(lane1 < halo, pltpu.roll(rx_h[0], halo, 1), pltpu.roll(rx_h[1], halo, 1))
        ohs2 = one_hot(send[...], 0, n0)
        own0 = jnp.concatenate([acc0[k] for k in range(fine.parts - 1)], axis=1)
        gf = gys[...] + own0 + join3(dot(split3(back), ohs2, NT))
        gradf[...] = gf.astype(BF)
        finish()

    n_sems = (
        2 * (2 * (NCH - 1)) + 4 + 2 * 3 + 3 * (2 * (H - 1) + 4 + 4 + 2) + 4
        + 4 * 7 + 4 * (2 * (T - 1)) + 4 * NCH + 3 * (2 + 4 + 4 + 2 * (H - 1) + 2) + 2 + 2 * (NCH - 1) + 32
    )
    V = pltpu.VMEM
    ls = 3 if inside else 1
    by_group = lambda n: V((C // 2, n // GROUP, 2 * GROUP, KW), BF)
    nf, nm_, nc_ = fine.nodes, NM, NC
    scratch = [
        V((C, nf), BF), V((C, nf), F32), V((3, nf), BF), V((3, mid.sources), BF), V((3, coarse.sources), BF),
        V((fine.slots, nf), I32), V((1, nf), I32), V((1, 2 * halo), I32), V((1, nf), I32), V((1, mid.sources), I32),
        V((mid.slots, nm_), I32), V((1, nm_), I32), V((nc_, coarse.slots), I32), V((1, nc_), I32),
        V((3, 6, 8), F32), V((3, 2, 8), F32), V((3, 8, KW), F32), V((ls, 8, HALF), F32),
        V((3, nm_), BF), V((128, coarse.slots), F32), V((1, 128), I32),
        V((nf, 128), BF), V((nm_, 128), BF), V((128, 128), BF), V((mid.parts, 8, 128), F32), V((coarse.parts, 8, 128), F32),
        V((80, nf + 2 * halo), BF),
        V((3, 2, A, 2, NG, 16, BW if inside else HALF), BF), V((2, A, 2, NG, 16, HALF), BF), V((ls, 8, HALF), F32),
        V((2, 8, KW), F32), V((2, 2, 8, KW), F32),
        V((NB, 2, 8, SMW), F32), V((1 if inside else 3, 1 if inside else NB, 2, 8, SMW), F32), V((3, KW, 8), BF), V((3, KW, KW), BF), V((3, KW, KW), BF), V((3, KW, 128), F32),
        by_group(nf), by_group(nm_), by_group(nc_), by_group(nm_), by_group(nc_),
        V((fine.steps, KW, LANES), BF), V((mid.steps, KW, LANES), BF), V((coarse.steps, KW, LANES), BF),
        V((fine.steps, C, LANES), BF), V((mid.steps, C, LANES), BF), V((coarse.steps, C, LANES), BF),
        V((fine.steps, 8, LANES), F32), V((mid.steps, 8, LANES), F32), V((coarse.steps, 8, LANES), F32),
        V((2 * NM, nf), BF),
        V((1, 80, 128), BF), V((2, 80, 128), BF),
        V((1, C + 8, 128), F32), V((2, C + 8, 128), F32),
        V((1, 2 * C + 8, 128), F32), V((2, 2 * C + 8, 128), F32),
        V((1, C, 128), F32), V((2, C, 128), F32),
        V((1, 2 * C, 128), F32), V((2, 2 * C, 128), F32),
        V((1, C, 128), F32), V((2, C, 128), F32),
        V((1, C, 128), F32), V((2, C, 128), F32),
        V((1, C, 128), F32), V((2, C, 128), F32),
        V((R, 2, C, 128), BF), V((coarse.parts, C, 128), BF), V((R, 2, C, 128), BF),
        V((fine.parts, C, 128), F32), V((mid.parts, C, 128), F32), V((coarse.parts, C, 128), F32),
        V((R, 2, C, 128), BF), V((R, 2, NC, 128), BF), V((R, C, 128), BF), V((R, NC, 128), BF),
        V((R - 1, C, 128), BF), V((R - 1, NC, 128), BF), V((C, nf), F32), V((C, nf), F32),
        V((min(ls, 2), A, 2, NG, 16, HALF), BF), V((ls, 2, A, 16, QH), BF), V((ls, 2, A, 16, HALF), BF),
        V((ls, A - 1, 16, HALF), BF), V((ls, 2, 8, HALF), F32), V((ls, 8, HALF), F32),
        V((3, NB, 2, 8, SMW), F32), V((ls, NB, 8, SMW), F32), V((NB - 1, 3, 8, SMW), F32),
        pltpu.SemaphoreType.DMA((n_sems,)),
    ]
    return kernel, scratch


def adamw(master, moment, square, grad, learn_rate):
    moment_new = B_ONE * moment + (1.0 - B_ONE) * grad
    square_new = B_TWO * square + (1.0 - B_TWO) * grad * grad
    fix_one = 1.0 - B_ONE**STEP
    fix_two = 1.0 - B_TWO**STEP
    master_new = master - learn_rate * (
        moment_new / fix_one / (jnp.sqrt(square_new / fix_two) + EPSILON) + WEIGHT_DECAY * master
    )
    return (master_new, moment_new, square_new)


def make_update(KW, NG, per, inside):
    rates = (RATE_FIRST, RATE_MAIN, RATE_MAIN, RATE_MAIN)

    def kernel(*refs):
        far_in, far_out, near_in, near_out, sems = refs[0:14], refs[16:28], refs[30:44], refs[44:56], refs[56]
        out = [pltpu.make_async_copy(refs[14 + k], refs[28 + k], sems.at[26 + k]) for k in range(2)]
        for c in out:
            c.start()
        copies = [pltpu.make_async_copy(a, b, sems.at[k]) for k, (a, b) in enumerate(zip(far_in, near_in))]
        for c in copies:
            c.start()
        for c in copies:
            c.wait()
        gwc, gsmall = near_in[0:2]
        order = column_order(KW, NG, False)

        def update(k, index, grad):
            new = adamw(*(near_in[2 + 4 * m + k][index] for m in range(3)), grad, rates[k])
            for m in range(3):
                near_out[4 * m + k][index] = new[m]

        def done(k):
            for m in range(3):
                c = pltpu.make_async_copy(near_out[4 * m + k], far_out[4 * m + k], sems.at[14 + 4 * m + k])
                c.start()
                out.append(c)

        for l in range(3):
            update(3, l, gwc[l])
        done(3)
        for l in range(3):
            grad = gsmall[l, :, 0:KW]
            update(2, l, join3(dot(split3(grad), order)) if inside else grad)
        done(2)
        for l in range(3):
            parts = split3(gsmall[l, :, KW:])
            parts = [parts[per * k : per * (k + 1)] for k in range(3)]
            for k, picks, rows in ((0, [(0, 0, 3), (3, 5, 3)], 6), (1, [(0, 3, 1), (1, 11, 1)], 2)):
                pick = place(rows, 128, picks)
                update(k, l, sum(dot(pick, part, NT) for part in parts))
        done(0)
        done(1)
        for c in out:
            c.wait()

    return kernel


def per_device(
    T, NG,
    features, cotangent, geom_fine, geom_mid, geom_coarse, links_fine, slots_fine, send_lists, parent_fine,
    parent_mid, links_mid, slots_mid, links_coarse, slots_coarse, kernel_in, kernel_bias, kernel_mid, kernel_out,
    *moments,
):
    C = features.shape[2]
    KW = kernel_mid.shape[2]
    NM, NC = links_mid.shape[1], links_coarse.shape[1]
    halo = send_lists.shape[1] // 2
    nf = features.shape[1]
    fine = Level(0, nf, links_fine.shape[2], nf + 2 * halo)
    mid = Level(1, NM, links_mid.shape[2], geom_mid.shape[1])
    coarse = Level(2, NC, links_coarse.shape[2], geom_coarse.shape[1])
    per = kernel_mid.shape[1]
    inside = per == 8
    everyone = ("tile", "grp")
    half = C * C // 2
    grid = (3, 2, KW // (32 * NG), 2, NG, 16, half)
    small = kernel_mid
    large = kernel_out.reshape(3, per, C, C).transpose(0, 3, 2, 1).reshape(3, 2, half, per).swapaxes(2, 3)
    if not inside:
        zero = jnp.zeros((3, per, 1), F32)
        first = kernel_in.swapaxes(1, 2)
        bias = kernel_bias.swapaxes(1, 2)
        small = jnp.concatenate(
            [kernel_mid, first[..., 0:3], bias[..., 0:1], zero, first[..., 3:6], bias[..., 1:2],
             jnp.zeros((3, per, 119), F32)], axis=2
        )
        small = lax.all_gather(small, everyone, axis=1, tiled=True).reshape(3, KW // 16, 2, 8, KW + 128)
        large = lax.all_gather(large.astype(BF), everyone, axis=2, tiled=True).reshape(grid)

    kernel, scratch = make_kernel(T, NG, C, KW, fine, mid, coarse, halo, inside)
    S = jax.ShapeDtypeStruct
    vm = pl.BlockSpec(memory_space=pltpu.VMEM)
    far = pl.BlockSpec(memory_space=pl.ANY)
    turn = lambda v: v[0].swapaxes(0, 1)
    operands = (
        turn(features), turn(cotangent), turn(geom_fine), turn(geom_mid), turn(geom_coarse),
        turn(links_fine), slots_fine, send_lists, parent_fine, parent_mid, turn(links_mid), slots_mid,
        links_coarse[0], slots_coarse, kernel_in, kernel_bias, small, large,
    )
    layer, gradf, gwc, gsmall = pl.pallas_call(
        kernel,
        out_shape=(S((C, nf), BF), S((C, nf), BF), S((3, 2, 8, half), F32) if inside else S(grid, BF),
                   S((3, 8, KW + 128) if inside else (3, KW // 16, 2, 8, KW + 128), F32)),
        in_specs=[far] * len(operands),
        out_specs=(vm, vm, vm if inside else far, vm),
        scratch_shapes=scratch,
        compiler_params=pltpu.CompilerParams(
            collective_id=0, has_side_effects=True, vmem_limit_bytes=63 << 20
        ),
        name="layer",
    )(*operands)
    if not inside:
        gwc = gwc.astype(F32).reshape(3, 2, KW, half)
        gwc = lax.psum_scatter(gwc, everyone, scatter_dimension=2, tiled=True)
        gsmall = lax.psum_scatter(gsmall.reshape(3, KW, KW + 128), everyone, scatter_dimension=1, tiled=True)
    gwc = gwc.swapaxes(1, 2).reshape(3, per, C, C).swapaxes(2, 3).reshape(3, per, C * C)
    state = (kernel_in, kernel_bias, kernel_mid, kernel_out) + moments
    new = pl.pallas_call(
        make_update(KW, NG, per, inside),
        out_shape=tuple(S(v.shape, F32) for v in state) + (S((C, nf), BF),) * 2,
        in_specs=[far] * 16,
        out_specs=(far,) * 14,
        scratch_shapes=[pltpu.VMEM(v.shape, F32) for v in (gwc, gsmall) + state]
        + [pltpu.VMEM(v.shape, F32) for v in state] + [pltpu.SemaphoreType.DMA((28,))],
        compiler_params=pltpu.CompilerParams(vmem_limit_bytes=63 << 20),
        name="update",
    )(gwc, gsmall, *state, layer, gradf)
    return tuple(v.swapaxes(0, 1)[None] for v in new[12:]) + tuple(new[:12])


def solution(mesh):
    nodes = P("grp", "tile", None)
    rows = P("grp", "tile")
    by_column = P(None, None, ("tile", "grp"))
    by_row = P(None, ("tile", "grp"), None)
    shards = (by_column, by_column, by_row, by_row)
    return jax.shard_map(
        functools.partial(per_device, mesh.shape["tile"], mesh.shape["grp"]),
        mesh=mesh,
        in_specs=(
            nodes, nodes, nodes, P("grp", None, None), P("grp", None, None), nodes, rows, rows, rows,
            P("grp", None), nodes, rows, nodes, rows,
        ) + shards * 3,
        out_specs=(nodes, nodes) + shards * 3,
        check_vma=False,
    )
```

```python
import functools

import jax
import jax.numpy as jnp
from jax import lax
from jax.experimental import pallas as pl
from jax.experimental.pallas import tpu as pltpu
from jax.sharding import PartitionSpec as P

STEP = 5
B_ONE = 0.9
B_TWO = 0.95
EPSILON = 1e-08
WEIGHT_DECAY = 0.1
RATE_FIRST = 0.4
RATE_MAIN = 0.02

BF = jnp.bfloat16
F32 = jnp.float32
I32 = jnp.int32
MESH = pl.DeviceIdType.MESH
NN = ((1,), (0,))
NT = ((1,), (1,))
TN = ((0,), (0,))
GROUP = 8


def dot(a, b, dims=NN):
    return lax.dot_general(a, b, (dims, ((), ())), preferred_element_type=F32)


def sig(v):
    return 0.5 + 0.5 * jnp.tanh(0.5 * v)


def split3(v):
    high = v.astype(BF)
    rest = v - high.astype(F32)
    mid = rest.astype(BF)
    low = (rest - mid.astype(F32)).astype(BF)
    return jnp.concatenate([high, mid, low], axis=0)


def join3(v):
    n = v.shape[0] // 3
    return v[:n] + v[n : 2 * n] + v[2 * n :]


def iota(shape, dim):
    return lax.broadcasted_iota(I32, shape, dim)


def log2(n):
    assert n & (n - 1) == 0
    return n.bit_length() - 1


def group_mask(width):
    return (iota((GROUP, width), 1) >> log2(width // GROUP) == iota((GROUP, width), 0)).astype(F32)


def one_hot(row, start, rows):
    return (iota((rows, row.shape[1]), 0) + start == row).astype(F32).astype(BF)


def spread(x, mask):
    return (x[:, None, :] * mask[None]).reshape(x.shape[0] * GROUP, mask.shape[1]).astype(BF)


def place(rows, columns, pairs):
    r, c = iota((rows, columns), 0), iota((rows, columns), 1)
    hit = jnp.zeros((rows, columns), F32)
    for row, column, count in pairs:
        hit = hit + jnp.where((r - row == c - column) & (r >= row) & (r < row + count), 1.0, 0.0)
    return hit.astype(BF)


def column_order(KW, NG, natural_rows):
    p = iota((KW, KW), 1 if natural_rows else 0)
    n = iota((KW, KW), 0 if natural_rows else 1)
    shift = log2(NG)
    inner, core, grp, chip = p & 7, (p >> 3) & 1, (p >> 4) & (NG - 1), p >> (4 + shift)
    return ((((((chip << 1) + core) << shift) + grp) << 3) + inner == n).astype(F32).astype(BF)


class Level:
    def __init__(self, index, nodes, slots, sources, lanes):
        self.lanes = lanes
        self.index, self.nodes, self.slots, self.sources = index, nodes, slots, sources
        self.steps = nodes * slots // lanes
        self.width = GROUP * slots
        self.blocks = lanes // self.width
        self.parts = sources // 128


def make_kernel(T, NG, C, KW, fine, mid, coarse, halo, inside):
    H = T // 4
    NCH = T // 2 * NG
    A = KW // (32 * NG)
    NB = KW // 16
    R = T // 2
    HALF = C * C // 2
    QH = HALF // 2
    SMW = KW + 128
    BW = HALF + KW
    levels = (fine, mid, coarse)
    NM, NC = mid.nodes, coarse.nodes

    def kernel(
        feat_h, cot_h, geof_h, geom_h, geoc_h, lkf_h, slf_h, send_h, parf_h, parm_h, lkm_h, slm_h, lkc_h, slc_h,
        kin_h, kb_h, kmid_h, kout_h,
        layer, gradf, gwc, gsmall,
        feat, cot, geof, geom, geoc, lkf, slf, send, parf, parm, lkm, slm, lkc, slc, kin, kb, kmid, ownw,
        geom_own, lkc_wide, slc_wide, pk0, pk1, pk2, gm, gc,
        extT, agbuf, gbuf, s0buf, s0x, smx, smfull, waT, wbT, wbr, bbc,
        mt0, mt1, mt2, qt1, qt2, as0, as1, as2, xs0, xs1, xs2, zs0, zs1, zs2,
        ohp, tx_s, rx_s, tx_w, rx_w, tx_q, rx_q, tx_u, rx_u, tx_g, rx_g, tx_f, rx_f,
        x1b, x2T, x2b, acc0, acc1, acc2, acc2b, rs1a, rs2a, rs1buf, rs2buf, v0s, gys,
        rsr0, rsr1, rsr2, rsr3, rsf, gsb, gp, rcA, rcB, sems,
    ):
        smbuf, rsr4, acc1b, tx_b, rx_b, tx_h, rx_h = gsb.at[0], s0buf, x1b, tx_u, rx_u, tx_u, rx_u
        t = lax.axis_index("tile")
        g = lax.axis_index("grp")
        core = lax.rem(t, 2)
        r = t // 2
        lo = lax.rem(r, 2)
        hi = r // 2
        ch = r * NG + g
        ocore, olo, og = 1 - core, 1 - lo, 1 - g

        def tile_of(hi_, lo_, core_):
            return (hi_ * 2 + lo_) * 2 + core_

        partner = {"tile": tile_of(hi, lo, ocore), "grp": g}
        xn = {"tile": tile_of(hi, olo, core), "grp": g}
        yn = {"tile": t, "grp": og}

        nil = t - t

        levels_at = [nil + k for k in range(3)]

        def ix(k):
            return levels_at[k]

        counter = [0]
        open_recv, open_send, out_copies = [], [], []

        def sem_block(n):
            base = counter[0]
            counter[0] += n
            return base

        def copy(src, dst, ssem, rsem, dev):
            return pltpu.make_async_remote_copy(
                src_ref=src, dst_ref=dst, send_sem=sems.at[nil + ssem], recv_sem=sems.at[nil + rsem],
                device_id=dev, device_id_type=MESH,
            )

        local = sem_block(1)

        def own_copy(src, dst):
            c = pltpu.make_async_copy(src, dst, sems.at[local])
            c.start()
            c.wait()

        class One:
            def __init__(self, src, dst, dev):
                self.s, self.r = sem_block(1), sem_block(1)
                self.parts = (src, dst, self.s, self.r, dev)

            def start(self):
                copy(*self.parts).start()
                open_recv.append(self)
                open_send.append(self)

            def recv(self):
                open_recv.remove(self)
                copy(*self.parts).wait_recv()

            def sent(self):
                open_send.remove(self)
                copy(*self.parts).wait_send()

        class Ring:
            def __init__(self, n, src, dst, dev):
                self.n, self.src, self.dst, self.dev = n, src, dst, dev
                self.s, self.r = sem_block(n - 1), sem_block(n - 1)

            def each(self, f):
                def body(i, _):
                    d = i + 1
                    f(copy(self.src(d), self.dst(d), self.s + i, self.r + i, self.dev(d)))
                    return 0

                lax.fori_loop(0, self.n - 1, body, 0)

            def start(self):
                self.each(lambda c: c.start())
                open_recv.append(self)
                open_send.append(self)

            def recv(self):
                open_recv.remove(self)
                self.each(lambda c: c.wait_recv())

            def sent(self):
                open_send.remove(self)
                self.each(lambda c: c.wait_send())

        class Sides:
            def __init__(self, src_left, src_right, rx):
                self.ls, self.lr, self.rs, self.rr = (sem_block(1) for _ in range(4))
                self.rx = rx
                self.src_left, self.src_right = src_left, src_right

            @property
            def to_left(self):
                return copy(self.src_left, self.rx.at[1], self.ls, self.lr, {"tile": t - 1, "grp": g})

            @property
            def to_right(self):
                return copy(self.src_right, self.rx.at[0], self.rs, self.rr, {"tile": t + 1, "grp": g})

            def start(self):
                open_recv.append(self)
                open_send.append(self)

                @pl.when(t > 0)
                def _():
                    self.to_left.start()

                @pl.when(t < T - 1)
                def _():
                    self.to_right.start()

                @pl.when(t == 0)
                def _():
                    self.rx[0] = jnp.zeros(self.rx.shape[1:], self.rx.dtype)

                @pl.when(t == T - 1)
                def _():
                    self.rx[1] = jnp.zeros(self.rx.shape[1:], self.rx.dtype)

            def recv(self):
                open_recv.remove(self)

                @pl.when(t < T - 1)
                def _():
                    self.to_left.wait_recv()

                @pl.when(t > 0)
                def _():
                    self.to_right.wait_recv()

            def sent(self):
                open_send.remove(self)

                @pl.when(t > 0)
                def _():
                    self.to_left.wait_send()

                @pl.when(t < T - 1)
                def _():
                    self.to_right.wait_send()

        def started(c):
            c.start()
            return c

        def finish():
            loaded(*loads)
            for c in tuple(open_recv):
                c.recv()
            for c in tuple(open_send):
                c.sent()
            for src, dst, k in out_copies:
                pltpu.make_async_copy(src, dst, sems.at[nil + k]).wait()

        barrier = pltpu.get_barrier_semaphore()

        def chip_dev(d):
            o = lax.rem(ch + d, NCH)
            return {"tile": (o // NG) * 2 + core, "grp": lax.rem(o, NG)}

        def greet(dev):
            pl.semaphore_signal(barrier, inc=1, device_id=dev, device_id_type=MESH)

        def greet_chip(i, _):
            greet(chip_dev(i + 1))
            return 0

        lax.fori_loop(0, NCH - 1, greet_chip, 0)
        greet(partner)
        beside = t - 1 + 2 * core
        has_beside = (beside >= 0) & (beside < T)

        @pl.when(has_beside)
        def _():
            greet({"tile": beside, "grp": g})

        loads = {}

        def load(name, src, dst):
            c = pltpu.make_async_copy(src, dst, sems.at[sem_block(1)])
            c.start()
            loads[name] = c

        def loaded(*names):
            for name in names:
                loads.pop(name).wait()

        if inside:
            load("kmid", kmid_h, kmid)
            load("kin", kin_h, kin)
            load("kb", kb_h, kb)
        load("feat", feat_h, feat)
        load("geof", geof_h, geof)
        load("send", send_h, send)
        if inside:
            for l in range(3):
                load(l, kout_h.at[l, core], ownw.at[l])
        own_lanes = pl.ds(pl.multiple_of(t * NM, NM), NM)
        for name, src, dst in (
            ("lkf", lkf_h, lkf), ("slf", slf_h, slf), ("lkm", lkm_h, lkm), ("slm", slm_h, slm),
            ("own", geom_h.at[:, own_lanes], geom_own), ("lkc", lkc_h, lkc), ("slc", slc_h, slc), ("geom", geom_h, geom),
            ("geoc", geoc_h, geoc), ("parf", parf_h, parf), ("parm", parm_h, parm), ("cot", cot_h, cot),
        ):
            load(name, src, dst)

        if inside:
            loaded("kmid", "kin", "kb")
            order = column_order(KW, NG, True)
            for l in range(3):
                second = dot(kmid[l].astype(BF), order)
                first = dot(kin[l].astype(BF), place(6, 128, [(0, 0, 3), (3, 5, 3)]), TN)
                first = first + dot(kb[l].astype(BF), place(2, 128, [(0, 3, 1), (1, 8, 1)]), TN)
                if l == 0:
                    smbuf[ch, core] = jnp.concatenate([second, first], axis=1)
                else:
                    smx[l - 1, 0] = second
                    smx[l - 1, 1] = jnp.concatenate([first, jnp.zeros((8, KW - 128), F32)], axis=1)
        pl.semaphore_wait(barrier, NCH + has_beside.astype(I32))
        if inside:
            sm_a0 = started(Ring(NCH, lambda d: smbuf.at[ch, core], lambda d: smbuf.at[ch, core], chip_dev))
            s0c = [[started(One(kout_h.at[l, ocore], s0buf.at[l], partner))] for l in range(3)]
            for l in range(2):
                s0c[l].append(started(One(smx.at[l, ocore], s0x.at[l], partner)))
        loaded("feat", "geof", "send")
        n0 = fine.nodes
        extT[:, 0:n0] = (
            dot(place(80, C, [(0, 0, C)]), feat[...]) + dot(place(80, 3, [(C + 5, 0, 3)]), geof[...])
        ).astype(BF)
        tx_s[0] = dot(extT[:, 0:n0], one_hot(send[...], 0, n0)).astype(BF)
        halo_x = started(Sides(tx_s.at[0], tx_s.at[0], rx_s))

        def window(index, start, n, at):
            off = index - start
            return jnp.where(off < 0, off + at + 8, jnp.where(off >= n, off - n + at + 8, off))

        if not inside:
            own_copy(kmid_h, smfull)
            own_copy(kout_h, agbuf)

        ag = [[] for _ in range(3)]
        wide = (BW, BW, HALF)

        def ag_s1(l):
            if not inside:
                return
            for c in s0c[l]:
                c.recv()
            mine, theirs = ownw[l], s0buf[l]
            if l < 2:
                mine = jnp.concatenate([mine, smx[l, core]], axis=1)
                theirs = jnp.concatenate([theirs, s0x[l]], axis=1)
            first = core == 0
            agbuf[l, core, hi, lo, g, :, 0 : wide[l]] = jnp.concatenate(
                [jnp.where(first, mine, theirs), jnp.where(first, theirs, mine)], axis=0
            ).astype(BF)

            def part(d):
                return agbuf.at[ix(l), core, hi, lo, g, :, 0 : wide[l]]

            c = Ring(H, part, part, lambda d: {"tile": tile_of(lax.rem(hi + d, H), lo, core), "grp": g})
            c.start()
            ag[l].append([c])

        def ag_next(l, *copies):
            if not inside:
                return
            for c in ag[l][-1]:
                c.recv()
            for c in copies:
                c.start()
            ag[l].append(copies)

        def ag_s2(l):
            part = agbuf.at[ix(l), core, :, lo, g, :, 0 : wide[l]]
            ag_next(l, One(part, part, xn), One(part, part, yn))

        def ag_s3(l):
            a = agbuf.at[ix(l), core, :, olo, g, :, 0:QH]
            b = agbuf.at[ix(l), core, :, lo, og, :, QH : wide[l]]
            ag_next(l, One(a, a, yn), One(b, b, xn))

        def ag_s4(l):
            part = agbuf.at[ix(l), core, :, :, :, :, 0 : wide[l]]
            ag_next(l, One(part, part, partner))

        def ag_fin(l):
            if inside:
                for c in ag[l][-1]:
                    c.recv()
                for cs in ag[l]:
                    for c in cs:
                        c.sent()
        def unpack_small(l):
            if not inside:
                block = smfull[l].reshape(KW, SMW)
                second, first = block[:, 0:KW], block[:, KW:]
            elif l == 0:
                block = smbuf[...].reshape(KW, SMW)
                second, first = block[:, 0:KW], block[:, KW:]
            else:
                second = agbuf[l - 1, 0, :, :, :, :, HALF:BW].reshape(KW, KW).astype(F32)
                first = agbuf[l - 1, 1, :, :, :, :, HALF : HALF + 128].reshape(KW, 128).astype(F32)
            wbr[l] = second.astype(BF)
            wbT[l] = second.T.astype(BF)
            waT[l] = first[:, 0:8].astype(BF)
            bbc[:, l : l + 1] = first[:, 8:9]

        mts, qts = (mt0, mt1, mt2), (mt0, qt1, qt2)
        xss, zss, pks, a2s = (xs0, xs1, xs2), (zs0, zs1, zs2), (pk0, pk1, pk2), (as0, as1, as2)

        def pack_nodes(lv, links, used, geometry):
            k, n = links.shape
            links = jnp.where(iota((k, n), 0) < used, links, -1).astype(F32)
            high = links.astype(BF).astype(F32)
            rows = dot(place(8, 3, [(0, 0, 3)]), geometry) + jnp.where(iota((8, n), 0) == 3, 1.0, 0.0)
            pad = jnp.zeros((128 - 2 * k - 8, n), F32)
            pks[lv.index][...] = jnp.concatenate([high, links - high, rows, pad], axis=0).T.astype(BF)

        def edge_columns(lv, i):
            k = lv.slots
            n = lv.lanes // k
            at = pl.ds(pl.multiple_of(i * n, n), n)
            nodes = (iota((n, lv.lanes), 1) >> log2(k) == iota((n, lv.lanes), 0)).astype(F32).astype(BF)
            got = dot(pks[lv.index][at, :], nodes, TN)
            slot = iota((k, lv.lanes), 1) & (k - 1) == iota((k, lv.lanes), 0)
            links = jnp.sum(jnp.where(slot, got[0:k] + got[k : 2 * k], 0.0), axis=0, keepdims=True)
            return links, got[2 * k : 2 * k + 8]

        def take(table, row, lv, rows):
            top, hot = row >> 7, one_hot(row & 127, 0, 128)
            n = min(lv.parts, 16)

            def some(first):
                got = dot(table(first, n), hot)
                acc = jnp.zeros((rows, lv.lanes), F32)
                for h in range(n):
                    acc = acc + jnp.where(top == first + h, got[rows * h : rows * (h + 1)], 0.0)
                return acc

            if n == lv.parts:
                return some(0)
            return lax.fori_loop(0, lv.parts // n, lambda k, acc: acc + some(k * n), jnp.zeros((rows, lv.lanes), F32))

        def put(acc, values, row, lv):
            top, hot = row >> 7, one_hot(row & 127, 0, 128)
            n = min(lv.parts, 16)

            def some(first):
                each = [values * jnp.where(top == first + h, 1.0, 0.0).astype(BF) for h in range(n)]
                acc[pl.ds(first, n)] += dot(jnp.concatenate(each, axis=0), hot, NT).reshape(n, C, 128)

            if n == lv.parts:
                some(0)
                return

            def body(k, _):
                some(k * n)
                return 0

            lax.fori_loop(0, lv.parts // n, body, 0)

        def at_step(i, events):
            for when, call in events:

                @pl.when(i == when)
                def _():
                    call()

        def edge_geometry(lv, x_table, g_table, events=()):
            l = lv.index

            def body(i, _):
                at_step(i, events)
                links, z = edge_columns(lv, i)
                row = links.astype(I32)
                if g_table is None:
                    got = dot(x_table[...], one_hot(row, 0, lv.sources))
                    xss[l][i] = got[0:C].astype(BF)
                    z = z + got[C : C + 8]
                else:
                    z = z + take(g_table, row, lv, 8)
                zss[l][i] = jnp.where(iota((8, lv.lanes), 0) == 4, links, z)
                return 0

            lax.fori_loop(0, lv.steps, body, 0)

        def hidden(l, z):
            t1 = dot(waT[l], z.astype(BF))
            a1 = (t1 * sig(t1)).astype(BF)
            t2 = dot(wbT[l], a1) + bbc[:, l : l + 1]
            return (t2 * sig(t2)).astype(BF)

        def edge_hidden(lv):
            l = lv.index

            def body(i, _):
                a2s[l][i] = hidden(l, zss[l][i])
                return 0

            lax.fori_loop(0, lv.steps, body, 0)

        def edges_forward(lv, x_table, events=()):
            l = lv.index
            mask = group_mask(lv.width)

            def body(i, _):
                at_step(i, events)
                if x_table is None:
                    x = xss[l][i].astype(F32)
                    a2 = hidden(l, zss[l][i])
                    a2s[l][i] = a2
                else:
                    x = take(x_table, zss[l][i, 4:5, :].astype(I32), lv, C)
                    xss[l][i] = x.astype(BF)
                    a2 = a2s[l][i]
                for k in range(lv.blocks):
                    sl = slice(lv.width * k, lv.width * (k + 1))
                    m = dot(spread(x[:, sl], mask), a2[:, sl], NT)
                    mts[l][:, lv.blocks * i + k] = m.astype(BF).reshape(C // 2, 2 * GROUP, KW)
                return 0

            lax.fori_loop(0, lv.steps, body, 0)

        def third(l, pair):
            per_half = C // 4
            half, k = pair // per_half, lax.rem(pair, per_half)
            return agbuf[l, half, :, :, :, :, pl.ds(pl.multiple_of(k * 128, 128), 128)].reshape(KW, 2 * C)

        def node_sums(lv):
            l, n = lv.index, lv.nodes
            each = 8

            def body(i, acc):
                w = jnp.concatenate([third(l, each * i + u) for u in range(each)], axis=0)
                m = jnp.concatenate([mts[l][each * i + u].reshape(2 * n, KW) for u in range(each)], axis=1)
                return acc + dot(m, w)

            acc = lax.fori_loop(0, C // 2 // each, body, jnp.zeros((2 * n, 2 * C), F32))
            acc = acc.reshape(n // GROUP, 2, GROUP, 2 * C)
            both = acc[:, 0].reshape(n, 2 * C) + pltpu.roll(acc[:, 1].reshape(n, 2 * C), C, 1)
            return both.T[0:C]

        def by_parity(lv, gsT):
            n = lv.nodes
            gsT = gsT.astype(F32)
            even = jnp.concatenate([gsT, jnp.zeros(gsT.shape, F32)], axis=0).T[0:n]
            odd = pltpu.roll(even, C, 1)
            shape = (n // GROUP, 1, GROUP, 2 * C)
            return jnp.concatenate([even.reshape(shape), odd.reshape(shape)], axis=1).reshape(2 * n, 2 * C)

        def stage(l):
            return agbuf.at[ix(l), :, :, :, :, :, 0:HALF] if l else gbuf

        def third_grad(lv, gs):
            l = lv.index
            n = C // 4
            each = 8
            turned = gs.T.astype(BF)

            def body(j, _):
                for u in range(each):
                    i = each * j + u
                    both = dot(turned, mts[l][i].reshape(2 * lv.nodes, KW))
                    out = both.T.astype(BF).reshape(A, 2, NG, 16, 128)
                    stage(l)[i // n, :, :, :, :, pl.ds(pl.multiple_of(lax.rem(i, n) * 128, 128), 128)] = out
                return 0

            lax.fori_loop(0, C // 2 // each, body, 0)

        def node_weights(lv, gs):
            l = lv.index
            each = 8
            gs = gs.astype(BF)

            def body(j, _):
                for u in range(each):
                    i = each * j + u
                    q = dot(gs, third(l, i), NT)
                    qts[l][i] = q.astype(BF).reshape(lv.nodes // GROUP, 2 * GROUP, KW)
                return 0

            lax.fori_loop(0, C // 2 // each, body, 0)

        def source_grads(lv, acc, events=()):
            l = lv.index
            mask = group_mask(lv.width)
            fold = (iota((C, C * GROUP), 1) >> log2(GROUP) == iota((C, C * GROUP), 0)).astype(F32).astype(BF)

            def body(i, _):
                at_step(i, events)
                gxs = []
                for k in range(lv.blocks):
                    sl = slice(lv.width * k, lv.width * (k + 1))
                    q = qts[l][:, lv.blocks * i + k].reshape(C * GROUP, KW)
                    every = dot(q, a2s[l][i, :, sl])
                    own = (every.reshape(C, GROUP, lv.width) * mask[None]).reshape(C * GROUP, lv.width).astype(BF)
                    gxs.append(own)
                gx = dot(fold, jnp.concatenate(gxs, axis=1)).astype(BF)
                put(acc, gx, zss[l][i, 4:5, :].astype(I32), lv)
                return 0

            lax.fori_loop(0, lv.steps, body, 0)

        def weight_grads(lv, first, last, events=()):
            l = lv.index
            mask = group_mask(lv.width)

            def body(i, _):
                at_step(i, events)
                zb = zss[l][i].astype(BF)
                t1 = dot(waT[l], zb)
                s1 = sig(t1)
                f1 = t1 * s1
                d1 = s1 + f1 * (1.0 - s1)
                a1 = f1.astype(BF)
                t2 = dot(wbT[l], a1) + bbc[:, l : l + 1]
                s2 = sig(t2)
                d2 = s2 + t2 * s2 * (1.0 - s2)
                x = xss[l][i].astype(F32)
                g2s = []
                for k in range(lv.blocks):
                    sl = slice(lv.width * k, lv.width * (k + 1))
                    q = qts[l][:, lv.blocks * i + k].reshape(C * GROUP, KW)
                    g2s.append((dot(q, spread(x[:, sl], mask), TN) * d2[:, sl]).astype(BF))
                g2 = jnp.concatenate(g2s, axis=1)
                g1 = (dot(wbr[l], g2) * d1).astype(BF)
                zz = jnp.concatenate([zb, zb], axis=0)
                both = dot(jnp.concatenate([a1, zz], axis=0), g2, NT)
                gsb[l, :, :, :, 0:KW] += both[0:KW].reshape(NB, 2, 8, KW)
                gp[l, 0] += dot(zz, g1, NT)[0:8]
                gp[l, 1] += both[KW : KW + 8]
                return 0

            lax.fori_loop(first, last, body, 0)

        def roll_pick(left, right, n_left, left_lane, right_lane):
            lane = iota((1, 128), 1)
            a = pltpu.roll(left, (left_lane - (n_left - 8)) % 128, 1)
            b = pltpu.roll(right, right_lane % 128, 1)
            return jnp.where((lane >= left_lane) & (lane < left_lane + 8), a, 0.0) + jnp.where(
                (lane >= right_lane) & (lane < right_lane + 8), b, 0.0
            )

        def margin_pick(from_left, from_right, n_own, left_at, right_at):
            lane = iota((1, 128), 1)
            a = pltpu.roll(from_left, (0 - right_at) % 128, 1)
            b = pltpu.roll(from_right, (n_own - 8 - left_at) % 128, 1)
            return jnp.where(lane < 8, a, 0.0) + jnp.where((lane >= n_own - 8) & (lane < n_own), b, 0.0)

        if inside:
            loaded(0, 1, 2)
        ag_s1(0)
        loaded("lkf", "slf", "parf")
        pack_nodes(fine, lkf[...], slf[...], geof[...])
        ohp[...] = one_hot(window(parf[...], t * NM, NM, NM), 0, 2 * NM)
        halo_x.recv()
        near, far = (pltpu.roll(rx_s[k].astype(F32), halo, 1) for k in (0, 1))
        extT[:, n0:] = jnp.where(iota((1, 128), 1) < halo, near, far).astype(BF)
        small_b = []

        def a0_next():
            if inside:
                sm_a0.recv()
                small_b.append(started(One(smbuf.at[:, core], smbuf.at[:, core], partner)))

        edge_geometry(fine, extT, None, [(2, lambda: ag_s2(0)), (2, lambda: ag_s1(1)), (4, a0_next)])
        if inside:
            sm_b0 = small_b[0]
            sm_b0.recv()
        unpack_small(0)
        edges_forward(
            fine, None,
            [(3, lambda: ag_s3(0)), (3, lambda: ag_s1(2)), (6, lambda: ag_s4(0)), (6, lambda: ag_s2(1))],
        )
        loaded("lkm", "slm", "own", "lkc", "slc", "geom", "geoc", "parm", "cot")
        pack_nodes(mid, lkm[...], slm[...], geom_own[...])
        lkc_wide[...] = jnp.zeros(lkc_wide.shape, F32)
        lkc_wide[0:NC] = lkc[...].astype(F32)
        slc_wide[...] = jnp.ones(slc_wide.shape, I32)
        slc_wide[:, 0:NC] = slc[...]
        eye = place(coarse.slots, coarse.slots, [(0, 0, coarse.slots)])
        high = lkc_wide[...].astype(BF)
        low = (lkc_wide[...] - high.astype(F32)).astype(BF)
        turned = (dot(eye, high, NT) + dot(eye, low, NT)).astype(I32)
        lanes = iota((1, 128), 1)
        own_c = jnp.where(lanes < NC, t * NC + lanes, -1)
        geo = dot(geoc[...], one_hot(own_c, 0, coarse.sources)).astype(BF)
        pack_nodes(coarse, turned, jnp.where(lanes < NC, slc_wide[...], 0), geo)
        to_rows = place(8, 3, [(5, 0, 3)])
        for table, source, lv in ((gm, geom, mid), (gc, geoc, coarse)):
            rows = dot(to_rows, source[...])
            for k in range(lv.parts):
                table[k] = rows[:, 128 * k : 128 * (k + 1)]
        nf, nm, nc = (v[...].astype(F32) for v in (slf, slm, slc_wide))
        blocks = [parm[:, pl.ds(pl.multiple_of(b * NM, NM), NM)].astype(F32)
                  for b in (jnp.maximum(t - 1, 0), t, jnp.minimum(t + 1, T - 1))]
        before, after = (pltpu.roll(jnp.broadcast_to(v, (8, NM)), 8, 1)[0:1] for v in (blocks[0], blocks[2]))
        sides = jnp.where((lanes < 8) & (t > 0), before, jnp.where((lanes >= 8) & (lanes < 16) & (t < T - 1), after, -1.0))
        around = jnp.concatenate([blocks[1], sides], axis=1).astype(I32)
        pw = jnp.where(around < 0, -1, window(around, t * NC, NC, NC))
        g_rows = lambda table: lambda first, n: table[pl.ds(first, n)].reshape(n * 8, 128).astype(BF)
        edge_geometry(mid, None, g_rows(gm))
        edge_geometry(coarse, None, g_rows(gc))
        ag_fin(0)
        v0 = extT[0:C, 0 : fine.nodes].astype(F32) + node_sums(fine) / nf
        v0s[...] = v0

        ones8 = jnp.ones((8, fine.nodes), BF)
        part = dot(jnp.concatenate([split3(v0), ones8], axis=0), ohp[...], NT)
        sums = jnp.concatenate([join3(part[0 : 3 * C]), part[3 * C :]], axis=0)
        tx_w[0] = sums[:, NM:]
        ex_w = started(Sides(tx_w.at[0], tx_w.at[0], rx_w))
        unpack_small(1)
        ag_s3(1)
        ex_w.recv()
        own = sums[:, 0:NM] + margin_pick(rx_w[0], rx_w[1], NM, 0, 8)
        inv1 = 1.0 / jnp.maximum(own[C : C + 1], 1.0)
        v1 = own[0:C] / jnp.maximum(own[C : C + 1], 1.0)
        x1b[r, core] = v1.astype(BF)

        def chip_ring(src, dst):
            return Ring(R, src, dst, lambda d: {"tile": lax.rem(r + d, R) * 2 + core, "grp": g})

        ag1 = started(chip_ring(lambda d: x1b.at[r, core], lambda d: x1b.at[r, core]))
        ag_s2(2)
        edge_hidden(mid)
        ag_s4(1)
        ag1.recv()
        ag1p = started(One(x1b.at[:, core], x1b.at[:, core], partner))
        ag1p.recv()

        def x1_rows(first, n):
            return x1b[pl.ds(first // 2, n // 2)].reshape(n * C, 128)

        edges_forward(mid, x1_rows, [(2, lambda: ag_s3(2))])
        ag_fin(1)
        unpack_small(2)
        w1 = v1 + node_sums(mid) / nm
        tx_q[0, 0:C] = w1
        ohq = one_hot(pw, 0, 128)
        part = dot(jnp.concatenate([split3(w1), jnp.ones((8, NM), BF)], axis=0), ohq[:, 0:NM], NT)
        tx_q[0, C : 2 * C + 8] = jnp.concatenate([join3(part[0 : 3 * C]), part[3 * C :]], axis=0)
        ex_q = started(Sides(tx_q.at[0], tx_q.at[0], rx_q))
        edge_hidden(coarse)
        ag_s4(2)
        ex_q.recv()
        own = tx_q[0, C : 2 * C + 8] + margin_pick(rx_q[0, C : 2 * C + 8], rx_q[1, C : 2 * C + 8], NC, NC, NC + 8)
        w1m = roll_pick(rx_q[0, 0:C], rx_q[1, 0:C], NM, 0, 8)
        w1win = jnp.concatenate([w1, w1m], axis=1)
        lane = iota((1, 128), 1)
        mine = lane < NC
        cnt2 = jnp.maximum(own[C : C + 1], 1.0)
        v2 = jnp.where(mine, own[0:C] / cnt2, 0.0)

        x2b[r, core] = v2.astype(BF)
        ag2 = started(chip_ring(lambda d: x2b.at[r, core], lambda d: x2b.at[r, core]))
        ag2.recv()
        ag2p = started(One(x2b.at[:, core], x2b.at[:, core], partner))
        ag2p.recv()
        per = 128 // NC
        cols = []
        for k in range(coarse.sources // 128):
            block = x2b[per * k // 2, 0].astype(F32)
            for u in range(1, per):
                block = block + pltpu.roll(x2b[(per * k + u) // 2, (per * k + u) % 2].astype(F32), NC * u, 1)
            cols.append(block.astype(BF))
        for k, block in enumerate(cols):
            x2T[k] = block
        edges_forward(coarse, lambda first, n: x2T[pl.ds(first, n)].reshape(n * C, 128))
        ag_fin(2)
        sc = node_sums(coarse)
        sc = jnp.concatenate([sc, jnp.zeros((C, 128 - NC), F32)], axis=1)
        w2 = v2 + jnp.where(mine, sc / nc, 0.0)
        tx_u[0] = w2
        ex_u = started(Sides(tx_u.at[0], tx_u.at[0], rx_u))
        ex_u.recv()
        w2win = w2 + roll_pick(rx_u[0], rx_u[1], NC, NC, NC + 8)

        y1win = w1win + join3(dot(split3(w2win), ohq))
        y0 = v0s[...] + join3(dot(split3(y1win), ohp[...]))
        s0 = sig(y0)
        f0 = y0 * s0
        layer[...] = f0.astype(BF)
        gy0 = cot[...] * (s0 + f0 * (1.0 - s0))
        gys[...] = gy0
        gy1p = join3(dot(split3(gy0), ohp[...], NT))
        gw2p = join3(dot(split3(gy1p), ohq, NT))
        tx_g[0, 0:C] = gy1p[:, NM:]
        tx_g[0, C : 2 * C] = gw2p
        ex_g = started(Sides(tx_g.at[0], tx_g.at[0], rx_g))
        ex_g.recv()
        gy1 = gy1p[:, 0:NM] + margin_pick(rx_g[0, 0:C], rx_g[1, 0:C], NM, 0, 8)
        gw2 = jnp.where(mine, gw2p + margin_pick(rx_g[0, C:], rx_g[1, C:], NC, NC, NC + 8), 0.0)

        rs = [[] for _ in range(3)]

        def rs_step(l, fix, *copies):
            if not inside:
                return
            if rs[l]:
                for c in rs[l][-1]:
                    c.recv()
            fix()
            for c in copies:
                c.start()
            rs[l].append(copies)

        def landing(l):
            return gbuf.at[ix(2 - l)] if l and inside else rsr0

        def rs_s0(l):
            rs_step(l, lambda: None, One(stage(l).at[ocore], landing(l), partner))

        def rs_s1(l):
            def fix():
                def body(i, _):
                    both = stage(l)[core, i].astype(F32) + landing(l)[i].astype(F32)
                    stage(l)[core, i] = both.astype(BF)
                    return 0

                lax.fori_loop(0, H, body, 0)

            rs_step(
                l, fix,
                One(stage(l).at[core, :, olo, og, :, 0:QH], rsr1.at[ix(l % 2), ix(0)], xn),
                One(stage(l).at[core, :, olo, og, :, QH:HALF], rsr1.at[ix(l % 2), ix(1)], yn),
            )

        def rs_s2(l):
            def fix():
                def body(i, _):
                    a = stage(l)[core, i, lo, og, :, 0:QH].astype(F32) + rsr1[l % 2, 0, i].astype(F32)
                    stage(l)[core, i, lo, og, :, 0:QH] = a.astype(BF)
                    b = stage(l)[core, i, olo, g, :, QH:HALF].astype(F32) + rsr1[l % 2, 1, i].astype(F32)
                    stage(l)[core, i, olo, g, :, QH:HALF] = b.astype(BF)
                    return 0

                lax.fori_loop(0, H, body, 0)

            rs_step(
                l, fix,
                One(stage(l).at[core, :, lo, og], rsr2.at[ix(l % 2), ix(0)], yn),
                One(stage(l).at[core, :, olo, g], rsr2.at[ix(l % 2), ix(1)], xn),
            )

        def rs_s3(l):
            def fix():
                def body(i, _):
                    a = stage(l)[core, i, lo, g].astype(F32) + rsr2[l % 2, 0, i].astype(F32) + rsr2[l % 2, 1, i].astype(F32)
                    stage(l)[core, i, lo, g] = a.astype(BF)
                    return 0

                lax.fori_loop(0, H, body, 0)

            rs_step(
                l, fix,
                Ring(
                    H,
                    lambda d: stage(l).at[core, lax.rem(hi + d, H), lo, g],
                    lambda d: rsr3.at[ix(l % 2), d - 1],
                    lambda d: {"tile": tile_of(lax.rem(hi + d, H), lo, core), "grp": g},
                ),
            )

        def rs_s4(l):
            def fix():
                tot = stage(l)[core, hi, lo, g].astype(F32)
                for k in range(H - 1):
                    tot = tot + rsr3[l % 2, k].astype(F32)
                rsf[l, 0] = tot[0:8]
                rsf[l, 1] = tot[8:16]

            rs_step(l, fix, One(rsf.at[ix(l), ocore], rsr4.at[ix(l)], partner))

        def rs_s5(l):
            if not inside:
                own_copy(stage(l), gwc.at[l])
                return
            for c in rs[l][-1]:
                c.recv()
            for src, dst in ((rsf.at[ix(l), core], gwc.at[ix(l), core]), (rsr4.at[ix(l)], gwc.at[ix(l), ocore])):
                out_copies.append((src, dst, sem_block(1)))
                pltpu.make_async_copy(src, dst, sems.at[nil + out_copies[-1][2]]).start()

        if inside:
            sm_a0.sent()
            sm_b0.sent()
        gsb[...] = jnp.zeros(gsb.shape, F32)
        gp[...] = jnp.zeros(gp.shape, F32)
        gs_copies = {}

        def gs_start(a, b):
            for l in range(a, b):
                tall = jnp.concatenate([gp[l, 0], gp[l, 1], jnp.zeros((112, KW), F32)], axis=0)
                gsb[l, :, :, :, KW:] = tall.T.reshape(NB, 2, 8, 128)
            if inside:
                gs_copies[a] = started(One(gsb.at[a:b, :, ocore], rcA.at[a:b], partner))

        def gs_ring(a, b):
            if inside:
                gs_copies[a].recv()
                for l in range(a, b):
                    gsb[l, :, core] += rcA[l]
                gs_copies[a] = started(
                    Ring(
                        NCH,
                        lambda d: gsb.at[a:b, lax.rem(ch + d, NCH), core],
                        lambda d: rcB.at[d - 1, a:b],
                        chip_dev,
                    )
                )

        def gs_end(a, b):
            if not inside:
                gsmall[a:b] = gsb[a:b]
                return
            gs_copies[a].recv()

            def add3(k, acc):
                return acc + rcB[k, a:b]

            gsmall[a:b] = lax.fori_loop(0, NCH - 1, add3, gsb[a:b, ch, core])


        gs2T = jnp.where(mine, gw2 / nc, 0.0).astype(BF)
        gs2 = by_parity(coarse, gs2T)
        node_weights(coarse, gs2)
        acc2[...] = jnp.zeros(acc2.shape, F32)
        source_grads(coarse, acc2)
        zero = jnp.zeros((C, 128), F32)
        for k in range(coarse.parts):
            rows = jnp.concatenate([acc2[k], zero], axis=0).T.astype(BF)
            acc2b[per // 2 * k : per // 2 * (k + 1)] = rows.reshape(per // 2, 2, NC, 128)
        r2p = started(One(acc2b.at[:, ocore], rs2a, partner))
        weight_grads(coarse, 0, 1)
        r2p.recv()
        acc2b[:, core] = (acc2b[:, core].astype(F32) + rs2a[...].astype(F32)).astype(BF)
        r2 = started(chip_ring(lambda d: acc2b.at[lax.rem(r + d, R), core], lambda d: rs2buf.at[d - 1]))
        weight_grads(coarse, 1, coarse.steps)
        third_grad(coarse, gs2)
        r2.recv()

        def add2(k, acc):
            return acc + rs2buf[k].astype(F32)

        own2 = lax.fori_loop(0, R - 1, add2, acc2b[r, core].astype(F32))
        own2 = jnp.concatenate([own2, jnp.zeros((128 - NC, 128), F32)], axis=0).T[0:C]
        gv2 = jnp.where(mine, (gw2 + own2) / cnt2, 0.0)
        ex_u.sent()
        tx_b[0] = gv2
        ex_b = started(Sides(tx_b.at[0], tx_b.at[0], rx_b))
        rs_s0(2)
        ex_b.recv()
        gv2win = gv2 + roll_pick(rx_b[0], rx_b[1], NC, NC, NC + 8)
        gw1 = gy1 + join3(dot(split3(gv2win), ohq[:, 0:NM]))

        gs1T = (gw1 / nm).astype(BF)
        gs1 = by_parity(mid, gs1T)
        node_weights(mid, gs1)
        acc1[...] = jnp.zeros(acc1.shape, F32)
        rs_s1(2)
        source_grads(mid, acc1, [(2, lambda: rs_s2(2))])
        ag1.sent()
        ag1p.sent()
        acc1b[...] = acc1[...].astype(BF).reshape(acc1b.shape)
        r1p = started(One(acc1b.at[:, ocore], rs1a, partner))
        half = mid.steps // 2
        third_grad(mid, gs1)
        r1p.recv()
        acc1b[:, core] = (acc1b[:, core].astype(F32) + rs1a[...].astype(F32)).astype(BF)
        r1 = started(chip_ring(lambda d: acc1b.at[lax.rem(r + d, R), core], lambda d: rs1buf.at[d - 1]))
        rs_s0(1)
        weight_grads(mid, 0, half)
        r1.recv()

        def add1(k, acc):
            return acc + rs1buf[k].astype(F32)

        own1 = lax.fori_loop(0, R - 1, add1, acc1b[r, core].astype(F32))
        gv1 = (gw1 + own1) * inv1
        tx_f[0] = gv1
        ex_f = started(Sides(tx_f.at[0], tx_f.at[0], rx_f))
        rs_s1(1)
        rs_s3(2)
        weight_grads(mid, half, mid.steps)
        ex_f.recv()
        gv1win = jnp.concatenate([gv1, roll_pick(rx_f[0], rx_f[1], NM, 0, 8)], axis=1)
        gv0 = gys[...] + join3(dot(split3(gv1win), ohp[...]))
        gys[...] = gv0

        gs0 = gv0 / nf
        gs0T = gs0.astype(BF)
        gs0 = by_parity(fine, gs0T)
        rs_s2(1)
        third_grad(fine, gs0)
        rs_s0(0)
        node_weights(fine, gs0)
        rs_s1(0)
        rs_s4(2)
        rs_s3(1)
        gs_start(1, 3)
        weight_grads(
            fine, 0, fine.steps,
            [(1, lambda: rs_s4(1)), (2, lambda: rs_s5(2)), (3, lambda: rs_s2(0)), (4, lambda: gs_ring(1, 3)),
             (5, lambda: rs_s5(1)), (6, lambda: rs_s3(0))],
        )
        gs_start(0, 1)
        acc0[...] = jnp.zeros(acc0.shape, F32)
        source_grads(
            fine, acc0, [(1, lambda: gs_ring(0, 1)), (3, lambda: gs_end(1, 3)), (6, lambda: rs_s4(0))]
        )
        ex_b.sent()
        tx_h[0] = acc0[fine.parts - 1]
        ex_h = started(Sides(tx_h.at[0], tx_h.at[0], rx_h))
        rs_s5(0)
        gs_end(0, 1)
        ex_h.recv()
        lane1 = iota((1, 128), 1)
        back = jnp.where(lane1 < halo, pltpu.roll(rx_h[0], halo, 1), pltpu.roll(rx_h[1], halo, 1))
        ohs2 = one_hot(send[...], 0, n0)
        own0 = jnp.concatenate([acc0[k] for k in range(fine.parts - 1)], axis=1)
        gf = gys[...] + own0 + join3(dot(split3(back), ohs2, NT))
        gradf[...] = gf.astype(BF)
        finish()

    n_sems = (
        2 * (2 * (NCH - 1)) + 4 + 2 * 3 + 3 * (2 * (H - 1) + 4 + 4 + 2) + 4
        + 4 * 7 + 4 * (2 * (T - 1)) + 4 * NCH + 3 * (2 + 4 + 4 + 2 * (H - 1) + 2) + 2 + 2 * (NCH - 1) + 32
    )
    V = pltpu.VMEM
    ls, la = (3, A) if inside else (1, 1)
    by_group = lambda n: V((C // 2, n // GROUP, 2 * GROUP, KW), BF)
    nf, nm_, nc_ = fine.nodes, NM, NC
    scratch = [
        V((C, nf), BF), V((C, nf), F32), V((3, nf), BF), V((3, mid.sources), BF), V((3, coarse.sources), BF),
        V((fine.slots, nf), I32), V((1, nf), I32), V((1, 2 * halo), I32), V((1, nf), I32), V((1, mid.sources), I32),
        V((mid.slots, nm_), I32), V((1, nm_), I32), V((nc_, coarse.slots), I32), V((1, nc_), I32),
        V((3, 6, 8), F32), V((3, 2, 8), F32), V((3, 8, KW), F32), V((ls, 8, HALF), F32),
        V((3, nm_), BF), V((128, coarse.slots), F32), V((1, 128), I32),
        V((nf, 128), BF), V((nm_, 128), BF), V((128, 128), BF), V((mid.parts, 8, 128), F32), V((coarse.parts, 8, 128), F32),
        V((80, nf + 2 * halo), BF),
        V((3, 2, A, 2, NG, 16, BW if inside else HALF), BF), V((2, A, 2, NG, 16, HALF), BF), V((ls, 8, HALF), F32),
        V((2, 8, KW), F32), V((2, 2, 8, KW), F32),
        V((1 if inside else 3, 1 if inside else NB, 2, 8, SMW), F32), V((3, KW, 8), BF), V((3, KW, KW), BF), V((3, KW, KW), BF), V((KW, 128), F32),
        by_group(nf), by_group(nm_), by_group(nc_), by_group(nm_), by_group(nc_),
        V((fine.steps, KW, fine.lanes), BF), V((mid.steps, KW, fine.lanes), BF), V((coarse.steps, KW, fine.lanes), BF),
        V((fine.steps, C, fine.lanes), BF), V((mid.steps, C, fine.lanes), BF), V((coarse.steps, C, fine.lanes), BF),
        V((fine.steps, 8, fine.lanes), F32), V((mid.steps, 8, fine.lanes), F32), V((coarse.steps, 8, fine.lanes), F32),
        V((2 * NM, nf), BF),
        V((1, 80, 128), BF), V((2, 80, 128), BF),
        V((1, C + 8, 128), F32), V((2, C + 8, 128), F32),
        V((1, 2 * C + 8, 128), F32), V((2, 2 * C + 8, 128), F32),
        V((1, C, 128), F32), V((2, C, 128), F32),
        V((1, 2 * C, 128), F32), V((2, 2 * C, 128), F32),
        V((1, C, 128), F32), V((2, C, 128), F32),
        V((R, 2, C, 128), BF), V((coarse.parts, C, 128), BF), V((R, 2, C, 128), BF),
        V((fine.parts, C, 128), F32), V((mid.parts, C, 128), F32), V((coarse.parts, C, 128), F32),
        V((R, 2, NC, 128), BF), V((R, C, 128), BF), V((R, NC, 128), BF),
        V((R - 1, C, 128), BF), V((R - 1, NC, 128), BF), V((C, nf), F32), V((C, nf), F32),
        V((la, 2, NG, 16, HALF), BF), V((2, 2, la, 16, QH), BF), V((2, 2, la, 16, HALF), BF),
        V((2, A - 1, 16, HALF), BF), V((ls, 2, 8, HALF), F32),
        V((3, NB, 2, 8, SMW), F32), V((3, 2, 8, KW), F32), V((ls, NB, 8, SMW), F32), V((NB - 1, 3, 8, SMW), F32),
        pltpu.SemaphoreType.DMA((n_sems,)),
    ]
    return kernel, scratch


def adamw(master, moment, square, grad, learn_rate):
    moment_new = B_ONE * moment + (1.0 - B_ONE) * grad
    square_new = B_TWO * square + (1.0 - B_TWO) * grad * grad
    fix_one = 1.0 - B_ONE**STEP
    fix_two = 1.0 - B_TWO**STEP
    master_new = master - learn_rate * (
        moment_new / fix_one / (jnp.sqrt(square_new / fix_two) + EPSILON) + WEIGHT_DECAY * master
    )
    return (master_new, moment_new, square_new)


def make_update(KW, NG, per, inside):
    rates = (RATE_FIRST, RATE_MAIN, RATE_MAIN, RATE_MAIN)

    def kernel(*refs):
        far_in, far_out, near_in, near_out, sems = refs[0:14], refs[16:28], refs[30:44], refs[44:56], refs[56]
        passing = refs[57:59]
        first = [pltpu.make_async_copy(refs[14 + k], passing[k], sems.at[26 + k]) for k in range(2)]
        for c in first:
            c.start()
        out = []
        copies = [pltpu.make_async_copy(a, b, sems.at[k]) for k, (a, b) in enumerate(zip(far_in, near_in))]
        for c in copies:
            c.start()
        for k in range(2):
            first[k].wait()
            out.append(pltpu.make_async_copy(passing[k], refs[28 + k], sems.at[28 + k]))
            out[-1].start()
        for c in copies:
            c.wait()
        gwc, gsmall = near_in[0:2]
        order = column_order(KW, NG, False)

        def update(k, index, grad):
            new = adamw(*(near_in[2 + 4 * m + k][index] for m in range(3)), grad, rates[k])
            for m in range(3):
                near_out[4 * m + k][index] = new[m]

        def done(k):
            for m in range(3):
                c = pltpu.make_async_copy(near_out[4 * m + k], far_out[4 * m + k], sems.at[14 + 4 * m + k])
                c.start()
                out.append(c)

        for l in range(3):
            update(3, l, gwc[l])
        done(3)
        for l in range(3):
            grad = gsmall[l, :, 0:KW]
            update(2, l, join3(dot(split3(grad), order)) if inside else grad)
        done(2)
        for l in range(3):
            parts = split3(gsmall[l, :, KW:])
            parts = [parts[per * k : per * (k + 1)] for k in range(3)]
            for k, picks, rows in ((0, [(0, 0, 3), (3, 5, 3)], 6), (1, [(0, 3, 1), (1, 11, 1)], 2)):
                pick = place(rows, 128, picks)
                update(k, l, sum(dot(pick, part, NT) for part in parts))
        done(0)
        done(1)
        for c in out:
            c.wait()

    return kernel


def per_device(
    T, NG,
    features, cotangent, geom_fine, geom_mid, geom_coarse, links_fine, slots_fine, send_lists, parent_fine,
    parent_mid, links_mid, slots_mid, links_coarse, slots_coarse, kernel_in, kernel_bias, kernel_mid, kernel_out,
    *moments,
):
    C = features.shape[2]
    KW = kernel_mid.shape[2]
    NM, NC = links_mid.shape[1], links_coarse.shape[1]
    halo = send_lists.shape[1] // 2
    nf = features.shape[1]
    per = kernel_mid.shape[1]
    inside = per == 8
    lanes = 1024 if inside else 512
    fine = Level(0, nf, links_fine.shape[2], nf + 2 * halo, lanes)
    mid = Level(1, NM, links_mid.shape[2], geom_mid.shape[1], lanes)
    coarse = Level(2, NC, links_coarse.shape[2], geom_coarse.shape[1], lanes)
    everyone = ("tile", "grp")
    half = C * C // 2
    grid = (3, 2, KW // (32 * NG), 2, NG, 16, half)
    small = kernel_mid
    large = kernel_out.reshape(3, per, C, C).transpose(0, 3, 2, 1).reshape(3, 2, half, per).swapaxes(2, 3)
    if not inside:
        zero = jnp.zeros((3, per, 1), F32)
        first = kernel_in.swapaxes(1, 2)
        bias = kernel_bias.swapaxes(1, 2)
        small = jnp.concatenate(
            [kernel_mid, first[..., 0:3], bias[..., 0:1], zero, first[..., 3:6], bias[..., 1:2],
             jnp.zeros((3, per, 119), F32)], axis=2
        )
        small = lax.all_gather(small, everyone, axis=1, tiled=True).reshape(3, KW // 16, 2, 8, KW + 128)
        large = lax.all_gather(large.astype(BF), everyone, axis=2, tiled=True).reshape(grid)

    kernel, scratch = make_kernel(T, NG, C, KW, fine, mid, coarse, halo, inside)
    S = jax.ShapeDtypeStruct
    vm = pl.BlockSpec(memory_space=pltpu.VMEM)
    far = pl.BlockSpec(memory_space=pl.ANY)
    turn = lambda v: v[0].swapaxes(0, 1)
    operands = (
        turn(features), turn(cotangent), turn(geom_fine), turn(geom_mid), turn(geom_coarse),
        turn(links_fine), slots_fine, send_lists, parent_fine, parent_mid, turn(links_mid), slots_mid,
        links_coarse[0], slots_coarse, kernel_in, kernel_bias, small, large,
    )
    layer, gradf, gwc, gsmall = pl.pallas_call(
        kernel,
        out_shape=(S((C, nf), BF), S((C, nf), BF), S((3, 2, 8, half), F32) if inside else S(grid, BF),
                   S((3, 8, KW + 128) if inside else (3, KW // 16, 2, 8, KW + 128), F32)),
        in_specs=[far] * len(operands),
        out_specs=(vm, vm, far, vm),
        scratch_shapes=scratch,
        compiler_params=pltpu.CompilerParams(
            collective_id=0, has_side_effects=True, vmem_limit_bytes=(64 << 20) - (1 << 16)
        ),
        name="layer",
    )(*operands)
    if not inside:
        gwc = gwc.astype(F32).reshape(3, 2, KW, half)
        gwc = lax.psum_scatter(gwc, everyone, scatter_dimension=2, tiled=True)
        gsmall = lax.psum_scatter(gsmall.reshape(3, KW, KW + 128), everyone, scatter_dimension=1, tiled=True)
    gwc = gwc.swapaxes(1, 2).reshape(3, per, C, C).swapaxes(2, 3).reshape(3, per, C * C)
    state = (kernel_in, kernel_bias, kernel_mid, kernel_out) + moments
    new = pl.pallas_call(
        make_update(KW, NG, per, inside),
        out_shape=tuple(S(v.shape, F32) for v in state) + (S((C, nf), BF),) * 2,
        in_specs=[far] * 16,
        out_specs=(far,) * 14,
        scratch_shapes=[pltpu.VMEM(v.shape, F32) for v in (gwc, gsmall) + state]
        + [pltpu.VMEM(v.shape, F32) for v in state] + [pltpu.SemaphoreType.DMA((30,))] + [pltpu.VMEM((C, nf), BF)] * 2,
        compiler_params=pltpu.CompilerParams(vmem_limit_bytes=63 << 20),
        name="update",
    )(gwc, gsmall, *state, layer, gradf)
    return tuple(v.swapaxes(0, 1)[None] for v in new[12:]) + tuple(new[:12])


def solution(mesh):
    nodes = P("grp", "tile", None)
    rows = P("grp", "tile")
    by_column = P(None, None, ("tile", "grp"))
    by_row = P(None, ("tile", "grp"), None)
    shards = (by_column, by_column, by_row, by_row)
    return jax.shard_map(
        functools.partial(per_device, mesh.shape["tile"], mesh.shape["grp"]),
        mesh=mesh,
        in_specs=(
            nodes, nodes, nodes, P("grp", None, None), P("grp", None, None), nodes, rows, rows, rows,
            P("grp", None), nodes, rows, nodes, rows,
        ) + shards * 3,
        out_specs=(nodes, nodes) + shards * 3,
        check_vma=False,
    )
```

```python
import functools

import jax
import jax.numpy as jnp
from jax import lax
from jax.experimental import pallas as pl
from jax.experimental.pallas import tpu as pltpu
from jax.sharding import PartitionSpec as P

STEP = 5
B_ONE = 0.9
B_TWO = 0.95
EPSILON = 1e-08
WEIGHT_DECAY = 0.1
RATE_FIRST = 0.4
RATE_MAIN = 0.02

BF = jnp.bfloat16
F32 = jnp.float32
I32 = jnp.int32
MESH = pl.DeviceIdType.MESH
NN = ((1,), (0,))
NT = ((1,), (1,))
TN = ((0,), (0,))
GROUP = 8


def dot(a, b, dims=NN):
    return lax.dot_general(a, b, (dims, ((), ())), preferred_element_type=F32)


def sig(v):
    return 0.5 + 0.5 * jnp.tanh(0.5 * v)


def split3(v):
    high = v.astype(BF)
    rest = v - high.astype(F32)
    mid = rest.astype(BF)
    low = (rest - mid.astype(F32)).astype(BF)
    return jnp.concatenate([high, mid, low], axis=0)


def join3(v):
    n = v.shape[0] // 3
    return v[:n] + v[n : 2 * n] + v[2 * n :]


def iota(shape, dim):
    return lax.broadcasted_iota(I32, shape, dim)


def log2(n):
    assert n & (n - 1) == 0
    return n.bit_length() - 1


def group_mask(width):
    return (iota((GROUP, width), 1) >> log2(width // GROUP) == iota((GROUP, width), 0)).astype(F32)


def one_hot(row, start, rows):
    return (iota((rows, row.shape[1]), 0) + start == row).astype(F32).astype(BF)


def spread(x, mask):
    return (x[:, None, :] * mask[None]).reshape(x.shape[0] * GROUP, mask.shape[1]).astype(BF)


def place(rows, columns, pairs):
    r, c = iota((rows, columns), 0), iota((rows, columns), 1)
    hit = jnp.zeros((rows, columns), F32)
    for row, column, count in pairs:
        hit = hit + jnp.where((r - row == c - column) & (r >= row) & (r < row + count), 1.0, 0.0)
    return hit.astype(BF)


def column_order(KW, NG, natural_rows):
    p = iota((KW, KW), 1 if natural_rows else 0)
    n = iota((KW, KW), 0 if natural_rows else 1)
    shift = log2(NG)
    inner, core, grp, chip = p & 7, (p >> 3) & 1, (p >> 4) & (NG - 1), p >> (4 + shift)
    return ((((((chip << 1) + core) << shift) + grp) << 3) + inner == n).astype(F32).astype(BF)


class Level:
    def __init__(self, index, nodes, slots, sources, lanes):
        self.lanes = lanes
        self.index, self.nodes, self.slots, self.sources = index, nodes, slots, sources
        self.steps = nodes * slots // lanes
        self.width = GROUP * slots
        self.blocks = lanes // self.width
        self.parts = sources // 128


def make_kernel(T, NG, C, KW, fine, mid, coarse, halo, inside):
    H = T // 4
    NCH = T // 2 * NG
    A = KW // (32 * NG)
    NB = KW // 16
    R = T // 2
    HALF = C * C // 2
    QH = HALF // 2
    SMW = KW + 128
    BW = HALF + KW
    levels = (fine, mid, coarse)
    NM, NC = mid.nodes, coarse.nodes

    def kernel(
        feat_h, cot_h, geof_h, geom_h, geoc_h, lkf_h, slf_h, send_h, parf_h, parm_h, lkm_h, slm_h, lkc_h, slc_h,
        kin_h, kb_h, kmid_h, kout_h,
        layer, gradf, gwc, gsmall,
        feat, cot, geof, geom, geoc, lkf, slf, send, parf, parm, lkm, slm, lkc, slc, kin, kb, kmid, ownw,
        geom_own, lkc_wide, slc_wide, pk0, pk1, pk2, gm, gc,
        extT, agbuf, gbuf, s0buf, s0x, smx, smfull, waT, wbT, wbr, bbc,
        mt0, mt1, mt2, qt1, qt2, as0, as1, as2, xs0, xs1, xs2, zs0, zs1, zs2,
        ohp, tx_s, rx_s, tx_w, rx_w, tx_q, rx_q, tx_u, rx_u, tx_g, rx_g, tx_f, rx_f,
        x1b, x2T, x2b, acc0, acc1, acc2, acc2b, rs1a, rs2a, rs1buf, rs2buf, v0s, gys,
        rsr0, rsr1, rsr2, rsr3, rsf, gsb, gp, rcA, rcB, sems,
    ):
        smbuf, rsr4, acc1b, tx_b, rx_b, tx_h, rx_h = gsb.at[0], s0buf, x1b, tx_u, rx_u, tx_u, rx_u
        t = lax.axis_index("tile")
        g = lax.axis_index("grp")
        core = lax.rem(t, 2)
        r = t // 2
        lo = lax.rem(r, 2)
        hi = r // 2
        ch = r * NG + g
        ocore, olo, og = 1 - core, 1 - lo, 1 - g

        def tile_of(hi_, lo_, core_):
            return (hi_ * 2 + lo_) * 2 + core_

        partner = {"tile": tile_of(hi, lo, ocore), "grp": g}
        xn = {"tile": tile_of(hi, olo, core), "grp": g}
        yn = {"tile": t, "grp": og}

        nil = t - t

        levels_at = [nil + k for k in range(3)]

        def ix(k):
            return levels_at[k]

        counter = [0]
        open_recv, open_send, out_copies = [], [], []

        def sem_block(n):
            base = counter[0]
            counter[0] += n
            return base

        def copy(src, dst, ssem, rsem, dev):
            return pltpu.make_async_remote_copy(
                src_ref=src, dst_ref=dst, send_sem=sems.at[nil + ssem], recv_sem=sems.at[nil + rsem],
                device_id=dev, device_id_type=MESH,
            )

        local = sem_block(1)

        def own_copy(src, dst):
            c = pltpu.make_async_copy(src, dst, sems.at[local])
            c.start()
            c.wait()

        class One:
            def __init__(self, src, dst, dev):
                self.s, self.r = sem_block(1), sem_block(1)
                self.parts = (src, dst, self.s, self.r, dev)

            def start(self):
                copy(*self.parts).start()
                open_recv.append(self)
                open_send.append(self)

            def recv(self):
                open_recv.remove(self)
                copy(*self.parts).wait_recv()

            def sent(self):
                open_send.remove(self)
                copy(*self.parts).wait_send()

        class Ring:
            def __init__(self, n, src, dst, dev):
                self.n, self.src, self.dst, self.dev = n, src, dst, dev
                self.s, self.r = sem_block(n - 1), sem_block(n - 1)

            def each(self, f):
                def body(i, _):
                    d = i + 1
                    f(copy(self.src(d), self.dst(d), self.s + i, self.r + i, self.dev(d)))
                    return 0

                lax.fori_loop(0, self.n - 1, body, 0)

            def start(self):
                self.each(lambda c: c.start())
                open_recv.append(self)
                open_send.append(self)

            def recv(self):
                open_recv.remove(self)
                self.each(lambda c: c.wait_recv())

            def sent(self):
                open_send.remove(self)
                self.each(lambda c: c.wait_send())

        class Sides:
            def __init__(self, src_left, src_right, rx):
                self.ls, self.lr, self.rs, self.rr = (sem_block(1) for _ in range(4))
                self.rx = rx
                self.src_left, self.src_right = src_left, src_right

            @property
            def to_left(self):
                return copy(self.src_left, self.rx.at[1], self.ls, self.lr, {"tile": t - 1, "grp": g})

            @property
            def to_right(self):
                return copy(self.src_right, self.rx.at[0], self.rs, self.rr, {"tile": t + 1, "grp": g})

            def start(self):
                open_recv.append(self)
                open_send.append(self)

                @pl.when(t > 0)
                def _():
                    self.to_left.start()

                @pl.when(t < T - 1)
                def _():
                    self.to_right.start()

                @pl.when(t == 0)
                def _():
                    self.rx[0] = jnp.zeros(self.rx.shape[1:], self.rx.dtype)

                @pl.when(t == T - 1)
                def _():
                    self.rx[1] = jnp.zeros(self.rx.shape[1:], self.rx.dtype)

            def recv(self):
                open_recv.remove(self)

                @pl.when(t < T - 1)
                def _():
                    self.to_left.wait_recv()

                @pl.when(t > 0)
                def _():
                    self.to_right.wait_recv()

            def sent(self):
                open_send.remove(self)

                @pl.when(t > 0)
                def _():
                    self.to_left.wait_send()

                @pl.when(t < T - 1)
                def _():
                    self.to_right.wait_send()

        def started(c):
            c.start()
            return c

        def finish():
            loaded(*loads)
            for c in tuple(open_recv):
                c.recv()
            for c in tuple(open_send):
                c.sent()
            for src, dst, k in out_copies:
                pltpu.make_async_copy(src, dst, sems.at[nil + k]).wait()

        barrier = pltpu.get_barrier_semaphore()

        def chip_dev(d):
            o = lax.rem(ch + d, NCH)
            return {"tile": (o // NG) * 2 + core, "grp": lax.rem(o, NG)}

        def greet(dev):
            pl.semaphore_signal(barrier, inc=1, device_id=dev, device_id_type=MESH)

        def greet_chip(i, _):
            greet(chip_dev(i + 1))
            return 0

        lax.fori_loop(0, NCH - 1, greet_chip, 0)
        greet(partner)
        beside = t - 1 + 2 * core
        has_beside = (beside >= 0) & (beside < T)

        @pl.when(has_beside)
        def _():
            greet({"tile": beside, "grp": g})

        loads = {}

        def load(name, src, dst):
            c = pltpu.make_async_copy(src, dst, sems.at[sem_block(1)])
            c.start()
            loads[name] = c

        def loaded(*names):
            for name in names:
                loads.pop(name).wait()

        if inside:
            load("kmid", kmid_h, kmid)
            load("kin", kin_h, kin)
            load("kb", kb_h, kb)
        load("feat", feat_h, feat)
        load("geof", geof_h, geof)
        load("send", send_h, send)
        if inside:
            for l in range(3):
                load(l, kout_h.at[l, core], ownw.at[l])
        own_lanes = pl.ds(pl.multiple_of(t * NM, NM), NM)
        for name, src, dst in (
            ("lkf", lkf_h, lkf), ("slf", slf_h, slf), ("lkm", lkm_h, lkm), ("slm", slm_h, slm),
            ("own", geom_h.at[:, own_lanes], geom_own), ("lkc", lkc_h, lkc), ("slc", slc_h, slc), ("geom", geom_h, geom),
            ("geoc", geoc_h, geoc), ("parf", parf_h, parf), ("parm", parm_h, parm), ("cot", cot_h, cot),
        ):
            load(name, src, dst)

        if inside:
            loaded("kmid", "kin", "kb")
            order = column_order(KW, NG, True)
            for l in range(3):
                second = dot(kmid[l].astype(BF), order)
                first = dot(kin[l].astype(BF), place(6, 128, [(0, 0, 3), (3, 5, 3)]), TN)
                first = first + dot(kb[l].astype(BF), place(2, 128, [(0, 3, 1), (1, 8, 1)]), TN)
                if l == 0:
                    smbuf[ch, core] = jnp.concatenate([second, first], axis=1)
                else:
                    smx[l - 1, 0] = second
                    smx[l - 1, 1] = jnp.concatenate([first, jnp.zeros((8, KW - 128), F32)], axis=1)
        pl.semaphore_wait(barrier, NCH + has_beside.astype(I32))
        if inside:
            sm_a0 = started(Ring(NCH, lambda d: smbuf.at[ch, core], lambda d: smbuf.at[ch, core], chip_dev))
            s0c = [[started(One(kout_h.at[l, ocore], s0buf.at[l], partner))] for l in range(3)]
            for l in range(2):
                s0c[l].append(started(One(smx.at[l, ocore], s0x.at[l], partner)))
        loaded("feat", "geof", "send")
        n0 = fine.nodes
        extT[:, 0:n0] = (
            dot(place(80, C, [(0, 0, C)]), feat[...]) + dot(place(80, 3, [(C + 5, 0, 3)]), geof[...])
        ).astype(BF)
        tx_s[0] = dot(extT[:, 0:n0], one_hot(send[...], 0, n0)).astype(BF)
        halo_x = started(Sides(tx_s.at[0], tx_s.at[0], rx_s))

        def window(index, start, n, at):
            off = index - start
            return jnp.where(off < 0, off + at + 8, jnp.where(off >= n, off - n + at + 8, off))

        if not inside:
            own_copy(kmid_h, smfull)
            own_copy(kout_h, agbuf)

        ag = [[] for _ in range(3)]
        wide = (BW, BW, HALF)

        def ag_s1(l):
            if not inside:
                return
            for c in s0c[l]:
                c.recv()
            mine, theirs = ownw[l], s0buf[l]
            if l < 2:
                mine = jnp.concatenate([mine, smx[l, core]], axis=1)
                theirs = jnp.concatenate([theirs, s0x[l]], axis=1)
            first = core == 0
            agbuf[l, core, hi, lo, g, :, 0 : wide[l]] = jnp.concatenate(
                [jnp.where(first, mine, theirs), jnp.where(first, theirs, mine)], axis=0
            ).astype(BF)

            def part(d):
                return agbuf.at[ix(l), core, hi, lo, g, :, 0 : wide[l]]

            c = Ring(H, part, part, lambda d: {"tile": tile_of(lax.rem(hi + d, H), lo, core), "grp": g})
            c.start()
            ag[l].append([c])

        def ag_next(l, *copies):
            if not inside:
                return
            for c in ag[l][-1]:
                c.recv()
            for c in copies:
                c.start()
            ag[l].append(copies)

        def ag_s2(l):
            part = agbuf.at[ix(l), core, :, lo, g, :, 0 : wide[l]]
            ag_next(l, One(part, part, xn), One(part, part, yn))

        def ag_s3(l):
            a = agbuf.at[ix(l), core, :, olo, g, :, 0:QH]
            b = agbuf.at[ix(l), core, :, lo, og, :, QH : wide[l]]
            ag_next(l, One(a, a, yn), One(b, b, xn))

        def ag_s4(l):
            part = agbuf.at[ix(l), core, :, :, :, :, 0 : wide[l]]
            ag_next(l, One(part, part, partner))

        def ag_fin(l):
            if inside:
                for c in ag[l][-1]:
                    c.recv()
                for cs in ag[l]:
                    for c in cs:
                        c.sent()
        def unpack_small(l):
            if not inside:
                block = smfull[l].reshape(KW, SMW)
                second, first = block[:, 0:KW], block[:, KW:]
            elif l == 0:
                block = smbuf[...].reshape(KW, SMW)
                second, first = block[:, 0:KW], block[:, KW:]
            else:
                second = agbuf[l - 1, 0, :, :, :, :, HALF:BW].reshape(KW, KW).astype(F32)
                first = agbuf[l - 1, 1, :, :, :, :, HALF : HALF + 128].reshape(KW, 128).astype(F32)
            wbr[l] = second.astype(BF)
            wbT[l] = second.T.astype(BF)
            waT[l] = first[:, 0:8].astype(BF)
            bbc[:, l : l + 1] = first[:, 8:9]

        mts, qts = (mt0, mt1, mt2), (mt0, qt1, qt2)
        xss, zss, pks, a2s = (xs0, xs1, xs2), (zs0, zs1, zs2), (pk0, pk1, pk2), (as0, as1, as2)

        def pack_nodes(lv, links, used, geometry):
            k, n = links.shape
            links = jnp.where(iota((k, n), 0) < used, links, -1).astype(F32)
            high = links.astype(BF).astype(F32)
            rows = dot(place(8, 3, [(0, 0, 3)]), geometry) + jnp.where(iota((8, n), 0) == 3, 1.0, 0.0)
            pad = jnp.zeros((128 - 2 * k - 8, n), F32)
            pks[lv.index][...] = jnp.concatenate([high, links - high, rows, pad], axis=0).T.astype(BF)

        def edge_columns(lv, i):
            k = lv.slots
            n = lv.lanes // k
            at = pl.ds(pl.multiple_of(i * n, n), n)
            nodes = (iota((n, lv.lanes), 1) >> log2(k) == iota((n, lv.lanes), 0)).astype(F32).astype(BF)
            got = dot(pks[lv.index][at, :], nodes, TN)
            slot = iota((k, lv.lanes), 1) & (k - 1) == iota((k, lv.lanes), 0)
            links = jnp.sum(jnp.where(slot, got[0:k] + got[k : 2 * k], 0.0), axis=0, keepdims=True)
            return links, got[2 * k : 2 * k + 8]

        def take(table, row, lv, rows):
            top, hot = row >> 7, one_hot(row & 127, 0, 128)
            n = min(lv.parts, 16)

            def some(first):
                got = dot(table(first, n), hot)
                acc = jnp.zeros((rows, lv.lanes), F32)
                for h in range(n):
                    acc = acc + jnp.where(top == first + h, got[rows * h : rows * (h + 1)], 0.0)
                return acc

            if n == lv.parts:
                return some(0)
            return lax.fori_loop(0, lv.parts // n, lambda k, acc: acc + some(k * n), jnp.zeros((rows, lv.lanes), F32))

        def put(acc, values, row, lv):
            top, hot = row >> 7, one_hot(row & 127, 0, 128)
            n = min(lv.parts, 16)

            def some(first):
                each = [values * jnp.where(top == first + h, 1.0, 0.0).astype(BF) for h in range(n)]
                acc[pl.ds(first, n)] += dot(jnp.concatenate(each, axis=0), hot, NT).reshape(n, C, 128)

            if n == lv.parts:
                some(0)
                return

            def body(k, _):
                some(k * n)
                return 0

            lax.fori_loop(0, lv.parts // n, body, 0)

        def at_step(i, events):
            for when, call in events:

                @pl.when(i == when)
                def _():
                    call()

        def edge_geometry(lv, x_table, g_table, events=()):
            l = lv.index

            def body(i, _):
                at_step(i, events)
                links, z = edge_columns(lv, i)
                row = links.astype(I32)
                if g_table is None:
                    got = dot(x_table[...], one_hot(row, 0, lv.sources))
                    xss[l][i] = got[0:C].astype(BF)
                    z = z + got[C : C + 8]
                else:
                    z = z + take(g_table, row, lv, 8)
                zss[l][i] = jnp.where(iota((8, lv.lanes), 0) == 4, links, z)
                return 0

            lax.fori_loop(0, lv.steps, body, 0)

        def hidden(l, z):
            t1 = dot(waT[l], z.astype(BF))
            a1 = (t1 * sig(t1)).astype(BF)
            t2 = dot(wbT[l], a1) + bbc[:, l : l + 1]
            return (t2 * sig(t2)).astype(BF)

        def edge_hidden(lv):
            l = lv.index

            def body(i, _):
                a2s[l][i] = hidden(l, zss[l][i])
                return 0

            lax.fori_loop(0, lv.steps, body, 0)

        def edges_forward(lv, x_table, events=()):
            l = lv.index
            mask = group_mask(lv.width)

            def body(i, _):
                at_step(i, events)
                if x_table is None:
                    x = xss[l][i].astype(F32)
                    a2 = hidden(l, zss[l][i])
                    a2s[l][i] = a2
                else:
                    x = take(x_table, zss[l][i, 4:5, :].astype(I32), lv, C)
                    xss[l][i] = x.astype(BF)
                    a2 = a2s[l][i]
                for k in range(lv.blocks):
                    sl = slice(lv.width * k, lv.width * (k + 1))
                    m = dot(spread(x[:, sl], mask), a2[:, sl], NT)
                    mts[l][:, lv.blocks * i + k] = m.astype(BF).reshape(C // 2, 2 * GROUP, KW)
                return 0

            lax.fori_loop(0, lv.steps, body, 0)

        def third(l, pair):
            per_half = C // 4
            half, k = pair // per_half, lax.rem(pair, per_half)
            return agbuf[l, half, :, :, :, :, pl.ds(pl.multiple_of(k * 128, 128), 128)].reshape(KW, 2 * C)

        def node_sums(lv):
            l, n = lv.index, lv.nodes
            each = 8

            def body(i, acc):
                w = jnp.concatenate([third(l, each * i + u) for u in range(each)], axis=0)
                m = jnp.concatenate([mts[l][each * i + u].reshape(2 * n, KW) for u in range(each)], axis=1)
                return acc + dot(m, w)

            acc = lax.fori_loop(0, C // 2 // each, body, jnp.zeros((2 * n, 2 * C), F32))
            acc = acc.reshape(n // GROUP, 2, GROUP, 2 * C)
            both = acc[:, 0].reshape(n, 2 * C) + pltpu.roll(acc[:, 1].reshape(n, 2 * C), C, 1)
            return both.T[0:C]

        def by_parity(lv, gsT):
            n = lv.nodes
            gsT = gsT.astype(F32)
            even = jnp.concatenate([gsT, jnp.zeros(gsT.shape, F32)], axis=0).T[0:n]
            odd = pltpu.roll(even, C, 1)
            shape = (n // GROUP, 1, GROUP, 2 * C)
            return jnp.concatenate([even.reshape(shape), odd.reshape(shape)], axis=1).reshape(2 * n, 2 * C)

        def stage(l):
            return agbuf.at[ix(l), :, :, :, :, :, 0:HALF] if l else gbuf

        def third_grad(lv, gs):
            l = lv.index
            n = C // 4
            each = 8
            turned = gs.T.astype(BF)

            def body(j, _):
                for u in range(each):
                    i = each * j + u
                    both = dot(turned, mts[l][i].reshape(2 * lv.nodes, KW))
                    out = both.T.astype(BF).reshape(A, 2, NG, 16, 128)
                    stage(l)[i // n, :, :, :, :, pl.ds(pl.multiple_of(lax.rem(i, n) * 128, 128), 128)] = out
                return 0

            lax.fori_loop(0, C // 2 // each, body, 0)

        def node_weights(lv, gs, events=()):
            l = lv.index
            each = 8
            gs = gs.astype(BF)

            def body(j, _):
                at_step(j, events)
                for u in range(each):
                    i = each * j + u
                    q = dot(gs, third(l, i), NT)
                    qts[l][i] = q.astype(BF).reshape(lv.nodes // GROUP, 2 * GROUP, KW)
                return 0

            lax.fori_loop(0, C // 2 // each, body, 0)

        def source_grads(lv, acc, events=()):
            l = lv.index
            mask = group_mask(lv.width)
            fold = (iota((C, C * GROUP), 1) >> log2(GROUP) == iota((C, C * GROUP), 0)).astype(F32).astype(BF)

            def body(i, _):
                at_step(i, events)
                gxs = []
                for k in range(lv.blocks):
                    sl = slice(lv.width * k, lv.width * (k + 1))
                    q = qts[l][:, lv.blocks * i + k].reshape(C * GROUP, KW)
                    every = dot(q, a2s[l][i, :, sl])
                    own = (every.reshape(C, GROUP, lv.width) * mask[None]).reshape(C * GROUP, lv.width).astype(BF)
                    gxs.append(own)
                gx = dot(fold, jnp.concatenate(gxs, axis=1)).astype(BF)
                put(acc, gx, zss[l][i, 4:5, :].astype(I32), lv)
                return 0

            lax.fori_loop(0, lv.steps, body, 0)

        def weight_grads(lv, first, last, events=()):
            l = lv.index
            mask = group_mask(lv.width)

            def body(i, _):
                at_step(i, events)
                zb = zss[l][i].astype(BF)
                t1 = dot(waT[l], zb)
                s1 = sig(t1)
                f1 = t1 * s1
                d1 = s1 + f1 * (1.0 - s1)
                a1 = f1.astype(BF)
                t2 = dot(wbT[l], a1) + bbc[:, l : l + 1]
                s2 = sig(t2)
                d2 = s2 + t2 * s2 * (1.0 - s2)
                x = xss[l][i].astype(F32)
                g2s = []
                for k in range(lv.blocks):
                    sl = slice(lv.width * k, lv.width * (k + 1))
                    q = qts[l][:, lv.blocks * i + k].reshape(C * GROUP, KW)
                    g2s.append((dot(q, spread(x[:, sl], mask), TN) * d2[:, sl]).astype(BF))
                g2 = jnp.concatenate(g2s, axis=1)
                g1 = (dot(wbr[l], g2) * d1).astype(BF)
                zz = jnp.concatenate([zb, zb], axis=0)
                both = dot(jnp.concatenate([a1, zz], axis=0), g2, NT)
                gsb[l, :, :, :, 0:KW] += both[0:KW].reshape(NB, 2, 8, KW)
                gp[l, 0] += dot(zz, g1, NT)[0:8]
                gp[l, 1] += both[KW : KW + 8]
                return 0

            lax.fori_loop(first, last, body, 0)

        def roll_pick(left, right, n_left, left_lane, right_lane):
            lane = iota((1, 128), 1)
            a = pltpu.roll(left, (left_lane - (n_left - 8)) % 128, 1)
            b = pltpu.roll(right, right_lane % 128, 1)
            return jnp.where((lane >= left_lane) & (lane < left_lane + 8), a, 0.0) + jnp.where(
                (lane >= right_lane) & (lane < right_lane + 8), b, 0.0
            )

        def margin_pick(from_left, from_right, n_own, left_at, right_at):
            lane = iota((1, 128), 1)
            a = pltpu.roll(from_left, (0 - right_at) % 128, 1)
            b = pltpu.roll(from_right, (n_own - 8 - left_at) % 128, 1)
            return jnp.where(lane < 8, a, 0.0) + jnp.where((lane >= n_own - 8) & (lane < n_own), b, 0.0)

        if inside:
            loaded(0, 1, 2)
        ag_s1(0)
        loaded("lkf", "slf", "parf")
        pack_nodes(fine, lkf[...], slf[...], geof[...])
        halo_x.recv()
        near, far = (pltpu.roll(rx_s[k].astype(F32), halo, 1) for k in (0, 1))
        extT[:, n0:] = jnp.where(iota((1, 128), 1) < halo, near, far).astype(BF)
        small_b = []

        def a0_next():
            if inside:
                sm_a0.recv()
                small_b.append(started(One(smbuf.at[:, core], smbuf.at[:, core], partner)))

        edge_geometry(fine, extT, None, [(2, lambda: ag_s2(0)), (2, lambda: ag_s1(1)), (4, a0_next)])
        if inside:
            sm_b0 = small_b[0]
            sm_b0.recv()
        unpack_small(0)
        edges_forward(
            fine, None,
            [(2, lambda: ag_s3(0)), (2, lambda: ag_s1(2)), (5, lambda: ag_s4(0)), (5, lambda: ag_s2(1))],
        )
        ohp[...] = one_hot(window(parf[...], t * NM, NM, NM), 0, 2 * NM)
        nf = slf[...].astype(F32)
        ag_fin(0)
        v0 = extT[0:C, 0 : fine.nodes].astype(F32) + node_sums(fine) / nf
        v0s[...] = v0

        ones8 = jnp.ones((8, fine.nodes), BF)
        part = dot(jnp.concatenate([split3(v0), ones8], axis=0), ohp[...], NT)
        sums = jnp.concatenate([join3(part[0 : 3 * C]), part[3 * C :]], axis=0)
        tx_w[0] = sums[:, NM:]
        ex_w = started(Sides(tx_w.at[0], tx_w.at[0], rx_w))
        loaded("lkm", "slm", "own", "lkc", "slc", "geom", "geoc", "parm", "cot")
        pack_nodes(mid, lkm[...], slm[...], geom_own[...])
        lkc_wide[...] = jnp.zeros(lkc_wide.shape, F32)
        lkc_wide[0:NC] = lkc[...].astype(F32)
        slc_wide[...] = jnp.ones(slc_wide.shape, I32)
        slc_wide[:, 0:NC] = slc[...]
        eye = place(coarse.slots, coarse.slots, [(0, 0, coarse.slots)])
        high = lkc_wide[...].astype(BF)
        low = (lkc_wide[...] - high.astype(F32)).astype(BF)
        turned = (dot(eye, high, NT) + dot(eye, low, NT)).astype(I32)
        lanes = iota((1, 128), 1)
        own_c = jnp.where(lanes < NC, t * NC + lanes, -1)
        geo = dot(geoc[...], one_hot(own_c, 0, coarse.sources)).astype(BF)
        pack_nodes(coarse, turned, jnp.where(lanes < NC, slc_wide[...], 0), geo)
        to_rows = place(8, 3, [(5, 0, 3)])
        for table, source, lv in ((gm, geom, mid), (gc, geoc, coarse)):
            rows = dot(to_rows, source[...])
            for k in range(lv.parts):
                table[k] = rows[:, 128 * k : 128 * (k + 1)]
        nm, nc = (v[...].astype(F32) for v in (slm, slc_wide))
        blocks = [parm[:, pl.ds(pl.multiple_of(b * NM, NM), NM)].astype(F32)
                  for b in (jnp.maximum(t - 1, 0), t, jnp.minimum(t + 1, T - 1))]
        before, after = (pltpu.roll(jnp.broadcast_to(v, (8, NM)), 8, 1)[0:1] for v in (blocks[0], blocks[2]))
        sides = jnp.where((lanes < 8) & (t > 0), before, jnp.where((lanes >= 8) & (lanes < 16) & (t < T - 1), after, -1.0))
        around = jnp.concatenate([blocks[1], sides], axis=1).astype(I32)
        pw = jnp.where(around < 0, -1, window(around, t * NC, NC, NC))
        unpack_small(1)
        ag_s3(1)
        ex_w.recv()
        own = sums[:, 0:NM] + margin_pick(rx_w[0], rx_w[1], NM, 0, 8)
        inv1 = 1.0 / jnp.maximum(own[C : C + 1], 1.0)
        v1 = own[0:C] / jnp.maximum(own[C : C + 1], 1.0)
        x1b[r, core] = v1.astype(BF)

        def chip_ring(src, dst):
            return Ring(R, src, dst, lambda d: {"tile": lax.rem(r + d, R) * 2 + core, "grp": g})

        ag1 = started(chip_ring(lambda d: x1b.at[r, core], lambda d: x1b.at[r, core]))
        ag_s2(2)
        g_rows = lambda table: lambda first, n: table[pl.ds(first, n)].reshape(n * 8, 128).astype(BF)
        edge_geometry(mid, None, g_rows(gm))
        edge_hidden(mid)
        ag_s4(1)
        ag1.recv()
        ag1p = started(One(x1b.at[:, core], x1b.at[:, core], partner))
        ag1p.recv()

        def x1_rows(first, n):
            return x1b[pl.ds(first // 2, n // 2)].reshape(n * C, 128)

        edges_forward(mid, x1_rows, [(2, lambda: ag_s3(2))])
        ag_fin(1)
        unpack_small(2)
        w1 = v1 + node_sums(mid) / nm
        tx_q[0, 0:C] = w1
        ohq = one_hot(pw, 0, 128)
        part = dot(jnp.concatenate([split3(w1), jnp.ones((8, NM), BF)], axis=0), ohq[:, 0:NM], NT)
        tx_q[0, C : 2 * C + 8] = jnp.concatenate([join3(part[0 : 3 * C]), part[3 * C :]], axis=0)
        ex_q = started(Sides(tx_q.at[0], tx_q.at[0], rx_q))
        edge_geometry(coarse, None, g_rows(gc))
        edge_hidden(coarse)
        ag_s4(2)
        ex_q.recv()
        own = tx_q[0, C : 2 * C + 8] + margin_pick(rx_q[0, C : 2 * C + 8], rx_q[1, C : 2 * C + 8], NC, NC, NC + 8)
        w1m = roll_pick(rx_q[0, 0:C], rx_q[1, 0:C], NM, 0, 8)
        w1win = jnp.concatenate([w1, w1m], axis=1)
        lane = iota((1, 128), 1)
        mine = lane < NC
        cnt2 = jnp.maximum(own[C : C + 1], 1.0)
        v2 = jnp.where(mine, own[0:C] / cnt2, 0.0)

        x2b[r, core] = v2.astype(BF)
        ag2 = started(chip_ring(lambda d: x2b.at[r, core], lambda d: x2b.at[r, core]))
        ag2.recv()
        ag2p = started(One(x2b.at[:, core], x2b.at[:, core], partner))
        ag2p.recv()
        per = 128 // NC
        cols = []
        for k in range(coarse.sources // 128):
            block = x2b[per * k // 2, 0].astype(F32)
            for u in range(1, per):
                block = block + pltpu.roll(x2b[(per * k + u) // 2, (per * k + u) % 2].astype(F32), NC * u, 1)
            cols.append(block.astype(BF))
        for k, block in enumerate(cols):
            x2T[k] = block
        edges_forward(coarse, lambda first, n: x2T[pl.ds(first, n)].reshape(n * C, 128))
        ag_fin(2)
        sc = node_sums(coarse)
        sc = jnp.concatenate([sc, jnp.zeros((C, 128 - NC), F32)], axis=1)
        w2 = v2 + jnp.where(mine, sc / nc, 0.0)
        tx_u[0] = w2
        ex_u = started(Sides(tx_u.at[0], tx_u.at[0], rx_u))
        ex_u.recv()
        w2win = w2 + roll_pick(rx_u[0], rx_u[1], NC, NC, NC + 8)

        y1win = w1win + join3(dot(split3(w2win), ohq))
        y0 = v0s[...] + join3(dot(split3(y1win), ohp[...]))
        s0 = sig(y0)
        f0 = y0 * s0
        layer[...] = f0.astype(BF)
        gy0 = cot[...] * (s0 + f0 * (1.0 - s0))
        gys[...] = gy0
        gy1p = join3(dot(split3(gy0), ohp[...], NT))
        gw2p = join3(dot(split3(gy1p), ohq, NT))
        tx_g[0, 0:C] = gy1p[:, NM:]
        tx_g[0, C : 2 * C] = gw2p
        ex_g = started(Sides(tx_g.at[0], tx_g.at[0], rx_g))
        ex_g.recv()
        gy1 = gy1p[:, 0:NM] + margin_pick(rx_g[0, 0:C], rx_g[1, 0:C], NM, 0, 8)
        gw2 = jnp.where(mine, gw2p + margin_pick(rx_g[0, C:], rx_g[1, C:], NC, NC, NC + 8), 0.0)

        rs = [[] for _ in range(3)]

        def rs_step(l, fix, *copies):
            if not inside:
                return
            if rs[l]:
                for c in rs[l][-1]:
                    c.recv()
            fix()
            for c in copies:
                c.start()
            rs[l].append(copies)

        def landing(l):
            return gbuf.at[ix(2 - l)] if l and inside else rsr0

        def rs_s0(l):
            rs_step(l, lambda: None, One(stage(l).at[ocore], landing(l), partner))

        def rs_s1(l):
            def fix():
                def body(i, _):
                    both = stage(l)[core, i].astype(F32) + landing(l)[i].astype(F32)
                    stage(l)[core, i] = both.astype(BF)
                    return 0

                lax.fori_loop(0, H, body, 0)

            rs_step(
                l, fix,
                One(stage(l).at[core, :, olo, og, :, 0:QH], rsr1.at[ix(l % 2), ix(0)], xn),
                One(stage(l).at[core, :, olo, og, :, QH:HALF], rsr1.at[ix(l % 2), ix(1)], yn),
            )

        def rs_s2(l):
            def fix():
                def body(i, _):
                    a = stage(l)[core, i, lo, og, :, 0:QH].astype(F32) + rsr1[l % 2, 0, i].astype(F32)
                    stage(l)[core, i, lo, og, :, 0:QH] = a.astype(BF)
                    b = stage(l)[core, i, olo, g, :, QH:HALF].astype(F32) + rsr1[l % 2, 1, i].astype(F32)
                    stage(l)[core, i, olo, g, :, QH:HALF] = b.astype(BF)
                    return 0

                lax.fori_loop(0, H, body, 0)

            rs_step(
                l, fix,
                One(stage(l).at[core, :, lo, og], rsr2.at[ix(l % 2), ix(0)], yn),
                One(stage(l).at[core, :, olo, g], rsr2.at[ix(l % 2), ix(1)], xn),
            )

        def rs_s3(l):
            def fix():
                def body(i, _):
                    a = stage(l)[core, i, lo, g].astype(F32) + rsr2[l % 2, 0, i].astype(F32) + rsr2[l % 2, 1, i].astype(F32)
                    stage(l)[core, i, lo, g] = a.astype(BF)
                    return 0

                lax.fori_loop(0, H, body, 0)

            rs_step(
                l, fix,
                Ring(
                    H,
                    lambda d: stage(l).at[core, lax.rem(hi + d, H), lo, g],
                    lambda d: rsr3.at[ix(l % 2), d - 1],
                    lambda d: {"tile": tile_of(lax.rem(hi + d, H), lo, core), "grp": g},
                ),
            )

        def rs_s4(l):
            def fix():
                tot = stage(l)[core, hi, lo, g].astype(F32)
                for k in range(H - 1):
                    tot = tot + rsr3[l % 2, k].astype(F32)
                rsf[l, 0] = tot[0:8]
                rsf[l, 1] = tot[8:16]

            rs_step(l, fix, One(rsf.at[ix(l), ocore], rsr4.at[ix(l)], partner))

        def rs_s5(l):
            if not inside:
                own_copy(stage(l), gwc.at[l])
                return
            for c in rs[l][-1]:
                c.recv()
            for src, dst in ((rsf.at[ix(l), core], gwc.at[ix(l), core]), (rsr4.at[ix(l)], gwc.at[ix(l), ocore])):
                out_copies.append((src, dst, sem_block(1)))
                pltpu.make_async_copy(src, dst, sems.at[nil + out_copies[-1][2]]).start()

        if inside:
            sm_a0.sent()
            sm_b0.sent()
        gsb[...] = jnp.zeros(gsb.shape, F32)
        gp[...] = jnp.zeros(gp.shape, F32)
        gs_copies = {}

        def gs_start(a, b):
            for l in range(a, b):
                tall = jnp.concatenate([gp[l, 0], gp[l, 1], jnp.zeros((112, KW), F32)], axis=0)
                gsb[l, :, :, :, KW:] = tall.T.reshape(NB, 2, 8, 128)
            if inside:
                gs_copies[a] = started(One(gsb.at[a:b, :, ocore], rcA.at[a:b], partner))

        def gs_ring(a, b):
            if inside:
                gs_copies[a].recv()
                for l in range(a, b):
                    gsb[l, :, core] += rcA[l]
                gs_copies[a] = started(
                    Ring(
                        NCH,
                        lambda d: gsb.at[a:b, lax.rem(ch + d, NCH), core],
                        lambda d: rcB.at[d - 1, a:b],
                        chip_dev,
                    )
                )

        def gs_end(a, b):
            if not inside:
                gsmall[a:b] = gsb[a:b]
                return
            gs_copies[a].recv()

            def add3(k, acc):
                return acc + rcB[k, a:b]

            gsmall[a:b] = lax.fori_loop(0, NCH - 1, add3, gsb[a:b, ch, core])


        gs2T = jnp.where(mine, gw2 / nc, 0.0).astype(BF)
        gs2 = by_parity(coarse, gs2T)
        node_weights(coarse, gs2)
        acc2[...] = jnp.zeros(acc2.shape, F32)
        source_grads(coarse, acc2)
        zero = jnp.zeros((C, 128), F32)
        for k in range(coarse.parts):
            rows = jnp.concatenate([acc2[k], zero], axis=0).T.astype(BF)
            acc2b[per // 2 * k : per // 2 * (k + 1)] = rows.reshape(per // 2, 2, NC, 128)
        r2p = started(One(acc2b.at[:, ocore], rs2a, partner))
        weight_grads(coarse, 0, 1)
        r2p.recv()
        acc2b[:, core] = (acc2b[:, core].astype(F32) + rs2a[...].astype(F32)).astype(BF)
        r2 = started(chip_ring(lambda d: acc2b.at[lax.rem(r + d, R), core], lambda d: rs2buf.at[d - 1]))
        weight_grads(coarse, 1, coarse.steps)
        third_grad(coarse, gs2)
        r2.recv()

        def add2(k, acc):
            return acc + rs2buf[k].astype(F32)

        own2 = lax.fori_loop(0, R - 1, add2, acc2b[r, core].astype(F32))
        own2 = jnp.concatenate([own2, jnp.zeros((128 - NC, 128), F32)], axis=0).T[0:C]
        gv2 = jnp.where(mine, (gw2 + own2) / cnt2, 0.0)
        ex_u.sent()
        tx_b[0] = gv2
        ex_b = started(Sides(tx_b.at[0], tx_b.at[0], rx_b))
        rs_s0(2)
        ex_b.recv()
        gv2win = gv2 + roll_pick(rx_b[0], rx_b[1], NC, NC, NC + 8)
        gw1 = gy1 + join3(dot(split3(gv2win), ohq[:, 0:NM]))

        gs1T = (gw1 / nm).astype(BF)
        gs1 = by_parity(mid, gs1T)
        node_weights(mid, gs1)
        acc1[...] = jnp.zeros(acc1.shape, F32)
        rs_s1(2)
        source_grads(mid, acc1, [(2, lambda: rs_s2(2))])
        ag1.sent()
        ag1p.sent()
        acc1b[...] = acc1[...].astype(BF).reshape(acc1b.shape)
        r1p = started(One(acc1b.at[:, ocore], rs1a, partner))
        half = mid.steps // 2
        third_grad(mid, gs1)
        r1p.recv()
        acc1b[:, core] = (acc1b[:, core].astype(F32) + rs1a[...].astype(F32)).astype(BF)
        r1 = started(chip_ring(lambda d: acc1b.at[lax.rem(r + d, R), core], lambda d: rs1buf.at[d - 1]))
        rs_s0(1)
        weight_grads(mid, 0, half)
        r1.recv()

        def add1(k, acc):
            return acc + rs1buf[k].astype(F32)

        own1 = lax.fori_loop(0, R - 1, add1, acc1b[r, core].astype(F32))
        gv1 = (gw1 + own1) * inv1
        tx_f[0] = gv1
        ex_f = started(Sides(tx_f.at[0], tx_f.at[0], rx_f))
        rs_s1(1)
        rs_s3(2)
        weight_grads(mid, half, mid.steps)
        gs_start(1, 3)
        ex_f.recv()
        gv1win = jnp.concatenate([gv1, roll_pick(rx_f[0], rx_f[1], NM, 0, 8)], axis=1)
        gv0 = gys[...] + join3(dot(split3(gv1win), ohp[...]))
        gys[...] = gv0

        gs0 = gv0 / nf
        gs0T = gs0.astype(BF)
        gs0 = by_parity(fine, gs0T)
        rs_s2(1)
        gs_ring(1, 3)
        third_grad(fine, gs0)
        rs_s0(0)
        node_weights(fine, gs0, [(1, lambda: rs_s1(0))])
        rs_s4(2)
        rs_s3(1)
        weight_grads(
            fine, 0, fine.steps,
            [(2, lambda: rs_s2(0)), (3, lambda: rs_s5(2)), (5, lambda: rs_s4(1)), (7, lambda: rs_s3(0))],
        )
        gs_start(0, 1)
        acc0[...] = jnp.zeros(acc0.shape, F32)
        source_grads(
            fine, acc0, [(1, lambda: gs_ring(0, 1)), (2, lambda: rs_s5(1)), (3, lambda: gs_end(1, 3)), (6, lambda: rs_s4(0))]
        )
        ex_b.sent()
        tx_h[0] = acc0[fine.parts - 1]
        ex_h = started(Sides(tx_h.at[0], tx_h.at[0], rx_h))
        rs_s5(0)
        gs_end(0, 1)
        ex_h.recv()
        lane1 = iota((1, 128), 1)
        back = jnp.where(lane1 < halo, pltpu.roll(rx_h[0], halo, 1), pltpu.roll(rx_h[1], halo, 1))
        ohs2 = one_hot(send[...], 0, n0)
        own0 = jnp.concatenate([acc0[k] for k in range(fine.parts - 1)], axis=1)
        gf = gys[...] + own0 + join3(dot(split3(back), ohs2, NT))
        gradf[...] = gf.astype(BF)
        finish()

    n_sems = (
        2 * (2 * (NCH - 1)) + 4 + 2 * 3 + 3 * (2 * (H - 1) + 4 + 4 + 2) + 4
        + 4 * 7 + 4 * (2 * (T - 1)) + 4 * NCH + 3 * (2 + 4 + 4 + 2 * (H - 1) + 2) + 2 + 2 * (NCH - 1) + 32
    )
    V = pltpu.VMEM
    ls, la = (3, A) if inside else (1, 1)
    by_group = lambda n: V((C // 2, n // GROUP, 2 * GROUP, KW), BF)
    nf, nm_, nc_ = fine.nodes, NM, NC
    scratch = [
        V((C, nf), BF), V((C, nf), F32), V((3, nf), BF), V((3, mid.sources), BF), V((3, coarse.sources), BF),
        V((fine.slots, nf), I32), V((1, nf), I32), V((1, 2 * halo), I32), V((1, nf), I32), V((1, mid.sources), I32),
        V((mid.slots, nm_), I32), V((1, nm_), I32), V((nc_, coarse.slots), I32), V((1, nc_), I32),
        V((3, 6, 8), F32), V((3, 2, 8), F32), V((3, 8, KW), F32), V((ls, 8, HALF), F32),
        V((3, nm_), BF), V((128, coarse.slots), F32), V((1, 128), I32),
        V((nf, 128), BF), V((nm_, 128), BF), V((128, 128), BF), V((mid.parts, 8, 128), F32), V((coarse.parts, 8, 128), F32),
        V((80, nf + 2 * halo), BF),
        V((3, 2, A, 2, NG, 16, BW if inside else HALF), BF), V((2, A, 2, NG, 16, HALF), BF), V((ls, 8, HALF), F32),
        V((2, 8, KW), F32), V((2, 2, 8, KW), F32),
        V((1 if inside else 3, 1 if inside else NB, 2, 8, SMW), F32), V((3, KW, 8), BF), V((3, KW, KW), BF), V((3, KW, KW), BF), V((KW, 128), F32),
        by_group(nf), by_group(nm_), by_group(nc_), by_group(nm_), by_group(nc_),
        V((fine.steps, KW, fine.lanes), BF), V((mid.steps, KW, fine.lanes), BF), V((coarse.steps, KW, fine.lanes), BF),
        V((fine.steps, C, fine.lanes), BF), V((mid.steps, C, fine.lanes), BF), V((coarse.steps, C, fine.lanes), BF),
        V((fine.steps, 8, fine.lanes), F32), V((mid.steps, 8, fine.lanes), F32), V((coarse.steps, 8, fine.lanes), F32),
        V((2 * NM, nf), BF),
        V((1, 80, 128), BF), V((2, 80, 128), BF),
        V((1, C + 8, 128), F32), V((2, C + 8, 128), F32),
        V((1, 2 * C + 8, 128), F32), V((2, 2 * C + 8, 128), F32),
        V((1, C, 128), F32), V((2, C, 128), F32),
        V((1, 2 * C, 128), F32), V((2, 2 * C, 128), F32),
        V((1, C, 128), F32), V((2, C, 128), F32),
        V((R, 2, C, 128), BF), V((coarse.parts, C, 128), BF), V((R, 2, C, 128), BF),
        V((fine.parts, C, 128), F32), V((mid.parts, C, 128), F32), V((coarse.parts, C, 128), F32),
        V((R, 2, NC, 128), BF), V((R, C, 128), BF), V((R, NC, 128), BF),
        V((R - 1, C, 128), BF), V((R - 1, NC, 128), BF), V((C, nf), F32), V((C, nf), F32),
        V((la, 2, NG, 16, HALF), BF), V((2, 2, la, 16, QH), BF), V((2, 2, la, 16, HALF), BF),
        V((2, A - 1, 16, HALF), BF), V((ls, 2, 8, HALF), F32),
        V((3, NB, 2, 8, SMW), F32), V((3, 2, 8, KW), F32), V((ls, NB, 8, SMW), F32), V((NB - 1, 3, 8, SMW), F32),
        pltpu.SemaphoreType.DMA((n_sems,)),
    ]
    return kernel, scratch


def adamw(master, moment, square, grad, learn_rate):
    moment_new = B_ONE * moment + (1.0 - B_ONE) * grad
    square_new = B_TWO * square + (1.0 - B_TWO) * grad * grad
    fix_one = 1.0 - B_ONE**STEP
    fix_two = 1.0 - B_TWO**STEP
    master_new = master - learn_rate * (
        moment_new / fix_one / (jnp.sqrt(square_new / fix_two) + EPSILON) + WEIGHT_DECAY * master
    )
    return (master_new, moment_new, square_new)


def make_update(KW, NG, per, inside):
    rates = (RATE_FIRST, RATE_MAIN, RATE_MAIN, RATE_MAIN)

    def kernel(*refs):
        far_in, far_out, near_in, near_out, sems = refs[0:14], refs[16:28], refs[30:44], refs[44:56], refs[56]
        passing = refs[57:59]
        first = [pltpu.make_async_copy(refs[14 + k], passing[k], sems.at[26 + k]) for k in range(2)]
        for c in first:
            c.start()
        out = []
        copies = [pltpu.make_async_copy(a, b, sems.at[k]) for k, (a, b) in enumerate(zip(far_in, near_in))]
        for c in copies:
            c.start()
        for k in range(2):
            first[k].wait()
            out.append(pltpu.make_async_copy(passing[k], refs[28 + k], sems.at[28 + k]))
            out[-1].start()
        for c in copies:
            c.wait()
        gwc, gsmall = near_in[0:2]
        order = column_order(KW, NG, False)

        def update(k, index, grad):
            new = adamw(*(near_in[2 + 4 * m + k][index] for m in range(3)), grad, rates[k])
            for m in range(3):
                near_out[4 * m + k][index] = new[m]

        def done(k):
            for m in range(3):
                c = pltpu.make_async_copy(near_out[4 * m + k], far_out[4 * m + k], sems.at[14 + 4 * m + k])
                c.start()
                out.append(c)

        for l in range(3):
            update(3, l, gwc[l])
        done(3)
        for l in range(3):
            grad = gsmall[l, :, 0:KW]
            update(2, l, join3(dot(split3(grad), order)) if inside else grad)
        done(2)
        for l in range(3):
            parts = split3(gsmall[l, :, KW:])
            parts = [parts[per * k : per * (k + 1)] for k in range(3)]
            for k, picks, rows in ((0, [(0, 0, 3), (3, 5, 3)], 6), (1, [(0, 3, 1), (1, 11, 1)], 2)):
                pick = place(rows, 128, picks)
                update(k, l, sum(dot(pick, part, NT) for part in parts))
        done(0)
        done(1)
        for c in out:
            c.wait()

    return kernel


def per_device(
    T, NG,
    features, cotangent, geom_fine, geom_mid, geom_coarse, links_fine, slots_fine, send_lists, parent_fine,
    parent_mid, links_mid, slots_mid, links_coarse, slots_coarse, kernel_in, kernel_bias, kernel_mid, kernel_out,
    *moments,
):
    C = features.shape[2]
    KW = kernel_mid.shape[2]
    NM, NC = links_mid.shape[1], links_coarse.shape[1]
    halo = send_lists.shape[1] // 2
    nf = features.shape[1]
    per = kernel_mid.shape[1]
    inside = per == 8
    lanes = 1024 if inside else 512
    fine = Level(0, nf, links_fine.shape[2], nf + 2 * halo, lanes)
    mid = Level(1, NM, links_mid.shape[2], geom_mid.shape[1], lanes)
    coarse = Level(2, NC, links_coarse.shape[2], geom_coarse.shape[1], lanes)
    everyone = ("tile", "grp")
    half = C * C // 2
    grid = (3, 2, KW // (32 * NG), 2, NG, 16, half)
    small = kernel_mid
    large = kernel_out.reshape(3, per, C, C).transpose(0, 3, 2, 1).reshape(3, 2, half, per).swapaxes(2, 3)
    if not inside:
        zero = jnp.zeros((3, per, 1), F32)
        first = kernel_in.swapaxes(1, 2)
        bias = kernel_bias.swapaxes(1, 2)
        small = jnp.concatenate(
            [kernel_mid, first[..., 0:3], bias[..., 0:1], zero, first[..., 3:6], bias[..., 1:2],
             jnp.zeros((3, per, 119), F32)], axis=2
        )
        small = lax.all_gather(small, everyone, axis=1, tiled=True).reshape(3, KW // 16, 2, 8, KW + 128)
        large = lax.all_gather(large.astype(BF), everyone, axis=2, tiled=True).reshape(grid)

    kernel, scratch = make_kernel(T, NG, C, KW, fine, mid, coarse, halo, inside)
    S = jax.ShapeDtypeStruct
    vm = pl.BlockSpec(memory_space=pltpu.VMEM)
    far = pl.BlockSpec(memory_space=pl.ANY)
    turn = lambda v: v[0].swapaxes(0, 1)
    operands = (
        turn(features), turn(cotangent), turn(geom_fine), turn(geom_mid), turn(geom_coarse),
        turn(links_fine), slots_fine, send_lists, parent_fine, parent_mid, turn(links_mid), slots_mid,
        links_coarse[0], slots_coarse, kernel_in, kernel_bias, small, large,
    )
    layer, gradf, gwc, gsmall = pl.pallas_call(
        kernel,
        out_shape=(S((C, nf), BF), S((C, nf), BF), S((3, 2, 8, half), F32) if inside else S(grid, BF),
                   S((3, 8, KW + 128) if inside else (3, KW // 16, 2, 8, KW + 128), F32)),
        in_specs=[far] * len(operands),
        out_specs=(vm, vm, far, vm),
        scratch_shapes=scratch,
        compiler_params=pltpu.CompilerParams(
            collective_id=0, has_side_effects=True, vmem_limit_bytes=(64 << 20) - (1 << 16)
        ),
        name="layer",
    )(*operands)
    if not inside:
        gwc = gwc.astype(F32).reshape(3, 2, KW, half)
        gwc = lax.psum_scatter(gwc, everyone, scatter_dimension=2, tiled=True)
        gsmall = lax.psum_scatter(gsmall.reshape(3, KW, KW + 128), everyone, scatter_dimension=1, tiled=True)
    gwc = gwc.swapaxes(1, 2).reshape(3, per, C, C).swapaxes(2, 3).reshape(3, per, C * C)
    state = (kernel_in, kernel_bias, kernel_mid, kernel_out) + moments
    new = pl.pallas_call(
        make_update(KW, NG, per, inside),
        out_shape=tuple(S(v.shape, F32) for v in state) + (S((C, nf), BF),) * 2,
        in_specs=[far] * 16,
        out_specs=(far,) * 14,
        scratch_shapes=[pltpu.VMEM(v.shape, F32) for v in (gwc, gsmall) + state]
        + [pltpu.VMEM(v.shape, F32) for v in state] + [pltpu.SemaphoreType.DMA((30,))] + [pltpu.VMEM((C, nf), BF)] * 2,
        compiler_params=pltpu.CompilerParams(vmem_limit_bytes=63 << 20),
        name="update",
    )(gwc, gsmall, *state, layer, gradf)
    return tuple(v.swapaxes(0, 1)[None] for v in new[12:]) + tuple(new[:12])


def solution(mesh):
    nodes = P("grp", "tile", None)
    rows = P("grp", "tile")
    by_column = P(None, None, ("tile", "grp"))
    by_row = P(None, ("tile", "grp"), None)
    shards = (by_column, by_column, by_row, by_row)
    return jax.shard_map(
        functools.partial(per_device, mesh.shape["tile"], mesh.shape["grp"]),
        mesh=mesh,
        in_specs=(
            nodes, nodes, nodes, P("grp", None, None), P("grp", None, None), nodes, rows, rows, rows,
            P("grp", None), nodes, rows, nodes, rows,
        ) + shards * 3,
        out_specs=(nodes, nodes) + shards * 3,
        check_vma=False,
    )
```

```python
import functools

import jax
import jax.numpy as jnp
from jax import lax
from jax.experimental import pallas as pl
from jax.experimental.pallas import tpu as pltpu
from jax.sharding import PartitionSpec as P

STEP = 5
B_ONE = 0.9
B_TWO = 0.95
EPSILON = 1e-08
WEIGHT_DECAY = 0.1
RATE_FIRST = 0.4
RATE_MAIN = 0.02

BF = jnp.bfloat16
F32 = jnp.float32
I32 = jnp.int32
MESH = pl.DeviceIdType.MESH
NN = ((1,), (0,))
NT = ((1,), (1,))
TN = ((0,), (0,))
GROUP = 8


def dot(a, b, dims=NN):
    return lax.dot_general(a, b, (dims, ((), ())), preferred_element_type=F32)


def sig(v):
    return 0.5 + 0.5 * jnp.tanh(0.5 * v)


def split3(v):
    high = v.astype(BF)
    rest = v - high.astype(F32)
    mid = rest.astype(BF)
    low = (rest - mid.astype(F32)).astype(BF)
    return jnp.concatenate([high, mid, low], axis=0)


def join3(v):
    n = v.shape[0] // 3
    return v[:n] + v[n : 2 * n] + v[2 * n :]


def iota(shape, dim):
    return lax.broadcasted_iota(I32, shape, dim)


def log2(n):
    assert n & (n - 1) == 0
    return n.bit_length() - 1


def group_mask(width):
    return (iota((GROUP, width), 1) >> log2(width // GROUP) == iota((GROUP, width), 0)).astype(F32)


def one_hot(row, start, rows):
    return (iota((rows, row.shape[1]), 0) + start == row).astype(F32).astype(BF)


def spread(x, mask):
    return (x[:, None, :] * mask[None]).reshape(x.shape[0] * GROUP, mask.shape[1]).astype(BF)


def place(rows, columns, pairs):
    r, c = iota((rows, columns), 0), iota((rows, columns), 1)
    hit = jnp.zeros((rows, columns), F32)
    for row, column, count in pairs:
        hit = hit + jnp.where((r - row == c - column) & (r >= row) & (r < row + count), 1.0, 0.0)
    return hit.astype(BF)


def column_order(KW, NG, natural_rows):
    p = iota((KW, KW), 1 if natural_rows else 0)
    n = iota((KW, KW), 0 if natural_rows else 1)
    shift = log2(NG)
    inner, core, grp, chip = p & 7, (p >> 3) & 1, (p >> 4) & (NG - 1), p >> (4 + shift)
    return ((((((chip << 1) + core) << shift) + grp) << 3) + inner == n).astype(F32).astype(BF)


class Level:
    def __init__(self, index, nodes, slots, sources, lanes):
        self.lanes = lanes
        self.index, self.nodes, self.slots, self.sources = index, nodes, slots, sources
        self.steps = nodes * slots // lanes
        self.width = GROUP * slots
        self.blocks = lanes // self.width
        self.parts = sources // 128


def make_kernel(T, NG, C, KW, fine, mid, coarse, halo, inside):
    H = T // 4
    NCH = T // 2 * NG
    A = KW // (32 * NG)
    NB = KW // 16
    R = T // 2
    HALF = C * C // 2
    QH = HALF // 2
    SMW = KW + 128
    BW = HALF + KW
    levels = (fine, mid, coarse)
    NM, NC = mid.nodes, coarse.nodes

    def kernel(
        feat_h, cot_h, geof_h, geom_h, geoc_h, lkf_h, slf_h, send_h, parf_h, parm_h, lkm_h, slm_h, lkc_h, slc_h,
        kin_h, kb_h, kmid_h, kout_h,
        layer, gradf, gwc, gsmall,
        feat, cot, geof, geom, geoc, lkf, slf, send, parf, parm, lkm, slm, lkc, slc, kin, kb, kmid, ownw,
        geom_own, lkc_wide, slc_wide, pk0, pk1, pk2, gm, gc,
        extT, agbuf, gbuf, s0buf, s0x, smx, smfull, waT, wbT, wbr, bbc,
        mt0, mt1, mt2, qt1, qt2, as0, as1, as2, xs0, xs1, xs2, zs0, zs1, zs2,
        ohp, tx_s, rx_s, tx_w, rx_w, tx_q, rx_q, tx_u, rx_u, tx_g, rx_g, tx_f, rx_f,
        x1b, x2T, x2b, acc0, acc1, acc2, acc2b, rs1a, rs2a, rs1buf, rs2buf, v0s, gys,
        rsr0, rsr1, rsr2, rsr3, rsf, gsb, gp, rcA, rcB, sems,
    ):
        smbuf, rsr4, acc1b, tx_b, rx_b, tx_h, rx_h = gsb.at[0], s0buf, x1b, tx_u, rx_u, tx_u, rx_u
        t = lax.axis_index("tile")
        g = lax.axis_index("grp")
        core = lax.rem(t, 2)
        r = t // 2
        lo = lax.rem(r, 2)
        hi = r // 2
        ch = r * NG + g
        ocore, olo, og = 1 - core, 1 - lo, 1 - g

        def tile_of(hi_, lo_, core_):
            return (hi_ * 2 + lo_) * 2 + core_

        partner = {"tile": tile_of(hi, lo, ocore), "grp": g}
        xn = {"tile": tile_of(hi, olo, core), "grp": g}
        yn = {"tile": t, "grp": og}

        nil = t - t

        levels_at = [nil + k for k in range(3)]

        def ix(k):
            return levels_at[k]

        counter = [0]
        open_recv, open_send, out_copies = [], [], []

        def sem_block(n):
            base = counter[0]
            counter[0] += n
            return base

        def copy(src, dst, ssem, rsem, dev):
            return pltpu.make_async_remote_copy(
                src_ref=src, dst_ref=dst, send_sem=sems.at[nil + ssem], recv_sem=sems.at[nil + rsem],
                device_id=dev, device_id_type=MESH,
            )

        local = sem_block(1)

        def own_copy(src, dst):
            c = pltpu.make_async_copy(src, dst, sems.at[local])
            c.start()
            c.wait()

        class One:
            def __init__(self, src, dst, dev):
                self.s, self.r = sem_block(1), sem_block(1)
                self.parts = (src, dst, self.s, self.r, dev)

            def start(self):
                copy(*self.parts).start()
                open_recv.append(self)
                open_send.append(self)

            def recv(self):
                open_recv.remove(self)
                copy(*self.parts).wait_recv()

            def sent(self):
                open_send.remove(self)
                copy(*self.parts).wait_send()

        class Ring:
            def __init__(self, n, src, dst, dev):
                self.n, self.src, self.dst, self.dev = n, src, dst, dev
                self.s, self.r = sem_block(n - 1), sem_block(n - 1)

            def each(self, f):
                def body(i, _):
                    d = i + 1
                    f(copy(self.src(d), self.dst(d), self.s + i, self.r + i, self.dev(d)))
                    return 0

                lax.fori_loop(0, self.n - 1, body, 0)

            def start(self):
                self.each(lambda c: c.start())
                open_recv.append(self)
                open_send.append(self)

            def recv(self):
                open_recv.remove(self)
                self.each(lambda c: c.wait_recv())

            def sent(self):
                open_send.remove(self)
                self.each(lambda c: c.wait_send())

        class Sides:
            def __init__(self, src_left, src_right, rx):
                self.ls, self.lr, self.rs, self.rr = (sem_block(1) for _ in range(4))
                self.rx = rx
                self.src_left, self.src_right = src_left, src_right

            @property
            def to_left(self):
                return copy(self.src_left, self.rx.at[1], self.ls, self.lr, {"tile": t - 1, "grp": g})

            @property
            def to_right(self):
                return copy(self.src_right, self.rx.at[0], self.rs, self.rr, {"tile": t + 1, "grp": g})

            def start(self):
                open_recv.append(self)
                open_send.append(self)

                @pl.when(t > 0)
                def _():
                    self.to_left.start()

                @pl.when(t < T - 1)
                def _():
                    self.to_right.start()

                @pl.when(t == 0)
                def _():
                    self.rx[0] = jnp.zeros(self.rx.shape[1:], self.rx.dtype)

                @pl.when(t == T - 1)
                def _():
                    self.rx[1] = jnp.zeros(self.rx.shape[1:], self.rx.dtype)

            def recv(self):
                open_recv.remove(self)

                @pl.when(t < T - 1)
                def _():
                    self.to_left.wait_recv()

                @pl.when(t > 0)
                def _():
                    self.to_right.wait_recv()

            def sent(self):
                open_send.remove(self)

                @pl.when(t > 0)
                def _():
                    self.to_left.wait_send()

                @pl.when(t < T - 1)
                def _():
                    self.to_right.wait_send()

        def started(c):
            c.start()
            return c

        def finish():
            loaded(*loads)
            for c in tuple(open_recv):
                c.recv()
            for c in tuple(open_send):
                c.sent()
            for src, dst, k in out_copies:
                pltpu.make_async_copy(src, dst, sems.at[nil + k]).wait()

        barrier = pltpu.get_barrier_semaphore()

        def chip_dev(d):
            o = lax.rem(ch + d, NCH)
            return {"tile": (o // NG) * 2 + core, "grp": lax.rem(o, NG)}

        def greet(dev):
            pl.semaphore_signal(barrier, inc=1, device_id=dev, device_id_type=MESH)

        def greet_chip(i, _):
            greet(chip_dev(i + 1))
            return 0

        lax.fori_loop(0, NCH - 1, greet_chip, 0)
        greet(partner)
        beside = t - 1 + 2 * core
        has_beside = (beside >= 0) & (beside < T)

        @pl.when(has_beside)
        def _():
            greet({"tile": beside, "grp": g})

        loads = {}

        def load(name, src, dst):
            c = pltpu.make_async_copy(src, dst, sems.at[sem_block(1)])
            c.start()
            loads[name] = c

        def loaded(*names):
            for name in names:
                loads.pop(name).wait()

        if inside:
            load("kmid", kmid_h, kmid)
            load("kin", kin_h, kin)
            load("kb", kb_h, kb)
        load("feat", feat_h, feat)
        load("geof", geof_h, geof)
        load("send", send_h, send)
        if inside:
            for l in range(3):
                load(l, kout_h.at[l, core], ownw.at[l])
        own_lanes = pl.ds(pl.multiple_of(t * NM, NM), NM)
        for name, src, dst in (
            ("lkf", lkf_h, lkf), ("slf", slf_h, slf), ("lkm", lkm_h, lkm), ("slm", slm_h, slm),
            ("own", geom_h.at[:, own_lanes], geom_own), ("lkc", lkc_h, lkc), ("slc", slc_h, slc), ("geom", geom_h, geom),
            ("geoc", geoc_h, geoc), ("parf", parf_h, parf), ("parm", parm_h, parm), ("cot", cot_h, cot),
        ):
            load(name, src, dst)

        if inside:
            loaded("kmid", "kin", "kb")
            order = column_order(KW, NG, True)
            for l in range(3):
                second = dot(kmid[l].astype(BF), order)
                first = dot(kin[l].astype(BF), place(6, 128, [(0, 0, 3), (3, 5, 3)]), TN)
                first = first + dot(kb[l].astype(BF), place(2, 128, [(0, 3, 1), (1, 8, 1)]), TN)
                if l == 0:
                    smbuf[ch, core] = jnp.concatenate([second, first], axis=1)
                else:
                    smx[l - 1, 0] = second
                    smx[l - 1, 1] = jnp.concatenate([first, jnp.zeros((8, KW - 128), F32)], axis=1)
        pl.semaphore_wait(barrier, NCH + has_beside.astype(I32))
        if inside:
            sm_a0 = started(Ring(NCH, lambda d: smbuf.at[ch, core], lambda d: smbuf.at[ch, core], chip_dev))
            s0c = [[started(One(kout_h.at[l, ocore], s0buf.at[l], partner))] for l in range(3)]
            for l in range(2):
                s0c[l].append(started(One(smx.at[l, ocore], s0x.at[l], partner)))
        loaded("feat", "geof", "send")
        n0 = fine.nodes
        extT[:, 0:n0] = (
            dot(place(80, C, [(0, 0, C)]), feat[...]) + dot(place(80, 3, [(C + 5, 0, 3)]), geof[...])
        ).astype(BF)
        tx_s[0] = dot(extT[:, 0:n0], one_hot(send[...], 0, n0)).astype(BF)
        halo_x = started(Sides(tx_s.at[0], tx_s.at[0], rx_s))

        def window(index, start, n, at):
            off = index - start
            return jnp.where(off < 0, off + at + 8, jnp.where(off >= n, off - n + at + 8, off))

        if not inside:
            own_copy(kmid_h, smfull)
            own_copy(kout_h, agbuf)

        ag = [[] for _ in range(3)]
        wide = (BW, BW, HALF)

        def ag_s1(l):
            if not inside:
                return
            for c in s0c[l]:
                c.recv()
            mine, theirs = ownw[l], s0buf[l]
            if l < 2:
                mine = jnp.concatenate([mine, smx[l, core]], axis=1)
                theirs = jnp.concatenate([theirs, s0x[l]], axis=1)
            first = core == 0
            agbuf[l, core, hi, lo, g, :, 0 : wide[l]] = jnp.concatenate(
                [jnp.where(first, mine, theirs), jnp.where(first, theirs, mine)], axis=0
            ).astype(BF)

            def part(d):
                return agbuf.at[ix(l), core, hi, lo, g, :, 0 : wide[l]]

            c = Ring(H, part, part, lambda d: {"tile": tile_of(lax.rem(hi + d, H), lo, core), "grp": g})
            c.start()
            ag[l].append([c])

        def ag_next(l, *copies):
            if not inside:
                return
            for c in ag[l][-1]:
                c.recv()
            for c in copies:
                c.start()
            ag[l].append(copies)

        def ag_s2(l):
            part = agbuf.at[ix(l), core, :, lo, g, :, 0 : wide[l]]
            ag_next(l, One(part, part, xn), One(part, part, yn))

        def ag_s3(l):
            a = agbuf.at[ix(l), core, :, olo, g, :, 0:QH]
            b = agbuf.at[ix(l), core, :, lo, og, :, QH : wide[l]]
            ag_next(l, One(a, a, yn), One(b, b, xn))

        def ag_s4(l):
            part = agbuf.at[ix(l), core, :, :, :, :, 0 : wide[l]]
            ag_next(l, One(part, part, partner))

        def ag_fin(l):
            if inside:
                for c in ag[l][-1]:
                    c.recv()
                for cs in ag[l]:
                    for c in cs:
                        c.sent()
        def unpack_small(l):
            if not inside:
                block = smfull[l].reshape(KW, SMW)
                second, first = block[:, 0:KW], block[:, KW:]
            elif l == 0:
                block = smbuf[...].reshape(KW, SMW)
                second, first = block[:, 0:KW], block[:, KW:]
            else:
                second = agbuf[l - 1, 0, :, :, :, :, HALF:BW].reshape(KW, KW).astype(F32)
                first = agbuf[l - 1, 1, :, :, :, :, HALF : HALF + 128].reshape(KW, 128).astype(F32)
            wbr[l] = second.astype(BF)
            wbT[l] = second.T.astype(BF)
            waT[l] = first[:, 0:8].astype(BF)
            bbc[:, l : l + 1] = first[:, 8:9]

        mts, qts = (mt0, mt1, mt2), (mt0, qt1, qt2)
        xss, zss, pks, a2s = (xs0, xs1, xs2), (zs0, zs1, zs2), (pk0, pk1, pk2), (as0, as1, as2)

        def pack_nodes(lv, links, used, geometry):
            k, n = links.shape
            links = jnp.where(iota((k, n), 0) < used, links, -1).astype(F32)
            high = links.astype(BF).astype(F32)
            rows = dot(place(8, 3, [(0, 0, 3)]), geometry) + jnp.where(iota((8, n), 0) == 3, 1.0, 0.0)
            pad = jnp.zeros((128 - 2 * k - 8, n), F32)
            pks[lv.index][...] = jnp.concatenate([high, links - high, rows, pad], axis=0).T.astype(BF)

        def edge_columns(lv, i):
            k = lv.slots
            n = lv.lanes // k
            at = pl.ds(pl.multiple_of(i * n, n), n)
            nodes = (iota((n, lv.lanes), 1) >> log2(k) == iota((n, lv.lanes), 0)).astype(F32).astype(BF)
            got = dot(pks[lv.index][at, :], nodes, TN)
            slot = iota((k, lv.lanes), 1) & (k - 1) == iota((k, lv.lanes), 0)
            links = jnp.sum(jnp.where(slot, got[0:k] + got[k : 2 * k], 0.0), axis=0, keepdims=True)
            return links, got[2 * k : 2 * k + 8]

        def take(table, row, lv, rows):
            top, hot = row >> 7, one_hot(row & 127, 0, 128)
            n = min(lv.parts, 16)

            def some(first):
                got = dot(table(first, n), hot)
                acc = jnp.zeros((rows, lv.lanes), F32)
                for h in range(n):
                    acc = acc + jnp.where(top == first + h, got[rows * h : rows * (h + 1)], 0.0)
                return acc

            if n == lv.parts:
                return some(0)
            return lax.fori_loop(0, lv.parts // n, lambda k, acc: acc + some(k * n), jnp.zeros((rows, lv.lanes), F32))

        def put(acc, values, row, lv):
            top, hot = row >> 7, one_hot(row & 127, 0, 128)
            n = min(lv.parts, 16)

            def some(first):
                each = [values * jnp.where(top == first + h, 1.0, 0.0).astype(BF) for h in range(n)]
                acc[pl.ds(first, n)] += dot(jnp.concatenate(each, axis=0), hot, NT).reshape(n, C, 128)

            if n == lv.parts:
                some(0)
                return

            def body(k, _):
                some(k * n)
                return 0

            lax.fori_loop(0, lv.parts // n, body, 0)

        def at_step(i, events):
            for when, call in events:

                @pl.when(i == when)
                def _():
                    call()

        def edge_geometry(lv, x_table, g_table, events=()):
            l = lv.index

            def body(i, _):
                at_step(i, events)
                links, z = edge_columns(lv, i)
                row = links.astype(I32)
                if g_table is None:
                    got = dot(x_table[...], one_hot(row, 0, lv.sources))
                    xss[l][i] = got[0:C].astype(BF)
                    z = z + got[C : C + 8]
                else:
                    z = z + take(g_table, row, lv, 8)
                zss[l][i] = jnp.where(iota((8, lv.lanes), 0) == 4, links, z)
                return 0

            lax.fori_loop(0, lv.steps, body, 0)

        def hidden(l, z):
            t1 = dot(waT[l], z.astype(BF))
            a1 = (t1 * sig(t1)).astype(BF)
            t2 = dot(wbT[l], a1) + bbc[:, l : l + 1]
            return (t2 * sig(t2)).astype(BF)

        def edge_hidden(lv):
            l = lv.index

            def body(i, _):
                a2s[l][i] = hidden(l, zss[l][i])
                return 0

            lax.fori_loop(0, lv.steps, body, 0)

        def edges_forward(lv, x_table, events=()):
            l = lv.index
            mask = group_mask(lv.width)

            def body(i, _):
                at_step(i, events)
                if x_table is None:
                    x = xss[l][i].astype(F32)
                    a2 = hidden(l, zss[l][i])
                    a2s[l][i] = a2
                else:
                    x = take(x_table, zss[l][i, 4:5, :].astype(I32), lv, C)
                    xss[l][i] = x.astype(BF)
                    a2 = a2s[l][i]
                for k in range(lv.blocks):
                    sl = slice(lv.width * k, lv.width * (k + 1))
                    m = dot(spread(x[:, sl], mask), a2[:, sl], NT)
                    mts[l][:, lv.blocks * i + k] = m.astype(BF).reshape(C // 2, 2 * GROUP, KW)
                return 0

            lax.fori_loop(0, lv.steps, body, 0)

        def third(l, pair):
            per_half = C // 4
            half, k = pair // per_half, lax.rem(pair, per_half)
            return agbuf[l, half, :, :, :, :, pl.ds(pl.multiple_of(k * 128, 128), 128)].reshape(KW, 2 * C)

        def node_sums(lv):
            l, n = lv.index, lv.nodes
            each = 8

            def body(i, acc):
                w = jnp.concatenate([third(l, each * i + u) for u in range(each)], axis=0)
                m = jnp.concatenate([mts[l][each * i + u].reshape(2 * n, KW) for u in range(each)], axis=1)
                return acc + dot(m, w)

            acc = lax.fori_loop(0, C // 2 // each, body, jnp.zeros((2 * n, 2 * C), F32))
            acc = acc.reshape(n // GROUP, 2, GROUP, 2 * C)
            both = acc[:, 0].reshape(n, 2 * C) + pltpu.roll(acc[:, 1].reshape(n, 2 * C), C, 1)
            return both.T[0:C]

        def by_parity(lv, gsT):
            n = lv.nodes
            gsT = gsT.astype(F32)
            even = jnp.concatenate([gsT, jnp.zeros(gsT.shape, F32)], axis=0).T[0:n]
            odd = pltpu.roll(even, C, 1)
            shape = (n // GROUP, 1, GROUP, 2 * C)
            return jnp.concatenate([even.reshape(shape), odd.reshape(shape)], axis=1).reshape(2 * n, 2 * C)

        def stage(l):
            return agbuf.at[ix(l), :, :, :, :, :, 0:HALF] if l else gbuf

        def third_grad(lv, gs):
            l = lv.index
            n = C // 4
            each = 8
            turned = gs.T.astype(BF)

            def body(j, _):
                for u in range(each):
                    i = each * j + u
                    both = dot(turned, mts[l][i].reshape(2 * lv.nodes, KW))
                    out = both.T.astype(BF).reshape(A, 2, NG, 16, 128)
                    stage(l)[i // n, :, :, :, :, pl.ds(pl.multiple_of(lax.rem(i, n) * 128, 128), 128)] = out
                return 0

            lax.fori_loop(0, C // 2 // each, body, 0)

        def node_weights(lv, gs, events=()):
            l = lv.index
            each = 8
            gs = gs.astype(BF)

            def body(j, _):
                at_step(j, events)
                for u in range(each):
                    i = each * j + u
                    q = dot(gs, third(l, i), NT)
                    qts[l][i] = q.astype(BF).reshape(lv.nodes // GROUP, 2 * GROUP, KW)
                return 0

            lax.fori_loop(0, C // 2 // each, body, 0)

        def source_grads(lv, acc, events=()):
            l = lv.index
            mask = group_mask(lv.width)
            fold = (iota((C, C * GROUP), 1) >> log2(GROUP) == iota((C, C * GROUP), 0)).astype(F32).astype(BF)

            def body(i, _):
                at_step(i, events)
                gxs = []
                for k in range(lv.blocks):
                    sl = slice(lv.width * k, lv.width * (k + 1))
                    q = qts[l][:, lv.blocks * i + k].reshape(C * GROUP, KW)
                    every = dot(q, a2s[l][i, :, sl])
                    own = (every.reshape(C, GROUP, lv.width) * mask[None]).reshape(C * GROUP, lv.width).astype(BF)
                    gxs.append(own)
                gx = dot(fold, jnp.concatenate(gxs, axis=1)).astype(BF)
                put(acc, gx, zss[l][i, 4:5, :].astype(I32), lv)
                return 0

            lax.fori_loop(0, lv.steps, body, 0)

        def weight_grads(lv, first, last, events=()):
            l = lv.index
            mask = group_mask(lv.width)

            def body(i, _):
                at_step(i, events)
                zb = zss[l][i].astype(BF)
                t1 = dot(waT[l], zb)
                s1 = sig(t1)
                f1 = t1 * s1
                d1 = s1 + f1 * (1.0 - s1)
                a1 = f1.astype(BF)
                t2 = dot(wbT[l], a1) + bbc[:, l : l + 1]
                s2 = sig(t2)
                d2 = s2 + t2 * s2 * (1.0 - s2)
                x = xss[l][i].astype(F32)
                g2s = []
                for k in range(lv.blocks):
                    sl = slice(lv.width * k, lv.width * (k + 1))
                    q = qts[l][:, lv.blocks * i + k].reshape(C * GROUP, KW)
                    g2s.append((dot(q, spread(x[:, sl], mask), TN) * d2[:, sl]).astype(BF))
                g2 = jnp.concatenate(g2s, axis=1)
                g1 = (dot(wbr[l], g2) * d1).astype(BF)
                zz = jnp.concatenate([zb, zb], axis=0)
                both = dot(jnp.concatenate([a1, zz], axis=0), g2, NT)
                gsb[l, :, :, :, 0:KW] += both[0:KW].reshape(NB, 2, 8, KW)
                gp[l, 0] += dot(zz, g1, NT)[0:8]
                gp[l, 1] += both[KW : KW + 8]
                return 0

            lax.fori_loop(first, last, body, 0)

        def roll_pick(left, right, n_left, left_lane, right_lane):
            lane = iota((1, 128), 1)
            a = pltpu.roll(left, (left_lane - (n_left - 8)) % 128, 1)
            b = pltpu.roll(right, right_lane % 128, 1)
            return jnp.where((lane >= left_lane) & (lane < left_lane + 8), a, 0.0) + jnp.where(
                (lane >= right_lane) & (lane < right_lane + 8), b, 0.0
            )

        def margin_pick(from_left, from_right, n_own, left_at, right_at):
            lane = iota((1, 128), 1)
            a = pltpu.roll(from_left, (0 - right_at) % 128, 1)
            b = pltpu.roll(from_right, (n_own - 8 - left_at) % 128, 1)
            return jnp.where(lane < 8, a, 0.0) + jnp.where((lane >= n_own - 8) & (lane < n_own), b, 0.0)

        if inside:
            loaded(0, 1, 2)
        ag_s1(0)
        loaded("lkf", "slf", "parf")
        pack_nodes(fine, lkf[...], slf[...], geof[...])
        halo_x.recv()
        near, far = (pltpu.roll(rx_s[k].astype(F32), halo, 1) for k in (0, 1))
        extT[:, n0:] = jnp.where(iota((1, 128), 1) < halo, near, far).astype(BF)
        small_b = []

        def a0_next():
            if inside:
                sm_a0.recv()
                small_b.append(started(One(smbuf.at[:, core], smbuf.at[:, core], partner)))

        edge_geometry(fine, extT, None, [(2, lambda: ag_s2(0)), (2, lambda: ag_s1(1)), (4, a0_next)])
        if inside:
            sm_b0 = small_b[0]
            sm_b0.recv()
        unpack_small(0)
        edges_forward(
            fine, None,
            [(2, lambda: ag_s3(0)), (2, lambda: ag_s1(2)), (5, lambda: ag_s4(0)), (5, lambda: ag_s2(1))],
        )
        ohp[...] = one_hot(window(parf[...], t * NM, NM, NM), 0, 2 * NM)
        nf = slf[...].astype(F32)
        ag_fin(0)
        v0 = extT[0:C, 0 : fine.nodes].astype(F32) + node_sums(fine) / nf
        v0s[...] = v0

        ones8 = jnp.ones((8, fine.nodes), BF)
        part = dot(jnp.concatenate([split3(v0), ones8], axis=0), ohp[...], NT)
        sums = jnp.concatenate([join3(part[0 : 3 * C]), part[3 * C :]], axis=0)
        tx_w[0] = sums[:, NM:]
        ex_w = started(Sides(tx_w.at[0], tx_w.at[0], rx_w))
        loaded("lkm", "slm", "own", "lkc", "slc", "geom", "geoc", "parm", "cot")
        pack_nodes(mid, lkm[...], slm[...], geom_own[...])
        lkc_wide[...] = jnp.zeros(lkc_wide.shape, F32)
        lkc_wide[0:NC] = lkc[...].astype(F32)
        slc_wide[...] = jnp.ones(slc_wide.shape, I32)
        slc_wide[:, 0:NC] = slc[...]
        eye = place(coarse.slots, coarse.slots, [(0, 0, coarse.slots)])
        high = lkc_wide[...].astype(BF)
        low = (lkc_wide[...] - high.astype(F32)).astype(BF)
        turned = (dot(eye, high, NT) + dot(eye, low, NT)).astype(I32)
        lanes = iota((1, 128), 1)
        own_c = jnp.where(lanes < NC, t * NC + lanes, -1)
        geo = dot(geoc[...], one_hot(own_c, 0, coarse.sources)).astype(BF)
        pack_nodes(coarse, turned, jnp.where(lanes < NC, slc_wide[...], 0), geo)
        to_rows = place(8, 3, [(5, 0, 3)])
        for table, source, lv in ((gm, geom, mid), (gc, geoc, coarse)):
            rows = dot(to_rows, source[...])
            for k in range(lv.parts):
                table[k] = rows[:, 128 * k : 128 * (k + 1)]
        nm, nc = (v[...].astype(F32) for v in (slm, slc_wide))
        blocks = [parm[:, pl.ds(pl.multiple_of(b * NM, NM), NM)].astype(F32)
                  for b in (jnp.maximum(t - 1, 0), t, jnp.minimum(t + 1, T - 1))]
        before, after = (pltpu.roll(jnp.broadcast_to(v, (8, NM)), 8, 1)[0:1] for v in (blocks[0], blocks[2]))
        sides = jnp.where((lanes < 8) & (t > 0), before, jnp.where((lanes >= 8) & (lanes < 16) & (t < T - 1), after, -1.0))
        around = jnp.concatenate([blocks[1], sides], axis=1).astype(I32)
        pw = jnp.where(around < 0, -1, window(around, t * NC, NC, NC))
        unpack_small(1)
        ag_s3(1)
        ex_w.recv()
        own = sums[:, 0:NM] + margin_pick(rx_w[0], rx_w[1], NM, 0, 8)
        inv1 = 1.0 / jnp.maximum(own[C : C + 1], 1.0)
        v1 = own[0:C] / jnp.maximum(own[C : C + 1], 1.0)
        x1b[r, core] = v1.astype(BF)

        def chip_ring(src, dst):
            return Ring(R, src, dst, lambda d: {"tile": lax.rem(r + d, R) * 2 + core, "grp": g})

        ag1 = started(chip_ring(lambda d: x1b.at[r, core], lambda d: x1b.at[r, core]))
        ag_s2(2)
        g_rows = lambda table: lambda first, n: table[pl.ds(first, n)].reshape(n * 8, 128).astype(BF)
        edge_geometry(mid, None, g_rows(gm))
        edge_hidden(mid)
        ag_s4(1)
        ag1.recv()
        ag1p = started(One(x1b.at[:, core], x1b.at[:, core], partner))
        ag1p.recv()

        def x1_rows(first, n):
            return x1b[pl.ds(first // 2, n // 2)].reshape(n * C, 128)

        edges_forward(mid, x1_rows, [(2, lambda: ag_s3(2))])
        ag_fin(1)
        unpack_small(2)
        w1 = v1 + node_sums(mid) / nm
        tx_q[0, 0:C] = w1
        ohq = one_hot(pw, 0, 128)
        part = dot(jnp.concatenate([split3(w1), jnp.ones((8, NM), BF)], axis=0), ohq[:, 0:NM], NT)
        tx_q[0, C : 2 * C + 8] = jnp.concatenate([join3(part[0 : 3 * C]), part[3 * C :]], axis=0)
        ex_q = started(Sides(tx_q.at[0], tx_q.at[0], rx_q))
        edge_geometry(coarse, None, g_rows(gc))
        edge_hidden(coarse)
        ag_s4(2)
        ex_q.recv()
        own = tx_q[0, C : 2 * C + 8] + margin_pick(rx_q[0, C : 2 * C + 8], rx_q[1, C : 2 * C + 8], NC, NC, NC + 8)
        w1m = roll_pick(rx_q[0, 0:C], rx_q[1, 0:C], NM, 0, 8)
        w1win = jnp.concatenate([w1, w1m], axis=1)
        lane = iota((1, 128), 1)
        mine = lane < NC
        cnt2 = jnp.maximum(own[C : C + 1], 1.0)
        v2 = jnp.where(mine, own[0:C] / cnt2, 0.0)

        per = 128 // NC
        group = C // per
        packed = v2[0:group]
        for q in range(1, per):
            packed = packed + pltpu.roll(v2[group * q : group * (q + 1)], NC * q, 1)
        x2b[r, core] = packed.astype(BF)
        ag2 = started(chip_ring(lambda d: x2b.at[r, core], lambda d: x2b.at[r, core]))
        ag2.recv()
        ag2p = started(One(x2b.at[:, core], x2b.at[:, core], partner))
        ag2p.recv()
        cols = []
        spot = iota((1, 128), 1) >> log2(NC)
        for k in range(coarse.sources // 128):
            parts = [x2b[(per * k + u) // 2, (per * k + u) % 2].astype(F32) for u in range(per)]
            rows = []
            for q in range(per):
                row = jnp.zeros((group, 128), F32)
                for u in range(per):
                    shift = NC * (u - q) % 128
                    moved = pltpu.roll(parts[u], shift, 1) if shift else parts[u]
                    row = jnp.where(spot == u, moved, row)
                rows.append(row)
            cols.append(jnp.concatenate(rows, axis=0).astype(BF))
        for k, block in enumerate(cols):
            x2T[k] = block
        edges_forward(coarse, lambda first, n: x2T[pl.ds(first, n)].reshape(n * C, 128))
        ag_fin(2)
        sc = node_sums(coarse)
        sc = jnp.concatenate([sc, jnp.zeros((C, 128 - NC), F32)], axis=1)
        w2 = v2 + jnp.where(mine, sc / nc, 0.0)
        tx_u[0] = w2
        ex_u = started(Sides(tx_u.at[0], tx_u.at[0], rx_u))
        ex_u.recv()
        w2win = w2 + roll_pick(rx_u[0], rx_u[1], NC, NC, NC + 8)

        y1win = w1win + join3(dot(split3(w2win), ohq))
        y0 = v0s[...] + join3(dot(split3(y1win), ohp[...]))
        s0 = sig(y0)
        f0 = y0 * s0
        layer[...] = f0.astype(BF)
        gy0 = cot[...] * (s0 + f0 * (1.0 - s0))
        gys[...] = gy0
        gy1p = join3(dot(split3(gy0), ohp[...], NT))
        gw2p = join3(dot(split3(gy1p), ohq, NT))
        tx_g[0, 0:C] = gy1p[:, NM:]
        tx_g[0, C : 2 * C] = gw2p
        ex_g = started(Sides(tx_g.at[0], tx_g.at[0], rx_g))
        ex_g.recv()
        gy1 = gy1p[:, 0:NM] + margin_pick(rx_g[0, 0:C], rx_g[1, 0:C], NM, 0, 8)
        gw2 = jnp.where(mine, gw2p + margin_pick(rx_g[0, C:], rx_g[1, C:], NC, NC, NC + 8), 0.0)

        rs = [[] for _ in range(3)]

        def rs_step(l, fix, *copies):
            if not inside:
                return
            if rs[l]:
                for c in rs[l][-1]:
                    c.recv()
            fix()
            for c in copies:
                c.start()
            rs[l].append(copies)

        def landing(l):
            return gbuf.at[ix(2 - l)] if l and inside else rsr0

        def rs_s0(l):
            rs_step(l, lambda: None, One(stage(l).at[ocore], landing(l), partner))

        def rs_s1(l):
            def fix():
                def body(i, _):
                    both = stage(l)[core, i].astype(F32) + landing(l)[i].astype(F32)
                    stage(l)[core, i] = both.astype(BF)
                    return 0

                lax.fori_loop(0, H, body, 0)

            rs_step(
                l, fix,
                One(stage(l).at[core, :, olo, og, :, 0:QH], rsr1.at[ix(l % 2), ix(0)], xn),
                One(stage(l).at[core, :, olo, og, :, QH:HALF], rsr1.at[ix(l % 2), ix(1)], yn),
            )

        def rs_s2(l):
            def fix():
                def body(i, _):
                    a = stage(l)[core, i, lo, og, :, 0:QH].astype(F32) + rsr1[l % 2, 0, i].astype(F32)
                    stage(l)[core, i, lo, og, :, 0:QH] = a.astype(BF)
                    b = stage(l)[core, i, olo, g, :, QH:HALF].astype(F32) + rsr1[l % 2, 1, i].astype(F32)
                    stage(l)[core, i, olo, g, :, QH:HALF] = b.astype(BF)
                    return 0

                lax.fori_loop(0, H, body, 0)

            rs_step(
                l, fix,
                One(stage(l).at[core, :, lo, og], rsr2.at[ix(l % 2), ix(0)], yn),
                One(stage(l).at[core, :, olo, g], rsr2.at[ix(l % 2), ix(1)], xn),
            )

        def rs_s3(l):
            def fix():
                def body(i, _):
                    a = stage(l)[core, i, lo, g].astype(F32) + rsr2[l % 2, 0, i].astype(F32) + rsr2[l % 2, 1, i].astype(F32)
                    stage(l)[core, i, lo, g] = a.astype(BF)
                    return 0

                lax.fori_loop(0, H, body, 0)

            rs_step(
                l, fix,
                Ring(
                    H,
                    lambda d: stage(l).at[core, lax.rem(hi + d, H), lo, g],
                    lambda d: rsr3.at[ix(l % 2), d - 1],
                    lambda d: {"tile": tile_of(lax.rem(hi + d, H), lo, core), "grp": g},
                ),
            )

        def rs_s4(l):
            def fix():
                tot = stage(l)[core, hi, lo, g].astype(F32)
                for k in range(H - 1):
                    tot = tot + rsr3[l % 2, k].astype(F32)
                rsf[l, 0] = tot[0:8]
                rsf[l, 1] = tot[8:16]

            rs_step(l, fix, One(rsf.at[ix(l), ocore], rsr4.at[ix(l)], partner))

        def rs_s5(l):
            if not inside:
                own_copy(stage(l), gwc.at[l])
                return
            for c in rs[l][-1]:
                c.recv()
            for src, dst in ((rsf.at[ix(l), core], gwc.at[ix(l), core]), (rsr4.at[ix(l)], gwc.at[ix(l), ocore])):
                out_copies.append((src, dst, sem_block(1)))
                pltpu.make_async_copy(src, dst, sems.at[nil + out_copies[-1][2]]).start()

        if inside:
            sm_a0.sent()
            sm_b0.sent()
        gsb[...] = jnp.zeros(gsb.shape, F32)
        gp[...] = jnp.zeros(gp.shape, F32)
        gs_copies = {}

        def gs_start(a, b):
            for l in range(a, b):
                tall = jnp.concatenate([gp[l, 0], gp[l, 1], jnp.zeros((112, KW), F32)], axis=0)
                gsb[l, :, :, :, KW:] = tall.T.reshape(NB, 2, 8, 128)
            if inside:
                gs_copies[a] = started(One(gsb.at[a:b, :, ocore], rcA.at[a:b], partner))

        def gs_ring(a, b):
            if inside:
                gs_copies[a].recv()
                for l in range(a, b):
                    gsb[l, :, core] += rcA[l]
                gs_copies[a] = started(
                    Ring(
                        NCH,
                        lambda d: gsb.at[a:b, lax.rem(ch + d, NCH), core],
                        lambda d: rcB.at[d - 1, a:b],
                        chip_dev,
                    )
                )

        def gs_end(a, b):
            if not inside:
                gsmall[a:b] = gsb[a:b]
                return
            gs_copies[a].recv()

            def add3(k, acc):
                return acc + rcB[k, a:b]

            gsmall[a:b] = lax.fori_loop(0, NCH - 1, add3, gsb[a:b, ch, core])


        gs2T = jnp.where(mine, gw2 / nc, 0.0).astype(BF)
        gs2 = by_parity(coarse, gs2T)
        node_weights(coarse, gs2)
        acc2[...] = jnp.zeros(acc2.shape, F32)
        source_grads(coarse, acc2)
        zero = jnp.zeros((C, 128), F32)
        for k in range(coarse.parts):
            rows = jnp.concatenate([acc2[k], zero], axis=0).T.astype(BF)
            acc2b[per // 2 * k : per // 2 * (k + 1)] = rows.reshape(per // 2, 2, NC, 128)
        r2p = started(One(acc2b.at[:, ocore], rs2a, partner))
        r2p.recv()
        acc2b[:, core] = (acc2b[:, core].astype(F32) + rs2a[...].astype(F32)).astype(BF)
        r2 = started(chip_ring(lambda d: acc2b.at[lax.rem(r + d, R), core], lambda d: rs2buf.at[d - 1]))
        third_grad(coarse, gs2)
        weight_grads(coarse, 0, coarse.steps)
        r2.recv()

        def add2(k, acc):
            return acc + rs2buf[k].astype(F32)

        own2 = lax.fori_loop(0, R - 1, add2, acc2b[r, core].astype(F32))
        own2 = jnp.concatenate([own2, jnp.zeros((128 - NC, 128), F32)], axis=0).T[0:C]
        gv2 = jnp.where(mine, (gw2 + own2) / cnt2, 0.0)
        ex_u.sent()
        tx_b[0] = gv2
        ex_b = started(Sides(tx_b.at[0], tx_b.at[0], rx_b))
        rs_s0(2)
        ex_b.recv()
        gv2win = gv2 + roll_pick(rx_b[0], rx_b[1], NC, NC, NC + 8)
        gw1 = gy1 + join3(dot(split3(gv2win), ohq[:, 0:NM]))

        gs1T = (gw1 / nm).astype(BF)
        gs1 = by_parity(mid, gs1T)
        node_weights(mid, gs1)
        acc1[...] = jnp.zeros(acc1.shape, F32)
        rs_s1(2)
        source_grads(mid, acc1, [(2, lambda: rs_s2(2))])
        ag1.sent()
        ag1p.sent()
        acc1b[...] = acc1[...].astype(BF).reshape(acc1b.shape)
        r1p = started(One(acc1b.at[:, ocore], rs1a, partner))
        half = mid.steps // 2
        r1p.recv()
        acc1b[:, core] = (acc1b[:, core].astype(F32) + rs1a[...].astype(F32)).astype(BF)
        r1 = started(chip_ring(lambda d: acc1b.at[lax.rem(r + d, R), core], lambda d: rs1buf.at[d - 1]))
        third_grad(mid, gs1)
        rs_s0(1)
        weight_grads(mid, 0, half)
        r1.recv()

        def add1(k, acc):
            return acc + rs1buf[k].astype(F32)

        own1 = lax.fori_loop(0, R - 1, add1, acc1b[r, core].astype(F32))
        gv1 = (gw1 + own1) * inv1
        tx_f[0] = gv1
        ex_f = started(Sides(tx_f.at[0], tx_f.at[0], rx_f))
        rs_s1(1)
        rs_s3(2)
        weight_grads(mid, half, mid.steps)
        gs_start(1, 3)
        ex_f.recv()
        gv1win = jnp.concatenate([gv1, roll_pick(rx_f[0], rx_f[1], NM, 0, 8)], axis=1)
        gv0 = gys[...] + join3(dot(split3(gv1win), ohp[...]))
        gys[...] = gv0

        gs0 = gv0 / nf
        gs0T = gs0.astype(BF)
        gs0 = by_parity(fine, gs0T)
        rs_s2(1)
        gs_ring(1, 3)
        third_grad(fine, gs0)
        rs_s0(0)
        node_weights(fine, gs0, [(1, lambda: rs_s1(0))])
        rs_s4(2)
        rs_s3(1)
        weight_grads(
            fine, 0, fine.steps,
            [(2, lambda: rs_s2(0)), (3, lambda: rs_s5(2)), (5, lambda: rs_s4(1)), (7, lambda: rs_s3(0))],
        )
        gs_start(0, 1)
        acc0[...] = jnp.zeros(acc0.shape, F32)
        source_grads(
            fine, acc0, [(1, lambda: gs_ring(0, 1)), (2, lambda: rs_s5(1)), (3, lambda: gs_end(1, 3)), (6, lambda: rs_s4(0))]
        )
        ex_b.sent()
        tx_h[0] = acc0[fine.parts - 1]
        ex_h = started(Sides(tx_h.at[0], tx_h.at[0], rx_h))
        rs_s5(0)
        gs_end(0, 1)
        ex_h.recv()
        lane1 = iota((1, 128), 1)
        back = jnp.where(lane1 < halo, pltpu.roll(rx_h[0], halo, 1), pltpu.roll(rx_h[1], halo, 1))
        ohs2 = one_hot(send[...], 0, n0)
        own0 = jnp.concatenate([acc0[k] for k in range(fine.parts - 1)], axis=1)
        gf = gys[...] + own0 + join3(dot(split3(back), ohs2, NT))
        gradf[...] = gf.astype(BF)
        finish()

    n_sems = (
        2 * (2 * (NCH - 1)) + 4 + 2 * 3 + 3 * (2 * (H - 1) + 4 + 4 + 2) + 4
        + 4 * 7 + 4 * (2 * (T - 1)) + 4 * NCH + 3 * (2 + 4 + 4 + 2 * (H - 1) + 2) + 2 + 2 * (NCH - 1) + 32
    )
    V = pltpu.VMEM
    ls, la = (3, A) if inside else (1, 1)
    by_group = lambda n: V((C // 2, n // GROUP, 2 * GROUP, KW), BF)
    nf, nm_, nc_ = fine.nodes, NM, NC
    scratch = [
        V((C, nf), BF), V((C, nf), F32), V((3, nf), BF), V((3, mid.sources), BF), V((3, coarse.sources), BF),
        V((fine.slots, nf), I32), V((1, nf), I32), V((1, 2 * halo), I32), V((1, nf), I32), V((1, mid.sources), I32),
        V((mid.slots, nm_), I32), V((1, nm_), I32), V((nc_, coarse.slots), I32), V((1, nc_), I32),
        V((3, 6, 8), F32), V((3, 2, 8), F32), V((3, 8, KW), F32), V((ls, 8, HALF), F32),
        V((3, nm_), BF), V((128, coarse.slots), F32), V((1, 128), I32),
        V((nf, 128), BF), V((nm_, 128), BF), V((128, 128), BF), V((mid.parts, 8, 128), F32), V((coarse.parts, 8, 128), F32),
        V((80, nf + 2 * halo), BF),
        V((3, 2, A, 2, NG, 16, BW if inside else HALF), BF), V((2, A, 2, NG, 16, HALF), BF), V((ls, 8, HALF), F32),
        V((2, 8, KW), F32), V((2, 2, 8, KW), F32),
        V((1 if inside else 3, 1 if inside else NB, 2, 8, SMW), F32), V((3, KW, 8), BF), V((3, KW, KW), BF), V((3, KW, KW), BF), V((KW, 128), F32),
        by_group(nf), by_group(nm_), by_group(nc_), by_group(nm_), by_group(nc_),
        V((fine.steps, KW, fine.lanes), BF), V((mid.steps, KW, fine.lanes), BF), V((coarse.steps, KW, fine.lanes), BF),
        V((fine.steps, C, fine.lanes), BF), V((mid.steps, C, fine.lanes), BF), V((coarse.steps, C, fine.lanes), BF),
        V((fine.steps, 8, fine.lanes), F32), V((mid.steps, 8, fine.lanes), F32), V((coarse.steps, 8, fine.lanes), F32),
        V((2 * NM, nf), BF),
        V((1, 80, 128), BF), V((2, 80, 128), BF),
        V((1, C + 8, 128), F32), V((2, C + 8, 128), F32),
        V((1, 2 * C + 8, 128), F32), V((2, 2 * C + 8, 128), F32),
        V((1, C, 128), F32), V((2, C, 128), F32),
        V((1, 2 * C, 128), F32), V((2, 2 * C, 128), F32),
        V((1, C, 128), F32), V((2, C, 128), F32),
        V((R, 2, C, 128), BF), V((coarse.parts, C, 128), BF), V((R, 2, C * NC // 128, 128), BF),
        V((fine.parts, C, 128), F32), V((mid.parts, C, 128), F32), V((coarse.parts, C, 128), F32),
        V((R, 2, NC, 128), BF), V((R, C, 128), BF), V((R, NC, 128), BF),
        V((R - 1, C, 128), BF), V((R - 1, NC, 128), BF), V((C, nf), F32), V((C, nf), F32),
        V((la, 2, NG, 16, HALF), BF), V((2, 2, la, 16, QH), BF), V((2, 2, la, 16, HALF), BF),
        V((2, A - 1, 16, HALF), BF), V((ls, 2, 8, HALF), F32),
        V((3, NB, 2, 8, SMW), F32), V((3, 2, 8, KW), F32), V((ls, NB, 8, SMW), F32), V((NB - 1, 3, 8, SMW), F32),
        pltpu.SemaphoreType.DMA((n_sems,)),
    ]
    return kernel, scratch


def adamw(master, moment, square, grad, learn_rate):
    moment_new = B_ONE * moment + (1.0 - B_ONE) * grad
    square_new = B_TWO * square + (1.0 - B_TWO) * grad * grad
    fix_one = 1.0 - B_ONE**STEP
    fix_two = 1.0 - B_TWO**STEP
    master_new = master - learn_rate * (
        moment_new / fix_one / (jnp.sqrt(square_new / fix_two) + EPSILON) + WEIGHT_DECAY * master
    )
    return (master_new, moment_new, square_new)


def make_update(KW, NG, per, inside):
    rates = (RATE_FIRST, RATE_MAIN, RATE_MAIN, RATE_MAIN)

    def kernel(*refs):
        far_in, far_out, near_in, near_out, sems = refs[0:14], refs[16:28], refs[30:44], refs[44:56], refs[56]
        passing = refs[57:59]
        first = [pltpu.make_async_copy(refs[14 + k], passing[k], sems.at[26 + k]) for k in range(2)]
        for c in first:
            c.start()
        out = []
        large = (0, 5, 9, 13)
        copies = [pltpu.make_async_copy(far_in[k], near_in[k], sems.at[k]) for k in range(14) if k not in large]
        levels = [
            [pltpu.make_async_copy(far_in[k].at[l], near_in[k].at[l], sems.at[30 + 4 * l + m]) for m, k in enumerate(large)]
            for l in range(3)
        ]
        for c in sum(levels, []) + copies:
            c.start()
        for k in range(2):
            first[k].wait()
            out.append(pltpu.make_async_copy(passing[k], refs[28 + k], sems.at[28 + k]))
            out[-1].start()
        gwc, gsmall = near_in[0:2]
        order = column_order(KW, NG, False)

        def update(k, index, grad):
            new = adamw(*(near_in[2 + 4 * m + k][index] for m in range(3)), grad, rates[k])
            for m in range(3):
                near_out[4 * m + k][index] = new[m]

        def done(k):
            for m in range(3):
                c = pltpu.make_async_copy(near_out[4 * m + k], far_out[4 * m + k], sems.at[14 + 4 * m + k])
                c.start()
                out.append(c)

        for l in range(3):
            for c in levels[l]:
                c.wait()
            update(3, l, gwc[l])
            for m in range(3):
                k = 4 * m + 3
                out.append(pltpu.make_async_copy(near_out[k].at[l], far_out[k].at[l], sems.at[42 + 3 * l + m]))
                out[-1].start()
        for c in copies:
            c.wait()
        for l in range(3):
            grad = gsmall[l, :, 0:KW]
            update(2, l, join3(dot(split3(grad), order)) if inside else grad)
        done(2)
        for l in range(3):
            parts = split3(gsmall[l, :, KW:])
            parts = [parts[per * k : per * (k + 1)] for k in range(3)]
            for k, picks, rows in ((0, [(0, 0, 3), (3, 5, 3)], 6), (1, [(0, 3, 1), (1, 11, 1)], 2)):
                pick = place(rows, 128, picks)
                update(k, l, sum(dot(pick, part, NT) for part in parts))
        done(0)
        done(1)
        for c in out:
            c.wait()

    return kernel


def per_device(
    T, NG,
    features, cotangent, geom_fine, geom_mid, geom_coarse, links_fine, slots_fine, send_lists, parent_fine,
    parent_mid, links_mid, slots_mid, links_coarse, slots_coarse, kernel_in, kernel_bias, kernel_mid, kernel_out,
    *moments,
):
    C = features.shape[2]
    KW = kernel_mid.shape[2]
    NM, NC = links_mid.shape[1], links_coarse.shape[1]
    halo = send_lists.shape[1] // 2
    nf = features.shape[1]
    per = kernel_mid.shape[1]
    inside = per == 8
    lanes = 1024 if inside else 512
    fine = Level(0, nf, links_fine.shape[2], nf + 2 * halo, lanes)
    mid = Level(1, NM, links_mid.shape[2], geom_mid.shape[1], lanes)
    coarse = Level(2, NC, links_coarse.shape[2], geom_coarse.shape[1], lanes)
    everyone = ("tile", "grp")
    half = C * C // 2
    grid = (3, 2, KW // (32 * NG), 2, NG, 16, half)
    small = kernel_mid
    large = kernel_out.reshape(3, per, C, C).transpose(0, 3, 2, 1).reshape(3, 2, half, per).swapaxes(2, 3)
    if not inside:
        zero = jnp.zeros((3, per, 1), F32)
        first = kernel_in.swapaxes(1, 2)
        bias = kernel_bias.swapaxes(1, 2)
        small = jnp.concatenate(
            [kernel_mid, first[..., 0:3], bias[..., 0:1], zero, first[..., 3:6], bias[..., 1:2],
             jnp.zeros((3, per, 119), F32)], axis=2
        )
        small = lax.all_gather(small, everyone, axis=1, tiled=True).reshape(3, KW // 16, 2, 8, KW + 128)
        large = lax.all_gather(large.astype(BF), everyone, axis=2, tiled=True).reshape(grid)

    kernel, scratch = make_kernel(T, NG, C, KW, fine, mid, coarse, halo, inside)
    S = jax.ShapeDtypeStruct
    vm = pl.BlockSpec(memory_space=pltpu.VMEM)
    far = pl.BlockSpec(memory_space=pl.ANY)
    turn = lambda v: v[0].swapaxes(0, 1)
    operands = (
        turn(features), turn(cotangent), turn(geom_fine), turn(geom_mid), turn(geom_coarse),
        turn(links_fine), slots_fine, send_lists, parent_fine, parent_mid, turn(links_mid), slots_mid,
        links_coarse[0], slots_coarse, kernel_in, kernel_bias, small, large,
    )
    layer, gradf, gwc, gsmall = pl.pallas_call(
        kernel,
        out_shape=(S((C, nf), BF), S((C, nf), BF), S((3, 2, 8, half), F32) if inside else S(grid, BF),
                   S((3, 8, KW + 128) if inside else (3, KW // 16, 2, 8, KW + 128), F32)),
        in_specs=[far] * len(operands),
        out_specs=(vm, vm, far, vm),
        scratch_shapes=scratch,
        compiler_params=pltpu.CompilerParams(
            collective_id=0, has_side_effects=True, vmem_limit_bytes=(64 << 20) - (1 << 16)
        ),
        name="layer",
    )(*operands)
    if not inside:
        gwc = gwc.astype(F32).reshape(3, 2, KW, half)
        gwc = lax.psum_scatter(gwc, everyone, scatter_dimension=2, tiled=True)
        gsmall = lax.psum_scatter(gsmall.reshape(3, KW, KW + 128), everyone, scatter_dimension=1, tiled=True)
    gwc = gwc.swapaxes(1, 2).reshape(3, per, C, C).swapaxes(2, 3).reshape(3, per, C * C)
    state = (kernel_in, kernel_bias, kernel_mid, kernel_out) + moments
    new = pl.pallas_call(
        make_update(KW, NG, per, inside),
        out_shape=tuple(S(v.shape, F32) for v in state) + (S((C, nf), BF),) * 2,
        in_specs=[far] * 16,
        out_specs=(far,) * 14,
        scratch_shapes=[pltpu.VMEM(v.shape, F32) for v in (gwc, gsmall) + state]
        + [pltpu.VMEM(v.shape, F32) for v in state] + [pltpu.SemaphoreType.DMA((51,))] + [pltpu.VMEM((C, nf), BF)] * 2,
        compiler_params=pltpu.CompilerParams(vmem_limit_bytes=63 << 20),
        name="update",
    )(gwc, gsmall, *state, layer, gradf)
    return tuple(v.swapaxes(0, 1)[None] for v in new[12:]) + tuple(new[:12])


def solution(mesh):
    nodes = P("grp", "tile", None)
    rows = P("grp", "tile")
    by_column = P(None, None, ("tile", "grp"))
    by_row = P(None, ("tile", "grp"), None)
    shards = (by_column, by_column, by_row, by_row)
    return jax.shard_map(
        functools.partial(per_device, mesh.shape["tile"], mesh.shape["grp"]),
        mesh=mesh,
        in_specs=(
            nodes, nodes, nodes, P("grp", None, None), P("grp", None, None), nodes, rows, rows, rows,
            P("grp", None), nodes, rows, nodes, rows,
        ) + shards * 3,
        out_specs=(nodes, nodes) + shards * 3,
        check_vma=False,
    )
```
